512 devices in a mesh: mem: 16 (over z, y_lo), lon: 32 (over y_hi, x, core).
Axes of the slice: x: 4, y: 8 (y_hi: 4, y_lo: 2; y = y_hi * 2 + y_lo), z: 8, core: 2. Of those that a mesh axis runs over, the one named last changes fastest.
Arguments:
- fields: bfloat16 [80, 64, 256, 128], P('mem', None, 'lon'), may hold values from -8 to 8
- w_query: bfloat16 [24, 576], replicated, may hold values from -1 to 1
- w_key: bfloat16 [24, 576], replicated, may hold values from -1 to 1
- w_value: bfloat16 [24, 576], replicated, may hold values from -0.25 to 0.25
- w_out: bfloat16 [64, 216], replicated, may hold values from -1.25 to 1.25
Outputs:
- updated: bfloat16 [80, 64, 256, 128], P('mem', None, 'lon')
The draws below stay inside these ranges and needn't reach their ends.
All inputs are finite; a program needn't handle non-finite values.
Results may differ from the reference program's by a relative error of at most 0.008.
Values may be sent and summed in bfloat16 or wider, within the bound.
No kernel may reach another device: no remote copies, remote signals or barrier semaphores. Data moves between devices by JAX's collectives and lax.ppermute only.
A program may use at most 64 MiB of HBM per device.

```python
import math
import jax
import jax.numpy as jnp
from jax import lax

CH = 64
CQ = 24
LAT = 128
MEMBERS = 80
LON = 256


def draw_fields(key, part):
    full_shape = (MEMBERS, CH, LON, LAT)
    shared_shape = (1, CH, LON, LAT)
    ramp = 0.45 + 0.9 * jnp.arange(LON, dtype=jnp.float32) / max(LON - 1, 1)
    ramp = ramp.reshape(1, 1, LON, 1)
    shared = jax.random.normal(jax.random.fold_in(key, 7), shared_shape, jnp.float32)
    own = jax.random.normal(jax.random.fold_in(key, 8), full_shape, jnp.float32)
    sample = ramp * (0.6 * shared + 0.8 * own)
    return jnp.clip(sample, -8.0, 8.0).astype(jnp.bfloat16)


def query_weight(key):
    fan_in = 9 * CH
    first_draw = jax.random.normal(jax.random.fold_in(key, 21), (CQ, 9 * CH), jnp.float32) / math.sqrt(fan_in)
    return jnp.clip(first_draw, -1.0, 1.0)


def draw_w_query(key, part):
    return query_weight(key).astype(jnp.bfloat16)


def draw_w_key(key, part):
    half = CH // 2
    rounded = query_weight(key).astype(jnp.bfloat16).astype(jnp.float32)
    shaped = rounded.reshape(CQ, 9, CH)
    factor = jnp.exp(jax.random.uniform(jax.random.fold_in(key, 23), (CQ, 9, half), jnp.float32, math.log(0.5), math.log(2.0)))
    key_weight = jnp.concatenate([factor * shaped[:, :, half:], -factor * shaped[:, :, :half]], axis=2)
    return jnp.clip(key_weight.reshape(CQ, 9 * CH), -1.0, 1.0).astype(jnp.bfloat16)


def bell_draw(stream_key, dims, width, bound, kind=jnp.bfloat16):
    return jnp.clip(width * jax.random.normal(stream_key, dims, jnp.float32), -bound, bound).astype(kind)


def setup_inputs(seed: int = 0) -> dict:
    key_of = jax.random.split(jax.random.key(seed), 6)
    fields = draw_fields(jax.random.fold_in(key_of[5], 71), 0)
    w_query = draw_w_query(jax.random.fold_in(key_of[5], 71), 0)
    w_key = draw_w_key(jax.random.fold_in(key_of[5], 71), 0)
    w_value = bell_draw(key_of[3], (CQ, 9 * CH), (9 * CH) ** -0.5, 0.25)
    w_out = bell_draw(key_of[4], (CH, 9 * CQ), CQ ** -0.5, 1.25)
    return dict(fields=fields, w_query=w_query, w_key=w_key, w_value=w_value, w_out=w_out)


def conv_member(member_field, weight):
    channels, longitudes, latitudes = member_field.shape
    wrapped = jnp.concatenate([member_field[:, -1:], member_field, member_field[:, :1]], axis=1)
    padded = jnp.pad(wrapped, ((0, 0), (0, 0), (1, 1)))
    patches = jnp.concatenate([padded[:, lon_step:lon_step + longitudes, lat_step:lat_step + latitudes] for lon_step in range(3) for lat_step in range(3)], axis=0)
    result = jnp.dot(weight, patches.reshape(9 * channels, longitudes * latitudes), preferred_element_type=jnp.float32)
    return result.reshape(weight.shape[0], longitudes, latitudes)

def reference(fields, w_query, w_key, w_value, w_out):
    w_inner = jnp.concatenate([w_query, w_key, w_value], axis=0)

    def project(member_field):
        return conv_member(member_field, w_inner).astype(jnp.bfloat16)
    projected = lax.map(project, fields)
    queries = projected[:, :CQ].reshape(MEMBERS, -1)
    keys_all = projected[:, CQ:2 * CQ].reshape(MEMBERS, -1)
    values = projected[:, 2 * CQ:]
    gram_sums = jnp.dot(queries, keys_all.T, preferred_element_type=jnp.float32)
    score_scale = 1.0 / math.sqrt(CQ * LAT * LON)
    weights = jax.nn.softmax(gram_sums * score_scale, axis=1).astype(jnp.bfloat16)
    mixed_values = jnp.dot(weights, values.reshape(MEMBERS, -1), preferred_element_type=jnp.float32)
    mixed_values = mixed_values.astype(jnp.bfloat16).reshape(values.shape)

    def finish(member_pair):
        member_field, member_mixed = member_pair
        return (member_field.astype(jnp.float32) + conv_member(member_mixed, w_out)).astype(jnp.bfloat16)
    return lax.map(finish, (fields, mixed_values))
```

```python
import functools
import math

import jax
import jax.numpy as jnp
from jax import lax
from jax.experimental import pallas as pl
from jax.experimental.pallas import tpu as pltpu
from jax.sharding import PartitionSpec as P

CH, CQ, LAT = 64, 24, 128
HALF = CQ // 2
MEM, LON = 16, 32
OWN = 5
TOTAL = MEM * OWN
COLS = 8
EXT = COLS + 2
ROWS = 16
F32, BF16 = jnp.float32, jnp.bfloat16
VMEM = pl.BlockSpec(memory_space=pltpu.VMEM)


def call(body, outs, scratch, flops, nbytes, *args):
    many = isinstance(outs, tuple)
    return pl.pallas_call(
        body,
        out_shape=outs,
        in_specs=[VMEM] * len(args),
        out_specs=(VMEM,) * len(outs) if many else VMEM,
        scratch_shapes=scratch,
        compiler_params=pltpu.CompilerParams(vmem_limit_bytes=32 * 1024 * 1024),
        cost_estimate=pl.CostEstimate(flops=flops, bytes_accessed=nbytes, transcendentals=0),
    )(*args)


def lat_shifts(x):
    lane = lax.broadcasted_iota(jnp.int32, x.shape, 1)
    before = jnp.where(lane == 0, 0.0, pltpu.roll(x, 1, 1))
    after = jnp.where(lane == LAT - 1, 0.0, pltpu.roll(x, LAT - 1, 1))
    return before, after


def project_kernel(f_ref, lo_ref, hi_ref, w_ref, qk_ref, v_ref, xf, xt, vs):
    width = 3 * CQ
    lane = lax.broadcasted_iota(jnp.int32, (width, LAT), 1)
    for m in range(OWN):
        xf[...] = f_ref[m].astype(F32).reshape(CH * COLS, LAT)
        for s in range(2):
            xt[s * CH : (s + 1) * CH] = lo_ref[m, s]
            xt[(EXT + s) * CH : (EXT + s + 1) * CH] = hi_ref[m, s]
        for i in range(COLS):
            xt[(i + 2) * CH : (i + 3) * CH] = xf[pl.ds(i, CH, stride=COLS), :].astype(BF16)
        for p in range(EXT // 2):
            r = jnp.dot(w_ref[...], xt[2 * p * CH : (2 * p + 4) * CH], preferred_element_type=F32)
            for s in range(2):
                y = [r[(3 * s + b) * width : (3 * s + b + 1) * width] for b in range(3)]
                out = (
                    y[1]
                    + jnp.where(lane == 0, 0.0, pltpu.roll(y[0], 1, 1))
                    + jnp.where(lane == LAT - 1, 0.0, pltpu.roll(y[2], LAT - 1, 1))
                )
                col = 2 * p + s
                vs[col * CQ : (col + 1) * CQ] = out[2 * CQ :]
                if 1 <= col <= COLS:
                    for h in range(2):
                        qk_ref[2 * (col - 1) + h, m] = out[h * CQ : (h + 1) * CQ].astype(BF16)
        vs[EXT * CQ :] = jnp.zeros((MEM * ROWS - EXT * CQ, LAT), F32)
        for j in range(MEM):
            v_ref[j, m] = vs[j * ROWS : (j + 1) * ROWS].astype(BF16)


def gram_kernel(x_ref, g_ref, xs, gs):
    xs[...] = x_ref[...].astype(F32).reshape(TOTAL * CQ, LAT)
    pad = jnp.zeros((LAT - TOTAL, LAT), BF16)
    q, k = [], []
    for r in range(HALF):
        q.append(xs[pl.ds(r, TOTAL, stride=CQ), :].astype(BF16))
        k.append(jnp.concatenate([xs[pl.ds(HALF + r, TOTAL, stride=CQ), :].astype(BF16), pad], axis=0))
    gs[...] = lax.dot_general(
        jnp.concatenate(q, axis=1),
        jnp.concatenate(k, axis=1),
        (((1,), (1,)), ((), ())),
        preferred_element_type=F32,
    )
    g_ref[...] = jnp.zeros(g_ref.shape, F32)
    for s in range(MEM):
        g_ref[s, 0:OWN, :] = gs[s * OWN : (s + 1) * OWN, :]


def spread_kernel(x_ref, o_ref):
    o_ref[...] = jnp.broadcast_to(jnp.sum(x_ref[...], axis=0)[None], o_ref.shape)


def softmax_kernel(scale, x_ref, o_ref):
    s = jnp.sum(x_ref[...], axis=0) * scale
    lane = lax.broadcasted_iota(jnp.int32, s.shape, 1)
    s = jnp.where(lane < TOTAL, s, -jnp.inf)
    e = jnp.exp(s - jnp.max(s, axis=1, keepdims=True))
    w = e / jnp.sum(e, axis=1, keepdims=True)
    o_ref[...] = jnp.broadcast_to(w.astype(BF16).astype(F32)[None], o_ref.shape)


def mix_kernel(w_ref, v_ref, o_ref, ws, vs, ms):
    for s in range(MEM):
        ws[s * OWN : (s + 1) * OWN, :] = w_ref[s, 0:OWN, :]
    w = ws[...].astype(BF16)[:, :TOTAL]
    vs[...] = v_ref[...].astype(F32).reshape(TOTAL * ROWS, LAT)
    v = jnp.concatenate([vs[pl.ds(r, TOTAL, stride=ROWS), :].astype(BF16) for r in range(ROWS)], axis=1)
    mixed = jnp.dot(w, v, preferred_element_type=F32)
    for r in range(ROWS):
        ms[pl.ds(r, TOTAL, stride=ROWS), :] = mixed[:, r * LAT : (r + 1) * LAT]
    o_ref[...] = ms[...].astype(BF16).reshape(o_ref.shape)


def finish_kernel(x_ref, f_ref, w_ref, o_ref, mc, mb, ma, br):
    for m in range(OWN):
        for j in range(MEM):
            mc[j * ROWS : (j + 1) * ROWS] = x_ref[j, m].astype(F32)
        mb[...], ma[...] = lat_shifts(mc[...])
        for i in range(0, COLS, 2):
            patches = []
            for col in (i, i + 1):
                parts = [
                    t[(col + a) * CQ : (col + a + 1) * CQ, :] for a in range(3) for t in (mb, mc, ma)
                ]
                patches.append(jnp.concatenate(parts, axis=0).astype(BF16))
            r = jnp.dot(w_ref[...], jnp.concatenate(patches, axis=1), preferred_element_type=F32)
            for s in range(2):
                br[pl.ds(i + s, CH, stride=COLS), :] = r[:, s * LAT : (s + 1) * LAT]
        o_ref[m] = (f_ref[m].astype(F32) + br[...].reshape(CH, COLS, LAT)).astype(BF16)


def shards(fields, w_query, w_key, w_value, w_out):
    forward = [(i, (i + 1) % LON) for i in range(LON)]
    backward = [(target, source) for source, target in forward]
    lo = lax.ppermute(jnp.transpose(fields[:, :, COLS - 2 :], (0, 2, 1, 3)), "lon", forward)
    hi = lax.ppermute(jnp.transpose(fields[:, :, :2], (0, 2, 1, 3)), "lon", backward)

    w = jnp.concatenate([w_query[:HALF], w_key[:HALF], w_query[HALF:], w_key[HALF:], w_value], axis=0)
    w = jnp.transpose(w.reshape(3 * CQ, 3, 3, CH), (2, 0, 1, 3)).reshape(9 * CQ, 3 * CH)
    w_pair = jnp.concatenate(
        [jnp.pad(w, ((0, 0), (0, CH))), jnp.pad(w, ((0, 0), (CH, 0)))], axis=0
    )
    qk, v = call(
        project_kernel,
        (
            jax.ShapeDtypeStruct((MEM, OWN, CQ, LAT), BF16),
            jax.ShapeDtypeStruct((MEM, OWN, ROWS, LAT), BF16),
        ),
        [
            pltpu.VMEM((CH * COLS, LAT), F32),
            pltpu.VMEM((CH * (COLS + 4), LAT), BF16),
            pltpu.VMEM((MEM * ROWS, LAT), F32),
        ],
        700_000_000,
        2_000_000,
        fields,
        lo,
        hi,
        w_pair,
    )
    qk = lax.all_to_all(qk, "mem", 0, 0, tiled=True)
    v = lax.all_to_all(v, "mem", 0, 0, tiled=True)

    tile = (8, LAT)
    gram = call(
        gram_kernel,
        jax.ShapeDtypeStruct((MEM, *tile), F32),
        [pltpu.VMEM((TOTAL * CQ, LAT), F32), pltpu.VMEM((TOTAL, LAT), F32)],
        20_000_000,
        600_000,
        qk,
    )
    gram = lax.all_to_all(gram, "mem", 0, 0, tiled=True)
    gram = call(spread_kernel, jax.ShapeDtypeStruct((LON, *tile), F32), [], 20_000, 200_000, gram)
    gram = lax.all_to_all(gram, "lon", 0, 0, tiled=True)
    scale = 1.0 / math.sqrt(CQ * LAT * COLS * LON)
    weights = call(
        functools.partial(softmax_kernel, scale),
        jax.ShapeDtypeStruct((MEM, *tile), F32),
        [],
        40_000,
        200_000,
        gram,
    )
    weights = lax.all_to_all(weights, "mem", 0, 0, tiled=True)
    mixed = call(
        mix_kernel,
        jax.ShapeDtypeStruct((MEM, OWN, ROWS, LAT), BF16),
        [
            pltpu.VMEM((TOTAL, LAT), F32),
            pltpu.VMEM((TOTAL * ROWS, LAT), F32),
            pltpu.VMEM((TOTAL * ROWS, LAT), F32),
        ],
        30_000_000,
        700_000,
        weights,
        v,
    )
    mixed = lax.all_to_all(mixed, "mem", 0, 0, tiled=True)
    return call(
        finish_kernel,
        jax.ShapeDtypeStruct(fields.shape, BF16),
        [pltpu.VMEM((MEM * ROWS, LAT), F32)] * 3 + [pltpu.VMEM((CH * COLS, LAT), F32)],
        150_000_000,
        1_700_000,
        mixed,
        fields,
        w_out,
    )


def solution(mesh):
    return jax.shard_map(
        shards,
        mesh=mesh,
        in_specs=(P("mem", None, "lon", None), P(), P(), P(), P()),
        out_specs=P("mem", None, "lon", None),
        check_vma=False,
    )
```

```python
import functools
import math

import jax
import jax.numpy as jnp
from jax import lax
from jax.experimental import pallas as pl
from jax.experimental.pallas import tpu as pltpu
from jax.sharding import Mesh
from jax.sharding import PartitionSpec as P

CH, CQ, LAT = 64, 24, 128
HALF = CQ // 2
MEM, LON = 16, 32
OWN = 5
TOTAL = MEM * OWN
COLS = 8
EXT = COLS + 2
ROWS = 16
F32, BF16 = jnp.float32, jnp.bfloat16
VMEM = pl.BlockSpec(memory_space=pltpu.VMEM)


def call(body, outs, scratch, flops, nbytes, *args, alias=None):
    many = isinstance(outs, tuple)
    return pl.pallas_call(
        body,
        out_shape=outs,
        in_specs=[VMEM] * len(args),
        out_specs=(VMEM,) * len(outs) if many else VMEM,
        scratch_shapes=scratch,
        input_output_aliases=alias or {},
        compiler_params=pltpu.CompilerParams(vmem_limit_bytes=32 * 1024 * 1024),
        cost_estimate=pl.CostEstimate(flops=flops, bytes_accessed=nbytes, transcendentals=0),
    )(*args)


def lat_shifts(x):
    lane = lax.broadcasted_iota(jnp.int32, x.shape, 1)
    before = jnp.where(lane == 0, 0.0, pltpu.roll(x, 1, 1))
    after = jnp.where(lane == LAT - 1, 0.0, pltpu.roll(x, LAT - 1, 1))
    return before, after


def edges_kernel(f_ref, sib_ref, nb_ref, xf):
    even = lax.axis_index("core") == 0
    for m in range(OWN):
        xf[...] = f_ref[m].astype(F32).reshape(CH * COLS, LAT)
        for s in range(2):
            left = xf[pl.ds(s, CH, stride=COLS), :]
            right = xf[pl.ds(COLS - 2 + s, CH, stride=COLS), :]
            sib_ref[m, s * CH : (s + 1) * CH] = jnp.where(even, right, left).astype(BF16)
            nb_ref[m, s * CH : (s + 1) * CH] = jnp.where(even, left, right).astype(BF16)


def conv_pair(w, x):
    width = 3 * CQ
    lane = lax.broadcasted_iota(jnp.int32, (width, LAT), 1)
    r = jnp.dot(w, x, preferred_element_type=F32)
    outs = []
    for s in range(2):
        y = [r[(3 * s + b) * width : (3 * s + b + 1) * width] for b in range(3)]
        outs.append(
            y[1]
            + jnp.where(lane == 0, 0.0, pltpu.roll(y[0], 1, 1))
            + jnp.where(lane == LAT - 1, 0.0, pltpu.roll(y[2], LAT - 1, 1))
        )
    return outs


def put_pair(o_ref, vs, m, p, outs):
    for s in range(2):
        col = 2 * p + s
        vs[s * CQ : (s + 1) * CQ] = outs[s][2 * CQ :]
        if 1 <= col <= COLS:
            for h in range(2):
                o_ref[2 * (col - 1) + h, m, 0:CQ] = outs[s][h * CQ : (h + 1) * CQ].astype(BF16)
    for j in range(3):
        o_ref[3 * p + j, m, CQ:] = vs[j * ROWS : (j + 1) * ROWS].astype(BF16)


def inner_kernel(f_ref, wq_ref, wk_ref, wv_ref, o_ref, wp_ref, ws, xf, xt, vs):
    ws[0:HALF] = wq_ref[...].astype(F32)[:HALF]
    ws[HALF : 2 * HALF] = wk_ref[...].astype(F32)[:HALF]
    ws[2 * HALF : 3 * HALF] = wq_ref[...].astype(F32)[HALF:]
    ws[3 * HALF : 4 * HALF] = wk_ref[...].astype(F32)[HALF:]
    ws[2 * CQ :] = wv_ref[...].astype(F32)
    zero = jnp.zeros((3 * CQ, CH), F32)
    for b in range(3):
        taps = [ws[:, (3 * a + b) * CH : (3 * a + b + 1) * CH] for a in range(3)]
        for s in range(2):
            row = (3 * s + b) * 3 * CQ
            full = [zero] + taps if s else taps + [zero]
            wp_ref[row : row + 3 * CQ] = jnp.concatenate(full, axis=1).astype(BF16)
    for m in range(OWN):
        xf[...] = f_ref[m].astype(F32).reshape(CH * COLS, LAT)
        for i in range(COLS):
            xt[i * CH : (i + 1) * CH] = xf[pl.ds(i, CH, stride=COLS), :].astype(BF16)
        for p in range(1, EXT // 2 - 1):
            x = xt[2 * (p - 1) * CH : 2 * (p + 1) * CH]
            put_pair(o_ref, vs, m, p, conv_pair(wp_ref[...], x))


def outer_kernel(i_ref, wp_ref, sib_ref, nb_ref, gs_ref, gn_ref, o_ref, xl, xr, vs):
    core = lax.axis_index("core")
    near = 2 * CH

    @pl.when(core == 0)
    def _():
        xl[:, :near] = gn_ref[...]
        xl[:, near:] = nb_ref[...]
        xr[:, :near] = sib_ref[...]
        xr[:, near:] = gs_ref[1]

    @pl.when(core == 1)
    def _():
        xl[:, :near] = gs_ref[0]
        xl[:, near:] = sib_ref[...]
        xr[:, :near] = nb_ref[...]
        xr[:, near:] = gn_ref[...]

    for m in range(OWN):
        put_pair(o_ref, vs, m, 0, conv_pair(wp_ref[...], xl[m]))
        put_pair(o_ref, vs, m, EXT // 2 - 1, conv_pair(wp_ref[...], xr[m]))
        o_ref[MEM - 1, m, CQ:] = jnp.zeros((ROWS, LAT), BF16)


def gram_kernel(x_ref, g_ref, xs, gs):
    xs[...] = x_ref[:, :, 0:CQ, :].astype(F32).reshape(TOTAL * CQ, LAT)
    pad = jnp.zeros((LAT - TOTAL, LAT), BF16)
    q, k = [], []
    for r in range(HALF):
        q.append(xs[pl.ds(r, TOTAL, stride=CQ), :].astype(BF16))
        k.append(jnp.concatenate([xs[pl.ds(HALF + r, TOTAL, stride=CQ), :].astype(BF16), pad], axis=0))
    gs[...] = lax.dot_general(
        jnp.concatenate(q, axis=1),
        jnp.concatenate(k, axis=1),
        (((1,), (1,)), ((), ())),
        preferred_element_type=F32,
    )
    g_ref[...] = jnp.zeros(g_ref.shape, F32)
    for s in range(MEM):
        g_ref[s, 0:OWN, :] = gs[s * OWN : (s + 1) * OWN, :]


def spread_kernel(x_ref, o_ref):
    o_ref[...] = jnp.broadcast_to(jnp.sum(x_ref[...], axis=0)[None], o_ref.shape)


def softmax_kernel(scale, x_ref, o_ref):
    s = jnp.sum(x_ref[...], axis=0) * scale
    lane = lax.broadcasted_iota(jnp.int32, s.shape, 1)
    s = jnp.where(lane < TOTAL, s, -jnp.inf)
    e = jnp.exp(s - jnp.max(s, axis=1, keepdims=True))
    w = e / jnp.sum(e, axis=1, keepdims=True)
    o_ref[...] = jnp.broadcast_to(w.astype(BF16).astype(F32)[None], o_ref.shape)


def mix_kernel(w_ref, v_ref, o_ref, ws, vs, ms):
    for s in range(MEM):
        ws[s * OWN : (s + 1) * OWN, :] = w_ref[s, 0:OWN, :]
    w = ws[...].astype(BF16)[:, :TOTAL]
    vs[...] = v_ref[:, :, CQ:, :].astype(F32).reshape(TOTAL * ROWS, LAT)
    v = jnp.concatenate([vs[pl.ds(r, TOTAL, stride=ROWS), :].astype(BF16) for r in range(ROWS)], axis=1)
    mixed = jnp.dot(w, v, preferred_element_type=F32)
    for r in range(ROWS):
        ms[pl.ds(r, TOTAL, stride=ROWS), :] = mixed[:, r * LAT : (r + 1) * LAT]
    o_ref[...] = ms[...].astype(BF16).reshape(o_ref.shape)


def finish_kernel(x_ref, f_ref, w_ref, o_ref, mc, mb, ma, br):
    for m in range(OWN):
        for j in range(MEM):
            mc[j * ROWS : (j + 1) * ROWS] = x_ref[j, m].astype(F32)
        mb[...], ma[...] = lat_shifts(mc[...])
        for i in range(0, COLS, 2):
            patches = []
            for col in (i, i + 1):
                parts = [
                    t[(col + a) * CQ : (col + a + 1) * CQ, :] for a in range(3) for t in (mb, mc, ma)
                ]
                patches.append(jnp.concatenate(parts, axis=0).astype(BF16))
            r = jnp.dot(w_ref[...], jnp.concatenate(patches, axis=1), preferred_element_type=F32)
            for s in range(2):
                br[pl.ds(i + s, CH, stride=COLS), :] = r[:, s * LAT : (s + 1) * LAT]
        o_ref[m] = (f_ref[m].astype(F32) + br[...].reshape(CH, COLS, LAT)).astype(BF16)


def shards(fields, w_query, w_key, w_value, w_out):
    edge = jax.ShapeDtypeStruct((OWN, 2 * CH, LAT), BF16)
    plane = pltpu.VMEM((CH * COLS, LAT), F32)
    sib, nb = call(edges_kernel, (edge, edge), [plane], 0, 1_000_000, fields)
    swaps = [(i, (i - 1 if i % 2 == 0 else i + 1) % LON) for i in range(LON)]
    got_nb = lax.ppermute(nb, ("chip", "core"), swaps)
    got_sib = lax.all_gather(sib, "core", axis=0, tiled=False)
    packed = jax.ShapeDtypeStruct((MEM, OWN, CQ + ROWS, LAT), BF16)
    pair = jax.ShapeDtypeStruct((18 * CQ, 4 * CH), BF16)
    part, w_pair = call(
        inner_kernel,
        (packed, pair),
        [
            pltpu.VMEM((3 * CQ, 9 * CH), F32),
            plane,
            pltpu.VMEM((CH * COLS, LAT), BF16),
            pltpu.VMEM((2 * CQ, LAT), F32),
        ],
        450_000_000,
        2_000_000,
        fields,
        w_query,
        w_key,
        w_value,
    )
    qkv = call(
        outer_kernel,
        packed,
        [pltpu.VMEM((OWN, 4 * CH, LAT), BF16)] * 2 + [pltpu.VMEM((2 * CQ, LAT), F32)],
        300_000_000,
        1_500_000,
        part,
        w_pair,
        sib,
        nb,
        got_sib,
        got_nb,
        alias={0: 0},
    )
    qkv = lax.all_to_all(qkv, "mem", 0, 0, tiled=True)

    tile = (8, LAT)
    gram = call(
        gram_kernel,
        jax.ShapeDtypeStruct((MEM, *tile), F32),
        [pltpu.VMEM((TOTAL * CQ, LAT), F32), pltpu.VMEM((TOTAL, LAT), F32)],
        20_000_000,
        600_000,
        qkv,
    )
    gram = lax.all_to_all(gram, "mem", 0, 0, tiled=True)
    gram = call(spread_kernel, jax.ShapeDtypeStruct((LON, *tile), F32), [], 20_000, 200_000, gram)
    gram = lax.all_to_all(gram, ("chip", "core"), 0, 0, tiled=True)
    scale = 1.0 / math.sqrt(CQ * LAT * COLS * LON)
    weights = call(
        functools.partial(softmax_kernel, scale),
        jax.ShapeDtypeStruct((MEM, *tile), F32),
        [],
        40_000,
        200_000,
        gram,
    )
    weights = lax.all_to_all(weights, "mem", 0, 0, tiled=True)
    mixed = call(
        mix_kernel,
        jax.ShapeDtypeStruct((MEM, OWN, ROWS, LAT), BF16),
        [
            pltpu.VMEM((TOTAL, LAT), F32),
            pltpu.VMEM((TOTAL * ROWS, LAT), F32),
            pltpu.VMEM((TOTAL * ROWS, LAT), F32),
        ],
        30_000_000,
        700_000,
        weights,
        qkv,
    )
    mixed = lax.all_to_all(mixed, "mem", 0, 0, tiled=True)
    return call(
        finish_kernel,
        jax.ShapeDtypeStruct(fields.shape, BF16),
        [pltpu.VMEM((MEM * ROWS, LAT), F32)] * 3 + [pltpu.VMEM((CH * COLS, LAT), F32)],
        150_000_000,
        1_700_000,
        mixed,
        fields,
        w_out,
    )


def solution(mesh):
    fine = Mesh(mesh.devices.reshape(MEM, LON // 2, 2), ("mem", "chip", "core"))
    spec = P("mem", None, ("chip", "core"), None)
    return jax.shard_map(
        shards,
        mesh=fine,
        in_specs=(spec, P(), P(), P(), P()),
        out_specs=spec,
        check_vma=False,
    )
```

```python
import functools
import math

import jax
import jax.numpy as jnp
from jax import lax
from jax.experimental import pallas as pl
from jax.experimental.pallas import tpu as pltpu
from jax.sharding import Mesh
from jax.sharding import PartitionSpec as P

CH, CQ, LAT = 64, 24, 128
HALF = CQ // 2
MEM, LON = 16, 32
OWN = 5
TOTAL = MEM * OWN
PART = TOTAL // 2
COLS = 8
EXT = COLS + 2
ROWS = 16
F32, BF16 = jnp.float32, jnp.bfloat16
VMEM = pl.BlockSpec(memory_space=pltpu.VMEM)


def call(body, outs, scratch, flops, nbytes, *args, alias=None):
    many = isinstance(outs, tuple)
    return pl.pallas_call(
        body,
        out_shape=outs,
        in_specs=[VMEM] * len(args),
        out_specs=(VMEM,) * len(outs) if many else VMEM,
        scratch_shapes=scratch,
        input_output_aliases=alias or {},
        compiler_params=pltpu.CompilerParams(vmem_limit_bytes=32 * 1024 * 1024),
        cost_estimate=pl.CostEstimate(flops=flops, bytes_accessed=nbytes, transcendentals=0),
    )(*args)


def lat_shifts(x):
    lane = lax.broadcasted_iota(jnp.int32, x.shape, 1)
    before = jnp.where(lane == 0, 0.0, pltpu.roll(x, 1, 1))
    after = jnp.where(lane == LAT - 1, 0.0, pltpu.roll(x, LAT - 1, 1))
    return before, after


def edges_kernel(f_ref, sib_ref, nb_ref, xf):
    even = lax.axis_index("core") == 0
    for m in range(OWN):
        xf[...] = f_ref[m].astype(F32).reshape(CH * COLS, LAT)
        for s in range(2):
            left = xf[pl.ds(s, CH, stride=COLS), :]
            right = xf[pl.ds(COLS - 2 + s, CH, stride=COLS), :]
            sib_ref[m, s * CH : (s + 1) * CH] = jnp.where(even, right, left).astype(BF16)
            nb_ref[m, s * CH : (s + 1) * CH] = jnp.where(even, left, right).astype(BF16)


def conv_pair(w, x):
    width = 3 * CQ
    lane = lax.broadcasted_iota(jnp.int32, (width, LAT), 1)
    r = jnp.dot(w, x, preferred_element_type=F32)
    outs = []
    for s in range(2):
        y = [r[(3 * s + b) * width : (3 * s + b + 1) * width] for b in range(3)]
        outs.append(
            y[1]
            + jnp.where(lane == 0, 0.0, pltpu.roll(y[0], 1, 1))
            + jnp.where(lane == LAT - 1, 0.0, pltpu.roll(y[2], LAT - 1, 1))
        )
    return outs


def put_pair(o_ref, vs, m, p, outs):
    for s in range(2):
        col = 2 * p + s
        vs[s * CQ : (s + 1) * CQ] = outs[s][2 * CQ :]
        if 1 <= col <= COLS:
            for h in range(2):
                o_ref[2 * (col - 1) + h, m, 0:CQ] = outs[s][h * CQ : (h + 1) * CQ].astype(BF16)
    for j in range(3):
        o_ref[3 * p + j, m, CQ:] = vs[j * ROWS : (j + 1) * ROWS].astype(BF16)


def inner_kernel(f_ref, wq_ref, wk_ref, wv_ref, o_ref, wp_ref, ws, xf, xt, vs):
    ws[0:HALF] = wq_ref[...].astype(F32)[:HALF]
    ws[HALF : 2 * HALF] = wk_ref[...].astype(F32)[:HALF]
    ws[2 * HALF : 3 * HALF] = wq_ref[...].astype(F32)[HALF:]
    ws[3 * HALF : 4 * HALF] = wk_ref[...].astype(F32)[HALF:]
    ws[2 * CQ :] = wv_ref[...].astype(F32)
    zero = jnp.zeros((3 * CQ, CH), F32)
    for b in range(3):
        taps = [ws[:, (3 * a + b) * CH : (3 * a + b + 1) * CH] for a in range(3)]
        for s in range(2):
            row = (3 * s + b) * 3 * CQ
            full = [zero] + taps if s else taps + [zero]
            wp_ref[row : row + 3 * CQ] = jnp.concatenate(full, axis=1).astype(BF16)
    for m in range(OWN):
        xf[...] = f_ref[m].astype(F32).reshape(CH * COLS, LAT)
        for i in range(COLS):
            xt[i * CH : (i + 1) * CH] = xf[pl.ds(i, CH, stride=COLS), :].astype(BF16)
        for p in range(1, EXT // 2 - 1):
            x = xt[2 * (p - 1) * CH : 2 * (p + 1) * CH]
            put_pair(o_ref, vs, m, p, conv_pair(wp_ref[...], x))


def outer_kernel(i_ref, wp_ref, sib_ref, nb_ref, gs_ref, gn_ref, o_ref, xl, xr, vs):
    core = lax.axis_index("core")
    near = 2 * CH

    @pl.when(core == 0)
    def _():
        xl[:, :near] = gn_ref[...]
        xl[:, near:] = nb_ref[...]
        xr[:, :near] = sib_ref[...]
        xr[:, near:] = gs_ref[1]

    @pl.when(core == 1)
    def _():
        xl[:, :near] = gs_ref[0]
        xl[:, near:] = sib_ref[...]
        xr[:, :near] = nb_ref[...]
        xr[:, near:] = gn_ref[...]

    for m in range(OWN):
        put_pair(o_ref, vs, m, 0, conv_pair(wp_ref[...], xl[m]))
        put_pair(o_ref, vs, m, EXT // 2 - 1, conv_pair(wp_ref[...], xr[m]))
        o_ref[MEM - 1, m, CQ:] = jnp.zeros((ROWS, LAT), BF16)


def gram_kernel(x_ref, g_ref, xs):
    xs[...] = x_ref[:, :, 0:CQ, :].astype(F32).reshape(TOTAL * CQ, LAT)
    pad = jnp.zeros((LAT - TOTAL, LAT), BF16)
    q, k = [], []
    for r in range(HALF):
        q.append(xs[pl.ds(r, TOTAL, stride=CQ), :].astype(BF16))
        k.append(jnp.concatenate([xs[pl.ds(HALF + r, TOTAL, stride=CQ), :].astype(BF16), pad], axis=0))
    g_ref[...] = lax.dot_general(
        jnp.concatenate(q, axis=1),
        jnp.concatenate(k, axis=1),
        (((1,), (1,)), ((), ())),
        preferred_element_type=F32,
    )


def halve_kernel(x_ref, o_ref):
    rows = pl.ds(pl.multiple_of(lax.axis_index("core") * PART, 8), PART)
    o_ref[...] = jnp.broadcast_to((x_ref[0, rows, :] + x_ref[1, rows, :])[None], o_ref.shape)


def spread_kernel(x_ref, o_ref):
    o_ref[...] = jnp.broadcast_to(jnp.sum(x_ref[...], axis=0)[None], o_ref.shape)


def softmax_kernel(scale, x_ref, o_ref):
    s = jnp.sum(x_ref[...], axis=0) * scale
    lane = lax.broadcasted_iota(jnp.int32, s.shape, 1)
    s = jnp.where(lane < TOTAL, s, -jnp.inf)
    e = jnp.exp(s - jnp.max(s, axis=1, keepdims=True))
    w = e / jnp.sum(e, axis=1, keepdims=True)
    o_ref[...] = w.astype(BF16)


def mix_kernel(w_ref, v_ref, o_ref, vs, ms):
    w = w_ref[...].astype(F32).reshape(TOTAL, LAT).astype(BF16)[:, :TOTAL]
    vs[...] = v_ref[:, :, CQ:, :].astype(F32).reshape(TOTAL * ROWS, LAT)
    v = jnp.concatenate([vs[pl.ds(r, TOTAL, stride=ROWS), :].astype(BF16) for r in range(ROWS)], axis=1)
    mixed = jnp.dot(w, v, preferred_element_type=F32)
    for r in range(ROWS):
        ms[pl.ds(r, TOTAL, stride=ROWS), :] = mixed[:, r * LAT : (r + 1) * LAT]
    o_ref[...] = ms[...].astype(BF16).reshape(o_ref.shape)


def finish_kernel(x_ref, f_ref, w_ref, o_ref, mc, mb, ma, br):
    for m in range(OWN):
        for j in range(MEM):
            mc[j * ROWS : (j + 1) * ROWS] = x_ref[j, m].astype(F32)
        mb[...], ma[...] = lat_shifts(mc[...])
        for i in range(0, COLS, 2):
            patches = []
            for col in (i, i + 1):
                parts = [
                    t[(col + a) * CQ : (col + a + 1) * CQ, :] for a in range(3) for t in (mb, mc, ma)
                ]
                patches.append(jnp.concatenate(parts, axis=0).astype(BF16))
            r = jnp.dot(w_ref[...], jnp.concatenate(patches, axis=1), preferred_element_type=F32)
            for s in range(2):
                br[pl.ds(i + s, CH, stride=COLS), :] = r[:, s * LAT : (s + 1) * LAT]
        o_ref[m] = (f_ref[m].astype(F32) + br[...].reshape(CH, COLS, LAT)).astype(BF16)


def shards(fields, w_query, w_key, w_value, w_out):
    edge = jax.ShapeDtypeStruct((OWN, 2 * CH, LAT), BF16)
    plane = pltpu.VMEM((CH * COLS, LAT), F32)
    sib, nb = call(edges_kernel, (edge, edge), [plane], 0, 1_000_000, fields)
    swaps = [(i, (i - 1 if i % 2 == 0 else i + 1) % LON) for i in range(LON)]
    got_nb = lax.ppermute(nb, ("chip", "core"), swaps)
    got_sib = lax.all_gather(sib, "core", axis=0, tiled=False)
    packed = jax.ShapeDtypeStruct((MEM, OWN, CQ + ROWS, LAT), BF16)
    pair = jax.ShapeDtypeStruct((18 * CQ, 4 * CH), BF16)
    part, w_pair = call(
        inner_kernel,
        (packed, pair),
        [
            pltpu.VMEM((3 * CQ, 9 * CH), F32),
            plane,
            pltpu.VMEM((CH * COLS, LAT), BF16),
            pltpu.VMEM((2 * CQ, LAT), F32),
        ],
        450_000_000,
        2_000_000,
        fields,
        w_query,
        w_key,
        w_value,
    )
    qkv = call(
        outer_kernel,
        packed,
        [pltpu.VMEM((OWN, 4 * CH, LAT), BF16)] * 2 + [pltpu.VMEM((2 * CQ, LAT), F32)],
        300_000_000,
        1_500_000,
        part,
        w_pair,
        sib,
        nb,
        got_sib,
        got_nb,
        alias={0: 0},
    )
    qkv = lax.all_to_all(qkv, "mem", 0, 0, tiled=True)

    gram = call(
        gram_kernel,
        jax.ShapeDtypeStruct((TOTAL, LAT), F32),
        [pltpu.VMEM((TOTAL * CQ, LAT), F32)],
        20_000_000,
        600_000,
        qkv,
    )
    gram = lax.all_gather(gram, "core", axis=0, tiled=False)
    copies = jax.ShapeDtypeStruct((MEM, PART, LAT), F32)
    gram = call(halve_kernel, copies, [], 20_000, 200_000, gram)
    gram = lax.all_to_all(gram, "chip", 0, 0, tiled=True)
    gram = call(spread_kernel, copies, [], 80_000, 400_000, gram)
    gram = lax.all_to_all(gram, "mem", 0, 0, tiled=True)
    scale = 1.0 / math.sqrt(CQ * LAT * COLS * LON)
    weights = call(
        functools.partial(softmax_kernel, scale),
        jax.ShapeDtypeStruct((PART, LAT), BF16),
        [],
        100_000,
        200_000,
        gram,
    )
    weights = lax.all_gather(weights, "core", axis=0, tiled=False)
    mixed = call(
        mix_kernel,
        jax.ShapeDtypeStruct((MEM, OWN, ROWS, LAT), BF16),
        [
            pltpu.VMEM((TOTAL * ROWS, LAT), F32),
            pltpu.VMEM((TOTAL * ROWS, LAT), F32),
        ],
        30_000_000,
        700_000,
        weights,
        qkv,
    )
    mixed = lax.all_to_all(mixed, "mem", 0, 0, tiled=True)
    return call(
        finish_kernel,
        jax.ShapeDtypeStruct(fields.shape, BF16),
        [pltpu.VMEM((MEM * ROWS, LAT), F32)] * 3 + [pltpu.VMEM((CH * COLS, LAT), F32)],
        150_000_000,
        1_700_000,
        mixed,
        fields,
        w_out,
    )


def solution(mesh):
    fine = Mesh(mesh.devices.reshape(MEM, LON // 2, 2), ("mem", "chip", "core"))
    spec = P("mem", None, ("chip", "core"), None)
    return jax.shard_map(
        shards,
        mesh=fine,
        in_specs=(spec, P(), P(), P(), P()),
        out_specs=spec,
        check_vma=False,
    )
```

```python
import functools
import math

import jax
import jax.numpy as jnp
from jax import lax
from jax.experimental import pallas as pl
from jax.experimental.pallas import tpu as pltpu
from jax.sharding import Mesh
from jax.sharding import PartitionSpec as P

CH, CQ, LAT = 64, 24, 128
HALF = CQ // 2
MEM, LON = 16, 32
OWN = 5
TOTAL = MEM * OWN
NEAR = 8
BAND = TOTAL // NEAR
CUT = LAT - TOTAL
COLS = 8
EXT = COLS + 2
ROWS = 16
F32, BF16 = jnp.float32, jnp.bfloat16
VMEM = pl.BlockSpec(memory_space=pltpu.VMEM)


def call(body, outs, scratch, flops, nbytes, *args, alias=None):
    many = isinstance(outs, tuple)
    return pl.pallas_call(
        body,
        out_shape=outs,
        in_specs=[VMEM] * len(args),
        out_specs=(VMEM,) * len(outs) if many else VMEM,
        scratch_shapes=scratch,
        input_output_aliases=alias or {},
        compiler_params=pltpu.CompilerParams(vmem_limit_bytes=32 * 1024 * 1024),
        cost_estimate=pl.CostEstimate(flops=flops, bytes_accessed=nbytes, transcendentals=0),
    )(*args)


def lat_shifts(x):
    lane = lax.broadcasted_iota(jnp.int32, x.shape, 1)
    before = jnp.where(lane == 0, 0.0, pltpu.roll(x, 1, 1))
    after = jnp.where(lane == LAT - 1, 0.0, pltpu.roll(x, LAT - 1, 1))
    return before, after


def edges_kernel(f_ref, sib_ref, nb_ref, xf):
    even = lax.axis_index("core") == 0
    for m in range(OWN):
        xf[...] = f_ref[m].astype(F32).reshape(CH * COLS, LAT)
        for s in range(2):
            left = xf[pl.ds(s, CH, stride=COLS), :]
            right = xf[pl.ds(COLS - 2 + s, CH, stride=COLS), :]
            sib_ref[m, s * CH : (s + 1) * CH] = jnp.where(even, right, left).astype(BF16)
            nb_ref[m, s * CH : (s + 1) * CH] = jnp.where(even, left, right).astype(BF16)


def conv_pair(w, x):
    width = 3 * CQ
    lane = lax.broadcasted_iota(jnp.int32, (width, LAT), 1)
    r = jnp.dot(w, x, preferred_element_type=F32)
    outs = []
    for s in range(2):
        y = [r[(3 * s + b) * width : (3 * s + b + 1) * width] for b in range(3)]
        outs.append(
            y[1]
            + jnp.where(lane == 0, 0.0, pltpu.roll(y[0], 1, 1))
            + jnp.where(lane == LAT - 1, 0.0, pltpu.roll(y[2], LAT - 1, 1))
        )
    return outs


def put_pair(o_ref, vs, m, p, outs):
    for s in range(2):
        col = 2 * p + s
        vs[s * CQ : (s + 1) * CQ] = outs[s][2 * CQ :]
        if 1 <= col <= COLS:
            for h in range(2):
                o_ref[2 * (col - 1) + h, m, 0:CQ] = outs[s][h * CQ : (h + 1) * CQ].astype(BF16)
    for j in range(3):
        o_ref[3 * p + j, m, CQ:] = vs[j * ROWS : (j + 1) * ROWS].astype(BF16)


def inner_kernel(f_ref, wq_ref, wk_ref, wv_ref, o_ref, wp_ref, ws, xf, xt, vs):
    ws[0:HALF] = wq_ref[...].astype(F32)[:HALF]
    ws[HALF : 2 * HALF] = wk_ref[...].astype(F32)[:HALF]
    ws[2 * HALF : 3 * HALF] = wq_ref[...].astype(F32)[HALF:]
    ws[3 * HALF : 4 * HALF] = wk_ref[...].astype(F32)[HALF:]
    ws[2 * CQ :] = wv_ref[...].astype(F32)
    zero = jnp.zeros((3 * CQ, CH), F32)
    for b in range(3):
        taps = [ws[:, (3 * a + b) * CH : (3 * a + b + 1) * CH] for a in range(3)]
        for s in range(2):
            row = (3 * s + b) * 3 * CQ
            full = [zero] + taps if s else taps + [zero]
            wp_ref[row : row + 3 * CQ] = jnp.concatenate(full, axis=1).astype(BF16)
    for m in range(OWN):
        xf[...] = f_ref[m].astype(F32).reshape(CH * COLS, LAT)
        for i in range(COLS):
            xt[i * CH : (i + 1) * CH] = xf[pl.ds(i, CH, stride=COLS), :].astype(BF16)
        for p in range(1, EXT // 2 - 1):
            x = xt[2 * (p - 1) * CH : 2 * (p + 1) * CH]
            put_pair(o_ref, vs, m, p, conv_pair(wp_ref[...], x))


def outer_kernel(i_ref, wp_ref, sib_ref, nb_ref, gs_ref, gn_ref, o_ref, xl, xr, vs):
    core = lax.axis_index("core")
    near = 2 * CH

    @pl.when(core == 0)
    def _():
        xl[:, :near] = gn_ref[...]
        xl[:, near:] = nb_ref[...]
        xr[:, :near] = sib_ref[...]
        xr[:, near:] = gs_ref[1]

    @pl.when(core == 1)
    def _():
        xl[:, :near] = gs_ref[0]
        xl[:, near:] = sib_ref[...]
        xr[:, :near] = nb_ref[...]
        xr[:, near:] = gn_ref[...]

    for m in range(OWN):
        put_pair(o_ref, vs, m, 0, conv_pair(wp_ref[...], xl[m]))
        put_pair(o_ref, vs, m, EXT // 2 - 1, conv_pair(wp_ref[...], xr[m]))
        o_ref[MEM - 1, m, CQ:] = jnp.zeros((ROWS, LAT), BF16)


def gram_kernel(x_ref, g_ref, xs, gs):
    xs[...] = x_ref[:, :, 0:CQ, :].astype(F32).reshape(TOTAL * CQ, LAT)
    pad = jnp.zeros((LAT - TOTAL, LAT), BF16)
    q, k = [], []
    for r in range(HALF):
        q.append(xs[pl.ds(r, TOTAL, stride=CQ), :].astype(BF16))
        k.append(jnp.concatenate([xs[pl.ds(HALF + r, TOTAL, stride=CQ), :].astype(BF16), pad], axis=0))
    gram = lax.dot_general(
        jnp.concatenate(q, axis=1),
        jnp.concatenate(k, axis=1),
        (((1,), (1,)), ((), ())),
        preferred_element_type=F32,
    )
    lane = lax.broadcasted_iota(jnp.int32, gram.shape, 1)
    gs[0] = gram
    gs[1] = jnp.where(lane < TOTAL, 0.0, pltpu.roll(gram, TOTAL, 1))
    gs[2] = jnp.where(lane < TOTAL, 0.0, pltpu.roll(gram, TOTAL - CUT, 1))
    rest = jnp.zeros((4, LAT), F32)
    for s in range(NEAR):
        row = s * BAND
        free = [gs[1 + h, row + 8 + e : row + 9 + e, :] for e in range(2) for h in range(2)]
        g_ref[s] = gs[0, row : row + 8, :] + jnp.concatenate(free + [rest], axis=0)


def spread_kernel(x_ref, o_ref):
    o_ref[...] = jnp.broadcast_to(jnp.sum(x_ref[...], axis=0)[None], o_ref.shape)


def mix_kernel(scale, g_ref, v_ref, o_ref, ws, vs, ms):
    lane = lax.broadcasted_iota(jnp.int32, (8, LAT), 1)
    for s in range(NEAR):
        tile = g_ref[s]
        head, tail = pltpu.roll(tile, LAT - TOTAL, 1), pltpu.roll(tile, LAT - TOTAL + CUT, 1)
        ws[s * BAND : s * BAND + 8] = tile
        for e in range(2):
            row = jnp.where(lane[:1] < CUT, head[2 * e : 2 * e + 1], tail[2 * e + 1 : 2 * e + 2])
            ws[s * BAND + 8 + e : s * BAND + 9 + e] = row
    lane = lax.broadcasted_iota(jnp.int32, (TOTAL, LAT), 1)
    s = jnp.where(lane < TOTAL, ws[...] * scale, -jnp.inf)
    e = jnp.exp(s - jnp.max(s, axis=1, keepdims=True))
    w = (e / jnp.sum(e, axis=1, keepdims=True)).astype(BF16)[:, :TOTAL]
    vs[...] = v_ref[:, :, CQ:, :].astype(F32).reshape(TOTAL * ROWS, LAT)
    v = jnp.concatenate([vs[pl.ds(r, TOTAL, stride=ROWS), :].astype(BF16) for r in range(ROWS)], axis=1)
    mixed = jnp.dot(w, v, preferred_element_type=F32)
    for r in range(ROWS):
        ms[pl.ds(r, TOTAL, stride=ROWS), :] = mixed[:, r * LAT : (r + 1) * LAT]
    o_ref[...] = ms[...].astype(BF16).reshape(o_ref.shape)


def finish_kernel(x_ref, f_ref, w_ref, o_ref, mc, mb, ma, br):
    for m in range(OWN):
        for j in range(MEM):
            mc[j * ROWS : (j + 1) * ROWS] = x_ref[j, m].astype(F32)
        mb[...], ma[...] = lat_shifts(mc[...])
        for i in range(0, COLS, 2):
            patches = []
            for col in (i, i + 1):
                parts = [
                    t[(col + a) * CQ : (col + a + 1) * CQ, :] for a in range(3) for t in (mb, mc, ma)
                ]
                patches.append(jnp.concatenate(parts, axis=0).astype(BF16))
            r = jnp.dot(w_ref[...], jnp.concatenate(patches, axis=1), preferred_element_type=F32)
            for s in range(2):
                br[pl.ds(i + s, CH, stride=COLS), :] = r[:, s * LAT : (s + 1) * LAT]
        o_ref[m] = (f_ref[m].astype(F32) + br[...].reshape(CH, COLS, LAT)).astype(BF16)


def shards(fields, w_query, w_key, w_value, w_out):
    edge = jax.ShapeDtypeStruct((OWN, 2 * CH, LAT), BF16)
    plane = pltpu.VMEM((CH * COLS, LAT), F32)
    sib, nb = call(edges_kernel, (edge, edge), [plane], 0, 1_000_000, fields)
    swaps = [(i, (i - 1 if i % 2 == 0 else i + 1) % LON) for i in range(LON)]
    got_nb = lax.ppermute(nb, ("yhi", "x", "core"), swaps)
    got_sib = lax.all_gather(sib, "core", axis=0, tiled=False)
    packed = jax.ShapeDtypeStruct((MEM, OWN, CQ + ROWS, LAT), BF16)
    pair = jax.ShapeDtypeStruct((18 * CQ, 4 * CH), BF16)
    part, w_pair = call(
        inner_kernel,
        (packed, pair),
        [
            pltpu.VMEM((3 * CQ, 9 * CH), F32),
            plane,
            pltpu.VMEM((CH * COLS, LAT), BF16),
            pltpu.VMEM((2 * CQ, LAT), F32),
        ],
        450_000_000,
        2_000_000,
        fields,
        w_query,
        w_key,
        w_value,
    )
    qkv = call(
        outer_kernel,
        packed,
        [pltpu.VMEM((OWN, 4 * CH, LAT), BF16)] * 2 + [pltpu.VMEM((2 * CQ, LAT), F32)],
        300_000_000,
        1_500_000,
        part,
        w_pair,
        sib,
        nb,
        got_sib,
        got_nb,
        alias={0: 0},
    )
    qkv = lax.all_to_all(qkv, "mem", 0, 0, tiled=True)

    near, far = ("x", "core"), ("mem", "yhi")
    tiles = jax.ShapeDtypeStruct((NEAR, 8, LAT), F32)
    copies = jax.ShapeDtypeStruct((MEM * LON // NEAR, 8, LAT), F32)
    gram = call(
        gram_kernel,
        tiles,
        [pltpu.VMEM((TOTAL * CQ, LAT), F32), pltpu.VMEM((3, TOTAL, LAT), F32)],
        20_000_000,
        600_000,
        qkv,
    )
    gram = lax.all_to_all(gram, near, 0, 0, tiled=True)
    gram = call(spread_kernel, copies, [], 20_000, 300_000, gram)
    gram = lax.all_to_all(gram, far, 0, 0, tiled=True)
    gram = call(spread_kernel, tiles, [], 80_000, 300_000, gram)
    gram = lax.all_to_all(gram, near, 0, 0, tiled=True)
    scale = 1.0 / math.sqrt(CQ * LAT * COLS * LON)
    mixed = call(
        functools.partial(mix_kernel, scale),
        jax.ShapeDtypeStruct((MEM, OWN, ROWS, LAT), BF16),
        [
            pltpu.VMEM((TOTAL, LAT), F32),
            pltpu.VMEM((TOTAL * ROWS, LAT), F32),
            pltpu.VMEM((TOTAL * ROWS, LAT), F32),
        ],
        30_000_000,
        700_000,
        gram,
        qkv,
    )
    mixed = lax.all_to_all(mixed, "mem", 0, 0, tiled=True)
    return call(
        finish_kernel,
        jax.ShapeDtypeStruct(fields.shape, BF16),
        [pltpu.VMEM((MEM * ROWS, LAT), F32)] * 3 + [pltpu.VMEM((CH * COLS, LAT), F32)],
        150_000_000,
        1_700_000,
        mixed,
        fields,
        w_out,
    )


def solution(mesh):
    fine = Mesh(mesh.devices.reshape(MEM, LON // NEAR, NEAR // 2, 2), ("mem", "yhi", "x", "core"))
    spec = P("mem", None, ("yhi", "x", "core"), None)
    return jax.shard_map(
        shards,
        mesh=fine,
        in_specs=(spec, P(), P(), P(), P()),
        out_specs=spec,
        check_vma=False,
    )
```

```python
import functools
import math

import jax
import jax.numpy as jnp
from jax import lax
from jax.experimental import pallas as pl
from jax.experimental.pallas import tpu as pltpu
from jax.sharding import Mesh
from jax.sharding import PartitionSpec as P

CH, CQ, LAT = 64, 24, 128
HALF = CQ // 2
MEM, LON = 16, 32
OWN = 5
TOTAL = MEM * OWN
NEAR = 16
BAND = TOTAL // NEAR
CUT = LAT - TOTAL
COLS = 8
EXT = COLS + 2
ROWS = 16
F32, BF16 = jnp.float32, jnp.bfloat16
VMEM = pl.BlockSpec(memory_space=pltpu.VMEM)


def call(body, outs, scratch, flops, nbytes, *args, alias=None):
    many = isinstance(outs, tuple)
    return pl.pallas_call(
        body,
        out_shape=outs,
        in_specs=[VMEM] * len(args),
        out_specs=(VMEM,) * len(outs) if many else VMEM,
        scratch_shapes=scratch,
        input_output_aliases=alias or {},
        compiler_params=pltpu.CompilerParams(vmem_limit_bytes=32 * 1024 * 1024),
        cost_estimate=pl.CostEstimate(flops=flops, bytes_accessed=nbytes, transcendentals=0),
    )(*args)


def lat_shifts(x):
    lane = lax.broadcasted_iota(jnp.int32, x.shape, 1)
    before = jnp.where(lane == 0, 0.0, pltpu.roll(x, 1, 1))
    after = jnp.where(lane == LAT - 1, 0.0, pltpu.roll(x, LAT - 1, 1))
    return before, after


def edges_kernel(f_ref, sib_ref, nb_ref, xf):
    even = lax.axis_index("core") == 0
    for m in range(OWN):
        xf[...] = f_ref[m].astype(F32).reshape(CH * COLS, LAT)
        for s in range(2):
            left = xf[pl.ds(s, CH, stride=COLS), :]
            right = xf[pl.ds(COLS - 2 + s, CH, stride=COLS), :]
            sib_ref[m, s * CH : (s + 1) * CH] = jnp.where(even, right, left).astype(BF16)
            nb_ref[m, s * CH : (s + 1) * CH] = jnp.where(even, left, right).astype(BF16)


def conv_pair(w, x):
    width = 3 * CQ
    lane = lax.broadcasted_iota(jnp.int32, (width, LAT), 1)
    r = jnp.dot(w, x, preferred_element_type=F32)
    outs = []
    for s in range(2):
        y = [r[(3 * s + b) * width : (3 * s + b + 1) * width] for b in range(3)]
        outs.append(
            y[1]
            + jnp.where(lane == 0, 0.0, pltpu.roll(y[0], 1, 1))
            + jnp.where(lane == LAT - 1, 0.0, pltpu.roll(y[2], LAT - 1, 1))
        )
    return outs


def put_pair(o_ref, vs, m, p, outs):
    for s in range(2):
        col = 2 * p + s
        vs[s * CQ : (s + 1) * CQ] = outs[s][2 * CQ :]
        if 1 <= col <= COLS:
            for h in range(2):
                o_ref[2 * (col - 1) + h, m, 0:CQ] = outs[s][h * CQ : (h + 1) * CQ].astype(BF16)
    for j in range(3):
        o_ref[3 * p + j, m, CQ:] = vs[j * ROWS : (j + 1) * ROWS].astype(BF16)


def inner_kernel(f_ref, wq_ref, wk_ref, wv_ref, o_ref, wp_ref, ws, xf, xt, vs):
    ws[0:HALF] = wq_ref[...].astype(F32)[:HALF]
    ws[HALF : 2 * HALF] = wk_ref[...].astype(F32)[:HALF]
    ws[2 * HALF : 3 * HALF] = wq_ref[...].astype(F32)[HALF:]
    ws[3 * HALF : 4 * HALF] = wk_ref[...].astype(F32)[HALF:]
    ws[2 * CQ :] = wv_ref[...].astype(F32)
    zero = jnp.zeros((3 * CQ, CH), F32)
    for b in range(3):
        taps = [ws[:, (3 * a + b) * CH : (3 * a + b + 1) * CH] for a in range(3)]
        for s in range(2):
            row = (3 * s + b) * 3 * CQ
            full = [zero] + taps if s else taps + [zero]
            wp_ref[row : row + 3 * CQ] = jnp.concatenate(full, axis=1).astype(BF16)
    for m in range(OWN):
        xf[...] = f_ref[m].astype(F32).reshape(CH * COLS, LAT)
        for i in range(COLS):
            xt[i * CH : (i + 1) * CH] = xf[pl.ds(i, CH, stride=COLS), :].astype(BF16)
        for p in range(1, EXT // 2 - 1):
            x = xt[2 * (p - 1) * CH : 2 * (p + 1) * CH]
            put_pair(o_ref, vs, m, p, conv_pair(wp_ref[...], x))


def outer_kernel(i_ref, wp_ref, sib_ref, nb_ref, gs_ref, gn_ref, o_ref, xl, xr, vs):
    core = lax.axis_index("core")
    near = 2 * CH

    @pl.when(core == 0)
    def _():
        xl[:, :near] = gn_ref[...]
        xl[:, near:] = nb_ref[...]
        xr[:, :near] = sib_ref[...]
        xr[:, near:] = gs_ref[1]

    @pl.when(core == 1)
    def _():
        xl[:, :near] = gs_ref[0]
        xl[:, near:] = sib_ref[...]
        xr[:, :near] = nb_ref[...]
        xr[:, near:] = gn_ref[...]

    for m in range(OWN):
        put_pair(o_ref, vs, m, 0, conv_pair(wp_ref[...], xl[m]))
        put_pair(o_ref, vs, m, EXT // 2 - 1, conv_pair(wp_ref[...], xr[m]))
        o_ref[MEM - 1, m, CQ:] = jnp.zeros((ROWS, LAT), BF16)


def gram_kernel(x_ref, g_ref, xs, gs):
    xs[...] = x_ref[:, :, 0:CQ, :].astype(F32).reshape(TOTAL * CQ, LAT)
    pad = jnp.zeros((LAT - TOTAL, LAT), BF16)
    q, k = [], []
    for r in range(HALF):
        q.append(xs[pl.ds(r, TOTAL, stride=CQ), :].astype(BF16))
        k.append(jnp.concatenate([xs[pl.ds(HALF + r, TOTAL, stride=CQ), :].astype(BF16), pad], axis=0))
    gram = lax.dot_general(
        jnp.concatenate(q, axis=1),
        jnp.concatenate(k, axis=1),
        (((1,), (1,)), ((), ())),
        preferred_element_type=F32,
    )
    lane = lax.broadcasted_iota(jnp.int32, gram.shape, 1)
    gs[0] = gram
    gs[1] = jnp.where(lane < TOTAL, 0.0, pltpu.roll(gram, TOTAL, 1))
    gs[2] = jnp.where(lane < TOTAL, 0.0, pltpu.roll(gram, TOTAL - CUT, 1))
    rest = jnp.zeros((2, LAT), F32)
    for s in range(NEAR):
        row = s * BAND
        free = [gs[1 + h, row + 4 : row + 5, :] for h in range(2)]
        g_ref[s] = gs[0, row : row + 4, :] + jnp.concatenate(free + [rest], axis=0)


def spread_kernel(x_ref, o_ref):
    o_ref[...] = jnp.broadcast_to(jnp.sum(x_ref[...], axis=0)[None], o_ref.shape)


def mix_kernel(scale, g_ref, v_ref, o_ref, gs, ws, vs, ms):
    for s in range(NEAR):
        gs[4 * s : 4 * s + 4] = g_ref[s]
    gram = gs[...]
    head, tail = pltpu.roll(gram, LAT - TOTAL, 1), pltpu.roll(gram, LAT - TOTAL + CUT, 1)
    lane = lax.broadcasted_iota(jnp.int32, (1, LAT), 1)
    for s in range(NEAR):
        ws[s * BAND : s * BAND + 4] = gram[4 * s : 4 * s + 4]
        row = jnp.where(lane < CUT, head[4 * s : 4 * s + 1], tail[4 * s + 1 : 4 * s + 2])
        ws[s * BAND + 4 : s * BAND + 5] = row
    lane = lax.broadcasted_iota(jnp.int32, (TOTAL, LAT), 1)
    s = jnp.where(lane < TOTAL, ws[...] * scale, -jnp.inf)
    e = jnp.exp(s - jnp.max(s, axis=1, keepdims=True))
    w = (e / jnp.sum(e, axis=1, keepdims=True)).astype(BF16)[:, :TOTAL]
    vs[...] = v_ref[:, :, CQ:, :].astype(F32).reshape(TOTAL * ROWS, LAT)
    v = jnp.concatenate([vs[pl.ds(r, TOTAL, stride=ROWS), :].astype(BF16) for r in range(ROWS)], axis=1)
    mixed = jnp.dot(w, v, preferred_element_type=F32)
    for r in range(ROWS):
        ms[pl.ds(r, TOTAL, stride=ROWS), :] = mixed[:, r * LAT : (r + 1) * LAT]
    o_ref[...] = ms[...].astype(BF16).reshape(o_ref.shape)


def finish_kernel(x_ref, f_ref, w_ref, o_ref, mc, mb, ma, br):
    for m in range(OWN):
        for j in range(MEM):
            mc[j * ROWS : (j + 1) * ROWS] = x_ref[j, m].astype(F32)
        mb[...], ma[...] = lat_shifts(mc[...])
        for i in range(0, COLS, 2):
            patches = []
            for col in (i, i + 1):
                parts = [
                    t[(col + a) * CQ : (col + a + 1) * CQ, :] for a in range(3) for t in (mb, mc, ma)
                ]
                patches.append(jnp.concatenate(parts, axis=0).astype(BF16))
            r = jnp.dot(w_ref[...], jnp.concatenate(patches, axis=1), preferred_element_type=F32)
            for s in range(2):
                br[pl.ds(i + s, CH, stride=COLS), :] = r[:, s * LAT : (s + 1) * LAT]
        o_ref[m] = (f_ref[m].astype(F32) + br[...].reshape(CH, COLS, LAT)).astype(BF16)


def shards(fields, w_query, w_key, w_value, w_out):
    edge = jax.ShapeDtypeStruct((OWN, 2 * CH, LAT), BF16)
    plane = pltpu.VMEM((CH * COLS, LAT), F32)
    sib, nb = call(edges_kernel, (edge, edge), [plane], 0, 1_000_000, fields)
    swaps = [(i, (i - 1 if i % 2 == 0 else i + 1) % LON) for i in range(LON)]
    got_nb = lax.ppermute(nb, ("yhi", "x", "core"), swaps)
    got_sib = lax.all_gather(sib, "core", axis=0, tiled=False)
    packed = jax.ShapeDtypeStruct((MEM, OWN, CQ + ROWS, LAT), BF16)
    pair = jax.ShapeDtypeStruct((18 * CQ, 4 * CH), BF16)
    part, w_pair = call(
        inner_kernel,
        (packed, pair),
        [
            pltpu.VMEM((3 * CQ, 9 * CH), F32),
            plane,
            pltpu.VMEM((CH * COLS, LAT), BF16),
            pltpu.VMEM((2 * CQ, LAT), F32),
        ],
        450_000_000,
        2_000_000,
        fields,
        w_query,
        w_key,
        w_value,
    )
    qkv = call(
        outer_kernel,
        packed,
        [pltpu.VMEM((OWN, 4 * CH, LAT), BF16)] * 2 + [pltpu.VMEM((2 * CQ, LAT), F32)],
        300_000_000,
        1_500_000,
        part,
        w_pair,
        sib,
        nb,
        got_sib,
        got_nb,
        alias={0: 0},
    )
    qkv = lax.all_to_all(qkv, ("z", "ylo"), 0, 0, tiled=True)

    near, far = ("x", "ylo", "core"), ("z", "yhi")
    tiles = jax.ShapeDtypeStruct((NEAR, 4, LAT), F32)
    copies = jax.ShapeDtypeStruct((MEM * LON // NEAR, 4, LAT), F32)
    gram = call(
        gram_kernel,
        tiles,
        [pltpu.VMEM((TOTAL * CQ, LAT), F32), pltpu.VMEM((3, TOTAL, LAT), F32)],
        20_000_000,
        600_000,
        qkv,
    )
    gram = lax.all_to_all(gram, near, 0, 0, tiled=True)
    gram = call(spread_kernel, copies, [], 20_000, 300_000, gram)
    gram = lax.all_to_all(gram, far, 0, 0, tiled=True)
    gram = call(spread_kernel, tiles, [], 80_000, 300_000, gram)
    gram = lax.all_to_all(gram, near, 0, 0, tiled=True)
    scale = 1.0 / math.sqrt(CQ * LAT * COLS * LON)
    mixed = call(
        functools.partial(mix_kernel, scale),
        jax.ShapeDtypeStruct((MEM, OWN, ROWS, LAT), BF16),
        [
            pltpu.VMEM((4 * NEAR, LAT), F32),
            pltpu.VMEM((TOTAL, LAT), F32),
            pltpu.VMEM((TOTAL * ROWS, LAT), F32),
            pltpu.VMEM((TOTAL * ROWS, LAT), F32),
        ],
        30_000_000,
        700_000,
        gram,
        qkv,
    )
    mixed = lax.all_to_all(mixed, ("z", "ylo"), 0, 0, tiled=True)
    return call(
        finish_kernel,
        jax.ShapeDtypeStruct(fields.shape, BF16),
        [pltpu.VMEM((MEM * ROWS, LAT), F32)] * 3 + [pltpu.VMEM((CH * COLS, LAT), F32)],
        150_000_000,
        1_700_000,
        mixed,
        fields,
        w_out,
    )


def solution(mesh):
    fine = Mesh(mesh.devices.reshape(MEM // 2, 2, LON // 8, 4, 2), ("z", "ylo", "yhi", "x", "core"))
    spec = P(("z", "ylo"), None, ("yhi", "x", "core"), None)
    return jax.shard_map(
        shards,
        mesh=fine,
        in_specs=(spec, P(), P(), P(), P()),
        out_specs=spec,
        check_vma=False,
    )
```

```python
import functools
import math

import jax
import jax.numpy as jnp
from jax import lax
from jax.experimental import pallas as pl
from jax.experimental.pallas import tpu as pltpu
from jax.sharding import Mesh
from jax.sharding import PartitionSpec as P

CH, CQ, LAT = 64, 24, 128
HALF = CQ // 2
MEM, LON = 16, 32
OWN = 5
TOTAL = MEM * OWN
NEAR = 16
BAND = TOTAL // NEAR
CUT = LAT - TOTAL
COLS = 8
EXT = COLS + 2
ROWS = 16
F32, BF16 = jnp.float32, jnp.bfloat16
VMEM = pl.BlockSpec(memory_space=pltpu.VMEM)


HBM = pl.BlockSpec(memory_space=pl.ANY)


def call(body, outs, scratch, flops, nbytes, *args, alias=None, far_out=False):
    many = isinstance(outs, tuple)
    one = HBM if far_out else VMEM
    return pl.pallas_call(
        body,
        out_shape=outs,
        in_specs=[VMEM] * len(args),
        out_specs=(one,) * len(outs) if many else one,
        scratch_shapes=scratch,
        input_output_aliases=alias or {},
        compiler_params=pltpu.CompilerParams(vmem_limit_bytes=32 * 1024 * 1024),
        cost_estimate=pl.CostEstimate(flops=flops, bytes_accessed=nbytes, transcendentals=0),
    )(*args)


def lat_shifts(x):
    lane = lax.broadcasted_iota(jnp.int32, x.shape, 1)
    before = jnp.where(lane == 0, 0.0, pltpu.roll(x, 1, 1))
    after = jnp.where(lane == LAT - 1, 0.0, pltpu.roll(x, LAT - 1, 1))
    return before, after


def edges_kernel(f_ref, sib_ref, nb_ref, xf):
    even = lax.axis_index("core") == 0
    for m in range(OWN):
        xf[...] = f_ref[m].astype(F32).reshape(CH * COLS, LAT)
        for s in range(2):
            left = xf[pl.ds(s, CH, stride=COLS), :]
            right = xf[pl.ds(COLS - 2 + s, CH, stride=COLS), :]
            sib_ref[m, s * CH : (s + 1) * CH] = jnp.where(even, right, left).astype(BF16)
            nb_ref[m, s * CH : (s + 1) * CH] = jnp.where(even, left, right).astype(BF16)


def conv_pairs(w, xs):
    width = 3 * CQ
    lane = lax.broadcasted_iota(jnp.int32, (width, LAT), 1)
    wide = jnp.dot(w, jnp.concatenate(xs, axis=1), preferred_element_type=F32)
    pairs = []
    for n in range(len(xs)):
        r = wide[:, n * LAT : (n + 1) * LAT]
        outs = []
        for s in range(2):
            y = [r[(3 * s + b) * width : (3 * s + b + 1) * width] for b in range(3)]
            outs.append(
                y[1]
                + jnp.where(lane == 0, 0.0, pltpu.roll(y[0], 1, 1))
                + jnp.where(lane == LAT - 1, 0.0, pltpu.roll(y[2], LAT - 1, 1))
            )
        pairs.append(outs)
    return pairs


def put_pair(o_ref, vs, m, p, outs):
    for s in range(2):
        col = 2 * p + s
        vs[s * CQ : (s + 1) * CQ] = outs[s][2 * CQ :]
        if 1 <= col <= COLS:
            for h in range(2):
                o_ref[2 * (col - 1) + h, m, 0:CQ] = outs[s][h * CQ : (h + 1) * CQ].astype(BF16)
    for j in range(3):
        o_ref[3 * p + j, m, CQ:] = vs[j * ROWS : (j + 1) * ROWS].astype(BF16)


def inner_kernel(f_ref, wq_ref, wk_ref, wv_ref, o_ref, wp_ref, ws, xf, xt, vs):
    ws[0:HALF] = wq_ref[...].astype(F32)[:HALF]
    ws[HALF : 2 * HALF] = wk_ref[...].astype(F32)[:HALF]
    ws[2 * HALF : 3 * HALF] = wq_ref[...].astype(F32)[HALF:]
    ws[3 * HALF : 4 * HALF] = wk_ref[...].astype(F32)[HALF:]
    ws[2 * CQ :] = wv_ref[...].astype(F32)
    zero = jnp.zeros((3 * CQ, CH), F32)
    for b in range(3):
        taps = [ws[:, (3 * a + b) * CH : (3 * a + b + 1) * CH] for a in range(3)]
        for s in range(2):
            row = (3 * s + b) * 3 * CQ
            full = [zero] + taps if s else taps + [zero]
            wp_ref[row : row + 3 * CQ] = jnp.concatenate(full, axis=1).astype(BF16)
    for m in range(OWN):
        xf[...] = f_ref[m].astype(F32).reshape(CH * COLS, LAT)
        for i in range(COLS):
            xt[m, i * CH : (i + 1) * CH] = xf[pl.ds(i, CH, stride=COLS), :].astype(BF16)
    units = [(m, p) for m in range(OWN) for p in range(1, EXT // 2 - 1)]
    for n in range(0, len(units), 2):
        two = units[n : n + 2]
        xs = [xt[m, 2 * (p - 1) * CH : 2 * (p + 1) * CH] for m, p in two]
        for (m, p), outs in zip(two, conv_pairs(wp_ref[...], xs)):
            put_pair(o_ref, vs, m, p, outs)


def outer_kernel(i_ref, wp_ref, sib_ref, nb_ref, gs_ref, gn_ref, o_ref, xl, xr, vs):
    core = lax.axis_index("core")
    near = 2 * CH

    @pl.when(core == 0)
    def _():
        xl[:, :near] = gn_ref[...]
        xl[:, near:] = nb_ref[...]
        xr[:, :near] = sib_ref[...]
        xr[:, near:] = gs_ref[1]

    @pl.when(core == 1)
    def _():
        xl[:, :near] = gs_ref[0]
        xl[:, near:] = sib_ref[...]
        xr[:, :near] = nb_ref[...]
        xr[:, near:] = gn_ref[...]

    for m in range(OWN):
        left, right = conv_pairs(wp_ref[...], [xl[m], xr[m]])
        put_pair(o_ref, vs, m, 0, left)
        put_pair(o_ref, vs, m, EXT // 2 - 1, right)
        o_ref[MEM - 1, m, CQ:] = jnp.zeros((ROWS, LAT), BF16)


def gram_kernel(x_ref, g_ref, xs, gs):
    xs[...] = x_ref[:, :, 0:CQ, :].astype(F32).reshape(TOTAL * CQ, LAT)
    pad = jnp.zeros((LAT - TOTAL, LAT), BF16)
    q, k = [], []
    for r in range(HALF):
        q.append(xs[pl.ds(r, TOTAL, stride=CQ), :].astype(BF16))
        k.append(jnp.concatenate([xs[pl.ds(HALF + r, TOTAL, stride=CQ), :].astype(BF16), pad], axis=0))
    gram = lax.dot_general(
        jnp.concatenate(q, axis=1),
        jnp.concatenate(k, axis=1),
        (((1,), (1,)), ((), ())),
        preferred_element_type=F32,
    )
    lane = lax.broadcasted_iota(jnp.int32, gram.shape, 1)
    gs[0] = gram
    gs[1] = jnp.where(lane < TOTAL, 0.0, pltpu.roll(gram, TOTAL, 1))
    gs[2] = jnp.where(lane < TOTAL, 0.0, pltpu.roll(gram, TOTAL - CUT, 1))
    rest = jnp.zeros((2, LAT), F32)
    for s in range(NEAR):
        row = s * BAND
        free = [gs[1 + h, row + 4 : row + 5, :] for h in range(2)]
        g_ref[s] = gs[0, row : row + 4, :] + jnp.concatenate(free + [rest], axis=0)


def spread_kernel(x_ref, o_ref):
    o_ref[...] = jnp.broadcast_to(jnp.sum(x_ref[...], axis=0)[None], o_ref.shape)


def mix_kernel(scale, g_ref, v_ref, o_ref, gs, ws, vs, ms):
    for s in range(NEAR):
        gs[4 * s : 4 * s + 4] = g_ref[s]
    gram = gs[...]
    head, tail = pltpu.roll(gram, LAT - TOTAL, 1), pltpu.roll(gram, LAT - TOTAL + CUT, 1)
    lane = lax.broadcasted_iota(jnp.int32, (1, LAT), 1)
    for s in range(NEAR):
        ws[s * BAND : s * BAND + 4] = gram[4 * s : 4 * s + 4]
        row = jnp.where(lane < CUT, head[4 * s : 4 * s + 1], tail[4 * s + 1 : 4 * s + 2])
        ws[s * BAND + 4 : s * BAND + 5] = row
    lane = lax.broadcasted_iota(jnp.int32, (TOTAL, LAT), 1)
    s = jnp.where(lane < TOTAL, ws[...] * scale, -jnp.inf)
    e = jnp.exp(s - jnp.max(s, axis=1, keepdims=True))
    w = (e / jnp.sum(e, axis=1, keepdims=True)).astype(BF16)[:, :TOTAL]
    vs[...] = v_ref[:, :, CQ:, :].astype(F32).reshape(TOTAL * ROWS, LAT)
    v = jnp.concatenate([vs[pl.ds(r, TOTAL, stride=ROWS), :].astype(BF16) for r in range(ROWS)], axis=1)
    mixed = jnp.dot(w, v, preferred_element_type=F32)
    for r in range(ROWS):
        ms[pl.ds(r, TOTAL, stride=ROWS), :] = mixed[:, r * LAT : (r + 1) * LAT]
    o_ref[...] = ms[...].astype(BF16).reshape(o_ref.shape)


def finish_kernel(x_ref, f_ref, w_ref, o_ref, mc, mb, ma, br, ob, sem):
    copies = [pltpu.make_async_copy(ob.at[m], o_ref.at[m], sem.at[m]) for m in range(OWN)]
    for m in range(OWN):
        for j in range(MEM):
            mc[j * ROWS : (j + 1) * ROWS] = x_ref[j, m].astype(F32)
        mb[...], ma[...] = lat_shifts(mc[...])
        for i in range(0, COLS, 2):
            patches = []
            for col in (i, i + 1):
                parts = [
                    t[(col + a) * CQ : (col + a + 1) * CQ, :] for a in range(3) for t in (mb, mc, ma)
                ]
                patches.append(jnp.concatenate(parts, axis=0).astype(BF16))
            r = jnp.dot(w_ref[...], jnp.concatenate(patches, axis=1), preferred_element_type=F32)
            for s in range(2):
                br[pl.ds(i + s, CH, stride=COLS), :] = r[:, s * LAT : (s + 1) * LAT]
        ob[m] = (f_ref[m].astype(F32) + br[...].reshape(CH, COLS, LAT)).astype(BF16)
        copies[m].start()
    for copy in copies:
        copy.wait()


def shards(fields, w_query, w_key, w_value, w_out):
    edge = jax.ShapeDtypeStruct((OWN, 2 * CH, LAT), BF16)
    plane = pltpu.VMEM((CH * COLS, LAT), F32)
    sib, nb = call(edges_kernel, (edge, edge), [plane], 0, 1_000_000, fields)
    swaps = [(i, (i - 1 if i % 2 == 0 else i + 1) % LON) for i in range(LON)]
    got_nb = lax.ppermute(nb, ("yhi", "x", "core"), swaps)
    got_sib = lax.all_gather(sib, "core", axis=0, tiled=False)
    packed = jax.ShapeDtypeStruct((MEM, OWN, CQ + ROWS, LAT), BF16)
    pair = jax.ShapeDtypeStruct((18 * CQ, 4 * CH), BF16)
    part, w_pair = call(
        inner_kernel,
        (packed, pair),
        [
            pltpu.VMEM((3 * CQ, 9 * CH), F32),
            plane,
            pltpu.VMEM((OWN, CH * COLS, LAT), BF16),
            pltpu.VMEM((2 * CQ, LAT), F32),
        ],
        450_000_000,
        2_000_000,
        fields,
        w_query,
        w_key,
        w_value,
    )
    qkv = call(
        outer_kernel,
        packed,
        [pltpu.VMEM((OWN, 4 * CH, LAT), BF16)] * 2 + [pltpu.VMEM((2 * CQ, LAT), F32)],
        300_000_000,
        1_500_000,
        part,
        w_pair,
        sib,
        nb,
        got_sib,
        got_nb,
        alias={0: 0},
    )
    qkv = lax.all_to_all(qkv, ("z", "ylo"), 0, 0, tiled=True)

    near, far = ("x", "ylo", "core"), ("z", "yhi")
    tiles = jax.ShapeDtypeStruct((NEAR, 4, LAT), F32)
    copies = jax.ShapeDtypeStruct((MEM * LON // NEAR, 4, LAT), F32)
    gram = call(
        gram_kernel,
        tiles,
        [pltpu.VMEM((TOTAL * CQ, LAT), F32), pltpu.VMEM((3, TOTAL, LAT), F32)],
        20_000_000,
        600_000,
        qkv,
    )
    gram = lax.all_to_all(gram, near, 0, 0, tiled=True)
    gram = call(spread_kernel, copies, [], 20_000, 300_000, gram)
    gram = lax.all_to_all(gram, far, 0, 0, tiled=True)
    gram = call(spread_kernel, tiles, [], 80_000, 300_000, gram)
    gram = lax.all_to_all(gram, near, 0, 0, tiled=True)
    scale = 1.0 / math.sqrt(CQ * LAT * COLS * LON)
    mixed = call(
        functools.partial(mix_kernel, scale),
        jax.ShapeDtypeStruct((MEM, OWN, ROWS, LAT), BF16),
        [
            pltpu.VMEM((4 * NEAR, LAT), F32),
            pltpu.VMEM((TOTAL, LAT), F32),
            pltpu.VMEM((TOTAL * ROWS, LAT), F32),
            pltpu.VMEM((TOTAL * ROWS, LAT), F32),
        ],
        30_000_000,
        700_000,
        gram,
        qkv,
    )
    mixed = lax.all_to_all(mixed, ("z", "ylo"), 0, 0, tiled=True)
    return call(
        finish_kernel,
        jax.ShapeDtypeStruct(fields.shape, BF16),
        [pltpu.VMEM((MEM * ROWS, LAT), F32)] * 3
        + [plane, pltpu.VMEM(fields.shape, BF16), pltpu.SemaphoreType.DMA((OWN,))],
        150_000_000,
        1_700_000,
        mixed,
        fields,
        w_out,
        far_out=True,
    )


def solution(mesh):
    fine = Mesh(mesh.devices.reshape(MEM // 2, 2, LON // 8, 4, 2), ("z", "ylo", "yhi", "x", "core"))
    spec = P(("z", "ylo"), None, ("yhi", "x", "core"), None)
    return jax.shard_map(
        shards,
        mesh=fine,
        in_specs=(spec, P(), P(), P(), P()),
        out_specs=spec,
        check_vma=False,
    )
```

```python
import functools
import math

import jax
import jax.numpy as jnp
from jax import lax
from jax.experimental import pallas as pl
from jax.experimental.pallas import tpu as pltpu
from jax.sharding import Mesh
from jax.sharding import PartitionSpec as P

CH, CQ, LAT = 64, 24, 128
HALF = CQ // 2
MEM, LON = 16, 32
OWN = 5
TOTAL = MEM * OWN
HEAD = 16
CUT = LAT - TOTAL
COLS = 8
EXT = COLS + 2
ROWS = 16
F32, BF16 = jnp.float32, jnp.bfloat16
VMEM = pl.BlockSpec(memory_space=pltpu.VMEM)


HBM = pl.BlockSpec(memory_space=pl.ANY)


def call(body, outs, scratch, flops, nbytes, *args, alias=None, far_out=False):
    many = isinstance(outs, tuple)
    one = HBM if far_out else VMEM
    return pl.pallas_call(
        body,
        out_shape=outs,
        in_specs=[VMEM] * len(args),
        out_specs=(one,) * len(outs) if many else one,
        scratch_shapes=scratch,
        input_output_aliases=alias or {},
        compiler_params=pltpu.CompilerParams(vmem_limit_bytes=32 * 1024 * 1024),
        cost_estimate=pl.CostEstimate(flops=flops, bytes_accessed=nbytes, transcendentals=0),
    )(*args)


def lat_shifts(x):
    lane = lax.broadcasted_iota(jnp.int32, x.shape, 1)
    before = jnp.where(lane == 0, 0.0, pltpu.roll(x, 1, 1))
    after = jnp.where(lane == LAT - 1, 0.0, pltpu.roll(x, LAT - 1, 1))
    return before, after


def edges_kernel(f_ref, sib_ref, nb_ref, xf):
    even = lax.axis_index("core") == 0
    for m in range(OWN):
        xf[...] = f_ref[m].astype(F32).reshape(CH * COLS, LAT)
        for s in range(2):
            left = xf[pl.ds(s, CH, stride=COLS), :]
            right = xf[pl.ds(COLS - 2 + s, CH, stride=COLS), :]
            sib_ref[m, s * CH : (s + 1) * CH] = jnp.where(even, right, left).astype(BF16)
            nb_ref[m, s * CH : (s + 1) * CH] = jnp.where(even, left, right).astype(BF16)


def conv_pairs(w, xs):
    width = 3 * CQ
    lane = lax.broadcasted_iota(jnp.int32, (width, LAT), 1)
    wide = jnp.dot(w, jnp.concatenate(xs, axis=1), preferred_element_type=F32)
    pairs = []
    for n in range(len(xs)):
        r = wide[:, n * LAT : (n + 1) * LAT]
        outs = []
        for s in range(2):
            y = [r[(3 * s + b) * width : (3 * s + b + 1) * width] for b in range(3)]
            outs.append(
                y[1]
                + jnp.where(lane == 0, 0.0, pltpu.roll(y[0], 1, 1))
                + jnp.where(lane == LAT - 1, 0.0, pltpu.roll(y[2], LAT - 1, 1))
            )
        pairs.append(outs)
    return pairs


def put_pair(qk_ref, v_ref, vs, m, p, outs):
    for s in range(2):
        col = 2 * p + s
        vs[s * CQ : (s + 1) * CQ] = outs[s][2 * CQ :]
        if 1 <= col <= COLS:
            for h in range(2):
                qk_ref[2 * (col - 1) + h, m] = outs[s][h * CQ : (h + 1) * CQ].astype(BF16)
    for n in range(6):
        v_ref[3 * p + n // 2, n % 2, m] = vs[n * 8 : (n + 1) * 8].astype(BF16)


def inner_kernel(f_ref, wq_ref, wk_ref, wv_ref, qk_ref, v_ref, wp_ref, ws, xf, xt, vs):
    ws[0:HALF] = wq_ref[...].astype(F32)[:HALF]
    ws[HALF : 2 * HALF] = wk_ref[...].astype(F32)[:HALF]
    ws[2 * HALF : 3 * HALF] = wq_ref[...].astype(F32)[HALF:]
    ws[3 * HALF : 4 * HALF] = wk_ref[...].astype(F32)[HALF:]
    ws[2 * CQ :] = wv_ref[...].astype(F32)
    zero = jnp.zeros((3 * CQ, CH), F32)
    for b in range(3):
        taps = [ws[:, (3 * a + b) * CH : (3 * a + b + 1) * CH] for a in range(3)]
        for s in range(2):
            row = (3 * s + b) * 3 * CQ
            full = [zero] + taps if s else taps + [zero]
            wp_ref[row : row + 3 * CQ] = jnp.concatenate(full, axis=1).astype(BF16)
    for m in range(OWN):
        xf[...] = f_ref[m].astype(F32).reshape(CH * COLS, LAT)
        for i in range(COLS):
            xt[m, i * CH : (i + 1) * CH] = xf[pl.ds(i, CH, stride=COLS), :].astype(BF16)
    units = [(m, p) for m in range(OWN) for p in range(1, EXT // 2 - 1)]
    for n in range(0, len(units), 2):
        two = units[n : n + 2]
        xs = [xt[m, 2 * (p - 1) * CH : 2 * (p + 1) * CH] for m, p in two]
        for (m, p), outs in zip(two, conv_pairs(wp_ref[...], xs)):
            put_pair(qk_ref, v_ref, vs, m, p, outs)


def outer_kernel(
    iq_ref, iv_ref, wp_ref, sib_ref, nb_ref, gs_ref, gn_ref, qk_ref, v_ref, xl, xr, vs
):
    core = lax.axis_index("core")
    near = 2 * CH

    @pl.when(core == 0)
    def _():
        xl[:, :near] = gn_ref[...]
        xl[:, near:] = nb_ref[...]
        xr[:, :near] = sib_ref[...]
        xr[:, near:] = gs_ref[1]

    @pl.when(core == 1)
    def _():
        xl[:, :near] = gs_ref[0]
        xl[:, near:] = sib_ref[...]
        xr[:, :near] = nb_ref[...]
        xr[:, near:] = gn_ref[...]

    for m in range(OWN):
        left, right = conv_pairs(wp_ref[...], [xl[m], xr[m]])
        put_pair(qk_ref, v_ref, vs, m, 0, left)
        put_pair(qk_ref, v_ref, vs, m, EXT // 2 - 1, right)
        for h in range(2):
            v_ref[MEM - 1, h, m] = jnp.zeros((8, LAT), BF16)


def gram_kernel(x_ref, v_ref, o_ref, xs, gs, ps):
    xs[...] = x_ref[...].astype(F32).reshape(TOTAL * CQ, LAT)
    pad = jnp.zeros((LAT - TOTAL, LAT), BF16)
    q, k = [], []
    for r in range(HALF):
        q.append(xs[pl.ds(r, TOTAL, stride=CQ), :].astype(BF16))
        k.append(jnp.concatenate([xs[pl.ds(HALF + r, TOTAL, stride=CQ), :].astype(BF16), pad], axis=0))
    gram = lax.dot_general(
        jnp.concatenate(q, axis=1),
        jnp.concatenate(k, axis=1),
        (((1,), (1,)), ((), ())),
        preferred_element_type=F32,
    )
    lane = lax.broadcasted_iota(jnp.int32, gram.shape, 1)
    gs[0] = gram
    gs[1] = jnp.where(lane < TOTAL, 0.0, pltpu.roll(gram, TOTAL, 1))
    gs[2] = jnp.where(lane < TOTAL, 0.0, pltpu.roll(gram, TOTAL - CUT, 1))
    rest = jnp.zeros((2, LAT), F32)
    for s in range(MEM):
        row = s * OWN
        free = [gs[1 + h, row + 4 : row + 5, :] for h in range(2)]
        ps[0, 4 * s : 4 * s + 4] = gs[0, row : row + 4, :] + jnp.concatenate(free + [rest], axis=0)
    for part in range(2):
        whole = ps[part]
        high = whole.astype(BF16).astype(F32)
        ps[part] = high
        ps[part + 1] = whole - high
    for s in range(MEM):
        for part in range(3):
            ps[3, 4 * part : 4 * part + 4] = ps[part, 4 * s : 4 * s + 4]
        ps[3, 12:HEAD] = jnp.zeros((HEAD - 12, LAT), F32)
        o_ref[s, 0:HEAD] = ps[3, 0:HEAD].astype(BF16)
    o_ref[:, HEAD:] = v_ref[:, 0].astype(F32).reshape(MEM, OWN * 8, LAT).astype(BF16)


def total_kernel(x_ref, o_ref):
    parts = jnp.sum(x_ref[:, 0:HEAD].astype(F32), axis=0)
    o_ref[...] = parts[0:4] + parts[4:8] + parts[8:12]


def spread_kernel(x_ref, o_ref):
    o_ref[...] = jnp.broadcast_to((x_ref[0] + x_ref[1])[None], o_ref.shape)


def softmax_kernel(scale, x_ref, v_ref, o_ref, gs):
    gs[...] = jnp.zeros(gs.shape, F32)
    gs[0:4] = jnp.sum(x_ref[...], axis=0)
    gram = gs[...]
    head, tail = pltpu.roll(gram, LAT - TOTAL, 1), pltpu.roll(gram, LAT - TOTAL + CUT, 1)
    lane = lax.broadcasted_iota(jnp.int32, gram.shape, 1)
    gs[4:5] = jnp.where(lane[0:1] < CUT, head[0:1], tail[1:2])
    s = jnp.where(lane < TOTAL, gs[...] * scale, -jnp.inf)
    e = jnp.exp(s - jnp.max(s, axis=1, keepdims=True))
    w = (e / jnp.sum(e, axis=1, keepdims=True)).astype(BF16)
    o_ref[:, 0:HEAD] = jnp.broadcast_to(w[None], (MEM, HEAD, LAT))
    o_ref[:, HEAD:] = v_ref[:, 1].astype(F32).reshape(MEM, OWN * 8, LAT).astype(BF16)


def mix_kernel(a_ref, b_ref, o_ref, ws, vs, ms):
    for s in range(MEM):
        ws[s * OWN : (s + 1) * OWN, :] = b_ref[s, 0:HEAD].astype(F32)[0:OWN]
    w = ws[...].astype(BF16)[:, :TOTAL]
    v = []
    for h, ref in enumerate((a_ref, b_ref)):
        vs[h] = ref[:, HEAD:].astype(F32).reshape(TOTAL * 8, LAT)
        v += [vs[h, pl.ds(r, TOTAL, stride=8), :].astype(BF16) for r in range(8)]
    mixed = jnp.dot(w, jnp.concatenate(v, axis=1), preferred_element_type=F32)
    for r in range(ROWS):
        ms[pl.ds(r, TOTAL, stride=ROWS), :] = mixed[:, r * LAT : (r + 1) * LAT]
    o_ref[...] = ms[...].astype(BF16).reshape(o_ref.shape)


def finish_kernel(x_ref, f_ref, w_ref, o_ref, mc, mb, ma, br, ob, sem):
    copies = [pltpu.make_async_copy(ob.at[m], o_ref.at[m], sem.at[m]) for m in range(OWN)]
    for m in range(OWN):
        for j in range(MEM):
            mc[j * ROWS : (j + 1) * ROWS] = x_ref[j, m].astype(F32)
        mb[...], ma[...] = lat_shifts(mc[...])
        for i in range(0, COLS, 2):
            patches = []
            for col in (i, i + 1):
                parts = [
                    t[(col + a) * CQ : (col + a + 1) * CQ, :] for a in range(3) for t in (mb, mc, ma)
                ]
                patches.append(jnp.concatenate(parts, axis=0).astype(BF16))
            r = jnp.dot(w_ref[...], jnp.concatenate(patches, axis=1), preferred_element_type=F32)
            for s in range(2):
                br[pl.ds(i + s, CH, stride=COLS), :] = r[:, s * LAT : (s + 1) * LAT]
        ob[m] = (f_ref[m].astype(F32) + br[...].reshape(CH, COLS, LAT)).astype(BF16)
        copies[m].start()
    for copy in copies:
        copy.wait()


def shards(fields, w_query, w_key, w_value, w_out):
    edge = jax.ShapeDtypeStruct((OWN, 2 * CH, LAT), BF16)
    plane = pltpu.VMEM((CH * COLS, LAT), F32)
    sib, nb = call(edges_kernel, (edge, edge), [plane], 0, 1_000_000, fields)
    swaps = [(i, (i - 1 if i % 2 == 0 else i + 1) % LON) for i in range(LON)]
    got_nb = lax.ppermute(nb, ("yhi", "x", "core"), swaps)
    got_sib = lax.all_gather(sib, "core", axis=0, tiled=False)
    qk_shape = jax.ShapeDtypeStruct((MEM, OWN, CQ, LAT), BF16)
    v_shape = jax.ShapeDtypeStruct((MEM, 2, OWN, 8, LAT), BF16)
    pair = jax.ShapeDtypeStruct((18 * CQ, 4 * CH), BF16)
    qk, v, w_pair = call(
        inner_kernel,
        (qk_shape, v_shape, pair),
        [
            pltpu.VMEM((3 * CQ, 9 * CH), F32),
            plane,
            pltpu.VMEM((OWN, CH * COLS, LAT), BF16),
            pltpu.VMEM((2 * CQ, LAT), F32),
        ],
        450_000_000,
        2_000_000,
        fields,
        w_query,
        w_key,
        w_value,
    )
    qk, v = call(
        outer_kernel,
        (qk_shape, v_shape),
        [pltpu.VMEM((OWN, 4 * CH, LAT), BF16)] * 2 + [pltpu.VMEM((2 * CQ, LAT), F32)],
        300_000_000,
        1_500_000,
        qk,
        v,
        w_pair,
        sib,
        nb,
        got_sib,
        got_nb,
        alias={0: 0, 1: 1},
    )
    mem, lon = ("z", "ylo"), ("yhi", "x")
    qk = lax.all_to_all(qk, mem, 0, 0, tiled=True)

    packed = jax.ShapeDtypeStruct((MEM, HEAD + OWN * 8, LAT), BF16)
    first = call(
        gram_kernel,
        packed,
        [
            pltpu.VMEM((TOTAL * CQ, LAT), F32),
            pltpu.VMEM((3, TOTAL, LAT), F32),
            pltpu.VMEM((4, 4 * MEM, LAT), F32),
        ],
        20_000_000,
        800_000,
        qk,
        v,
    )
    first = lax.all_to_all(first, mem, 0, 0, tiled=True)
    gram = call(total_kernel, jax.ShapeDtypeStruct((4, LAT), F32), [], 40_000, 200_000, first)
    gram = lax.all_gather(gram, "core", axis=0, tiled=False)
    copies = jax.ShapeDtypeStruct((LON // 2, 4, LAT), F32)
    gram = call(spread_kernel, copies, [], 10_000, 40_000, gram)
    gram = lax.all_to_all(gram, lon, 0, 0, tiled=True)
    scale = 1.0 / math.sqrt(CQ * LAT * COLS * LON)
    second = call(
        functools.partial(softmax_kernel, scale),
        packed,
        [pltpu.VMEM((HEAD, LAT), F32)],
        40_000,
        400_000,
        gram,
        v,
    )
    second = lax.all_to_all(second, mem, 0, 0, tiled=True)
    mixed = call(
        mix_kernel,
        jax.ShapeDtypeStruct((MEM, OWN, ROWS, LAT), BF16),
        [
            pltpu.VMEM((TOTAL, LAT), F32),
            pltpu.VMEM((2, TOTAL * 8, LAT), F32),
            pltpu.VMEM((TOTAL * ROWS, LAT), F32),
        ],
        30_000_000,
        700_000,
        first,
        second,
    )
    mixed = lax.all_to_all(mixed, ("z", "ylo"), 0, 0, tiled=True)
    return call(
        finish_kernel,
        jax.ShapeDtypeStruct(fields.shape, BF16),
        [pltpu.VMEM((MEM * ROWS, LAT), F32)] * 3
        + [plane, pltpu.VMEM(fields.shape, BF16), pltpu.SemaphoreType.DMA((OWN,))],
        150_000_000,
        1_700_000,
        mixed,
        fields,
        w_out,
        far_out=True,
    )


def solution(mesh):
    fine = Mesh(mesh.devices.reshape(MEM // 2, 2, LON // 8, 4, 2), ("z", "ylo", "yhi", "x", "core"))
    spec = P(("z", "ylo"), None, ("yhi", "x", "core"), None)
    return jax.shard_map(
        shards,
        mesh=fine,
        in_specs=(spec, P(), P(), P(), P()),
        out_specs=spec,
        check_vma=False,
    )
```

```python
import functools
import math

import jax
import jax.numpy as jnp
from jax import lax
from jax.experimental import pallas as pl
from jax.experimental.pallas import tpu as pltpu
from jax.sharding import Mesh
from jax.sharding import PartitionSpec as P

CH, CQ, LAT = 64, 24, 128
HALF = CQ // 2
MEM, LON = 16, 32
OWN = 5
TOTAL = MEM * OWN
CUT = LAT - TOTAL
COLS = 8
EXT = COLS + 2
ROWS = 16
USED = EXT * CQ // MEM
F32, BF16 = jnp.float32, jnp.bfloat16
VMEM = pl.BlockSpec(memory_space=pltpu.VMEM)


HBM = pl.BlockSpec(memory_space=pl.ANY)


def call(body, outs, scratch, flops, nbytes, *args, alias=None, far_out=False):
    many = isinstance(outs, tuple)
    one = HBM if far_out else VMEM
    return pl.pallas_call(
        body,
        out_shape=outs,
        in_specs=[VMEM] * len(args),
        out_specs=(one,) * len(outs) if many else one,
        scratch_shapes=scratch,
        input_output_aliases=alias or {},
        compiler_params=pltpu.CompilerParams(vmem_limit_bytes=32 * 1024 * 1024),
        cost_estimate=pl.CostEstimate(flops=flops, bytes_accessed=nbytes, transcendentals=0),
    )(*args)


def lat_shifts(x):
    lane = lax.broadcasted_iota(jnp.int32, x.shape, 1)
    before = jnp.where(lane == 0, 0.0, pltpu.roll(x, 1, 1))
    after = jnp.where(lane == LAT - 1, 0.0, pltpu.roll(x, LAT - 1, 1))
    return before, after


def edges_kernel(f_ref, sib_ref, nb_ref, xf):
    even = lax.axis_index("core") == 0
    for m in range(OWN):
        xf[...] = f_ref[m].astype(F32).reshape(CH * COLS, LAT)
        for s in range(2):
            left = xf[pl.ds(s, CH, stride=COLS), :]
            right = xf[pl.ds(COLS - 2 + s, CH, stride=COLS), :]
            sib_ref[m, s * CH : (s + 1) * CH] = jnp.where(even, right, left).astype(BF16)
            nb_ref[m, s * CH : (s + 1) * CH] = jnp.where(even, left, right).astype(BF16)


def conv_pairs(w, xs):
    width = 3 * CQ
    lane = lax.broadcasted_iota(jnp.int32, (width, LAT), 1)
    wide = jnp.dot(w, jnp.concatenate(xs, axis=1), preferred_element_type=F32)
    pairs = []
    for n in range(len(xs)):
        r = wide[:, n * LAT : (n + 1) * LAT]
        outs = []
        for s in range(2):
            y = [r[(3 * s + b) * width : (3 * s + b + 1) * width] for b in range(3)]
            outs.append(
                y[1]
                + jnp.where(lane == 0, 0.0, pltpu.roll(y[0], 1, 1))
                + jnp.where(lane == LAT - 1, 0.0, pltpu.roll(y[2], LAT - 1, 1))
            )
        pairs.append(outs)
    return pairs


def put_pair(qk_ref, vs, m, p, outs):
    for s in range(2):
        col = 2 * p + s
        vs[s * CQ : (s + 1) * CQ] = outs[s][2 * CQ :]
        if 1 <= col <= COLS:
            for h in range(2):
                qk_ref[2 * (col - 1) + h, m] = outs[s][h * CQ : (h + 1) * CQ].astype(BF16)


def inner_kernel(f_ref, wq_ref, wk_ref, wv_ref, qk_ref, v_ref, e_ref, wp_ref, ws, xf, xt, vs):
    ws[0:HALF] = wq_ref[...].astype(F32)[:HALF]
    ws[HALF : 2 * HALF] = wk_ref[...].astype(F32)[:HALF]
    ws[2 * HALF : 3 * HALF] = wq_ref[...].astype(F32)[HALF:]
    ws[3 * HALF : 4 * HALF] = wk_ref[...].astype(F32)[HALF:]
    ws[2 * CQ :] = wv_ref[...].astype(F32)
    zero = jnp.zeros((3 * CQ, CH), F32)
    for b in range(3):
        taps = [ws[:, (3 * a + b) * CH : (3 * a + b + 1) * CH] for a in range(3)]
        for s in range(2):
            row = (3 * s + b) * 3 * CQ
            full = [zero] + taps if s else taps + [zero]
            wp_ref[row : row + 3 * CQ] = jnp.concatenate(full, axis=1).astype(BF16)
    for m in range(OWN):
        xf[...] = f_ref[m].astype(F32).reshape(CH * COLS, LAT)
        for i in range(COLS):
            xt[m, i * CH : (i + 1) * CH] = xf[pl.ds(i, CH, stride=COLS), :].astype(BF16)
    units = [(m, p) for m in range(OWN) for p in range(1, EXT // 2 - 1)]
    for n in range(0, len(units), 2):
        two = units[n : n + 2]
        xs = [xt[m, 2 * (p - 1) * CH : 2 * (p + 1) * CH] for m, p in two]
        for (m, p), outs in zip(two, conv_pairs(wp_ref[...], xs)):
            put_pair(qk_ref, vs.at[m, pl.ds((p - 1) * 2 * CQ, 2 * CQ)], m, p, outs)
    for m in range(OWN):
        for j in range(4, 12):
            row = j * USED - 2 * CQ
            v_ref[j, m] = vs[m, row : row + ROWS].astype(BF16)
        e_ref[m, 0:ROWS] = vs[m, 0:ROWS]
        e_ref[m, ROWS:] = vs[m, 6 * CQ - ROWS :]


def outer_kernel(
    iq_ref, iv_ref, e_ref, wp_ref, sib_ref, nb_ref, gs_ref, gn_ref, qk_ref, v_ref, xl, xr, vl, vr
):
    core = lax.axis_index("core")
    near = 2 * CH

    @pl.when(core == 0)
    def _():
        xl[:, :near] = gn_ref[...]
        xl[:, near:] = nb_ref[...]
        xr[:, :near] = sib_ref[...]
        xr[:, near:] = gs_ref[1]

    @pl.when(core == 1)
    def _():
        xl[:, :near] = gs_ref[0]
        xl[:, near:] = sib_ref[...]
        xr[:, :near] = nb_ref[...]
        xr[:, near:] = gn_ref[...]

    for m in range(OWN):
        left, right = conv_pairs(wp_ref[...], [xl[m], xr[m]])
        put_pair(qk_ref, vl.at[pl.ds(0, 2 * CQ)], m, 0, left)
        put_pair(qk_ref, vr.at[pl.ds(ROWS, 2 * CQ)], m, EXT // 2 - 1, right)
        vl[2 * CQ :] = e_ref[m, 0:ROWS]
        vr[0:ROWS] = e_ref[m, ROWS:]
        vr[ROWS + 2 * CQ :] = jnp.zeros((8, LAT), F32)
        for j in range(4):
            v_ref[j, m] = vl[j * USED : j * USED + ROWS].astype(BF16)
            row = (12 + j) * USED - (8 * CQ - ROWS)
            v_ref[12 + j, m] = vr[row : row + ROWS].astype(BF16)


def gram_kernel(x_ref, g_ref, xs, gs):
    xs[...] = x_ref[...].astype(F32).reshape(TOTAL * CQ, LAT)
    pad = jnp.zeros((LAT - TOTAL, LAT), BF16)
    q, k = [], []
    for r in range(HALF):
        q.append(xs[pl.ds(r, TOTAL, stride=CQ), :].astype(BF16))
        k.append(jnp.concatenate([xs[pl.ds(HALF + r, TOTAL, stride=CQ), :].astype(BF16), pad], axis=0))
    gram = lax.dot_general(
        jnp.concatenate(q, axis=1),
        jnp.concatenate(k, axis=1),
        (((1,), (1,)), ((), ())),
        preferred_element_type=F32,
    )
    lane = lax.broadcasted_iota(jnp.int32, gram.shape, 1)
    gs[0] = gram
    gs[1] = jnp.where(lane < TOTAL, 0.0, pltpu.roll(gram, TOTAL, 1))
    gs[2] = jnp.where(lane < TOTAL, 0.0, pltpu.roll(gram, TOTAL - CUT, 1))
    rest = jnp.zeros((2, LAT), F32)
    for s in range(MEM):
        row = s * OWN
        free = [gs[1 + h, row + 4 : row + 5, :] for h in range(2)]
        g_ref[s] = gs[0, row : row + 4, :] + jnp.concatenate(free + [rest], axis=0)


def spread_kernel(x_ref, o_ref):
    o_ref[...] = jnp.broadcast_to(jnp.sum(x_ref[...], axis=0)[None], o_ref.shape)


def softmax_kernel(scale, x_ref, v_ref, o_ref, gs):
    gs[...] = jnp.zeros(gs.shape, F32)
    gs[0:4] = jnp.sum(x_ref[...], axis=0)
    gram = gs[...]
    head, tail = pltpu.roll(gram, LAT - TOTAL, 1), pltpu.roll(gram, LAT - TOTAL + CUT, 1)
    lane = lax.broadcasted_iota(jnp.int32, gram.shape, 1)
    gs[4:5] = jnp.where(lane[0:1] < CUT, head[0:1], tail[1:2])
    s = jnp.where(lane < TOTAL, gs[...] * scale, -jnp.inf)
    e = jnp.exp(s - jnp.max(s, axis=1, keepdims=True))
    w = e / jnp.sum(e, axis=1, keepdims=True)
    row = lax.broadcasted_iota(jnp.int32, (MEM, ROWS, LAT), 1)
    for m in range(OWN):
        block = v_ref[:, m].astype(F32)
        o_ref[:, m] = jnp.where(row == USED, w[m : m + 1][None], block).astype(BF16)


def mix_kernel(x_ref, o_ref, vs, ms):
    vs[...] = x_ref[...].astype(F32).reshape(TOTAL * ROWS, LAT)
    w = vs[pl.ds(USED, TOTAL, stride=ROWS), :].astype(BF16)[:, :TOTAL]
    v = jnp.concatenate([vs[pl.ds(r, TOTAL, stride=ROWS), :].astype(BF16) for r in range(USED)], axis=1)
    mixed = jnp.dot(w, v, preferred_element_type=F32)
    for r in range(USED):
        ms[pl.ds(r, TOTAL, stride=ROWS), :] = mixed[:, r * LAT : (r + 1) * LAT]
    ms[pl.ds(USED, TOTAL, stride=ROWS), :] = jnp.zeros((TOTAL, LAT), F32)
    o_ref[...] = ms[...].astype(BF16).reshape(o_ref.shape)


def finish_kernel(x_ref, f_ref, w_ref, o_ref, mc, mb, ma, br, ob, sem):
    copies = [pltpu.make_async_copy(ob.at[m], o_ref.at[m], sem.at[m]) for m in range(OWN)]
    for m in range(OWN):
        for j in range(MEM):
            mc[j * USED : j * USED + ROWS] = x_ref[j, m].astype(F32)
        mb[...], ma[...] = lat_shifts(mc[...])
        for i in range(0, COLS, 2):
            patches = []
            for col in (i, i + 1):
                parts = [
                    t[(col + a) * CQ : (col + a + 1) * CQ, :] for a in range(3) for t in (mb, mc, ma)
                ]
                patches.append(jnp.concatenate(parts, axis=0).astype(BF16))
            r = jnp.dot(w_ref[...], jnp.concatenate(patches, axis=1), preferred_element_type=F32)
            for s in range(2):
                br[pl.ds(i + s, CH, stride=COLS), :] = r[:, s * LAT : (s + 1) * LAT]
        ob[m] = (f_ref[m].astype(F32) + br[...].reshape(CH, COLS, LAT)).astype(BF16)
        copies[m].start()
    for copy in copies:
        copy.wait()


def shards(fields, w_query, w_key, w_value, w_out):
    edge = jax.ShapeDtypeStruct((OWN, 2 * CH, LAT), BF16)
    plane = pltpu.VMEM((CH * COLS, LAT), F32)
    sib, nb = call(edges_kernel, (edge, edge), [plane], 0, 1_000_000, fields)
    swaps = [(i, (i - 1 if i % 2 == 0 else i + 1) % LON) for i in range(LON)]
    got_nb = lax.ppermute(nb, ("yhi", "x", "core"), swaps)
    got_sib = lax.all_gather(sib, "core", axis=0, tiled=False)
    qk_shape = jax.ShapeDtypeStruct((MEM, OWN, CQ, LAT), BF16)
    v_shape = jax.ShapeDtypeStruct((MEM, OWN, ROWS, LAT), BF16)
    ends = jax.ShapeDtypeStruct((OWN, 2 * ROWS, LAT), F32)
    pair = jax.ShapeDtypeStruct((18 * CQ, 4 * CH), BF16)
    qk, v, ends, w_pair = call(
        inner_kernel,
        (qk_shape, v_shape, ends, pair),
        [
            pltpu.VMEM((3 * CQ, 9 * CH), F32),
            plane,
            pltpu.VMEM((OWN, CH * COLS, LAT), BF16),
            pltpu.VMEM((OWN, 6 * CQ, LAT), F32),
        ],
        450_000_000,
        2_000_000,
        fields,
        w_query,
        w_key,
        w_value,
    )
    qk, v = call(
        outer_kernel,
        (qk_shape, v_shape),
        [pltpu.VMEM((OWN, 4 * CH, LAT), BF16)] * 2
        + [pltpu.VMEM((2 * CQ + ROWS, LAT), F32), pltpu.VMEM((2 * CQ + ROWS + 8, LAT), F32)],
        300_000_000,
        1_500_000,
        qk,
        v,
        ends,
        w_pair,
        sib,
        nb,
        got_sib,
        got_nb,
        alias={0: 0, 1: 1},
    )
    mem, lon = ("z", "ylo"), ("yhi", "x", "core")
    qk = lax.all_to_all(qk, mem, 0, 0, tiled=True)
    gram = call(
        gram_kernel,
        jax.ShapeDtypeStruct((MEM, 4, LAT), F32),
        [pltpu.VMEM((TOTAL * CQ, LAT), F32), pltpu.VMEM((3, TOTAL, LAT), F32)],
        20_000_000,
        600_000,
        qk,
    )
    gram = lax.all_to_all(gram, mem, 0, 0, tiled=True)
    gram = call(spread_kernel, jax.ShapeDtypeStruct((LON, 4, LAT), F32), [], 10_000, 100_000, gram)
    gram = lax.all_to_all(gram, lon, 0, 0, tiled=True)
    scale = 1.0 / math.sqrt(CQ * LAT * COLS * LON)
    v = call(
        functools.partial(softmax_kernel, scale),
        v_shape,
        [pltpu.VMEM((8, LAT), F32)],
        40_000,
        700_000,
        gram,
        v,
        alias={1: 0},
    )
    v = lax.all_to_all(v, mem, 0, 0, tiled=True)
    mixed = call(
        mix_kernel,
        v_shape,
        [pltpu.VMEM((TOTAL * ROWS, LAT), F32)] * 2,
        30_000_000,
        700_000,
        v,
    )
    mixed = lax.all_to_all(mixed, ("z", "ylo"), 0, 0, tiled=True)
    return call(
        finish_kernel,
        jax.ShapeDtypeStruct(fields.shape, BF16),
        [pltpu.VMEM((MEM * ROWS, LAT), F32)] * 3
        + [plane, pltpu.VMEM(fields.shape, BF16), pltpu.SemaphoreType.DMA((OWN,))],
        150_000_000,
        1_700_000,
        mixed,
        fields,
        w_out,
        far_out=True,
    )


def solution(mesh):
    fine = Mesh(mesh.devices.reshape(MEM // 2, 2, LON // 8, 4, 2), ("z", "ylo", "yhi", "x", "core"))
    spec = P(("z", "ylo"), None, ("yhi", "x", "core"), None)
    return jax.shard_map(
        shards,
        mesh=fine,
        in_specs=(spec, P(), P(), P(), P()),
        out_specs=spec,
        check_vma=False,
    )
```

```python
import functools
import math

import jax
import jax.numpy as jnp
from jax import lax
from jax.experimental import pallas as pl
from jax.experimental.pallas import tpu as pltpu
from jax.sharding import Mesh
from jax.sharding import PartitionSpec as P

CH, CQ, LAT = 64, 24, 128
HALF = CQ // 2
MEM, LON = 16, 32
OWN = 5
TOTAL = MEM * OWN
CUT = LAT - TOTAL
COLS = 8
EXT = COLS + 2
ROWS = 16
USED = EXT * CQ // MEM
HEAD = 16
F32, BF16 = jnp.float32, jnp.bfloat16
VMEM = pl.BlockSpec(memory_space=pltpu.VMEM)


HBM = pl.BlockSpec(memory_space=pl.ANY)


def call(body, outs, scratch, flops, nbytes, *args, alias=None, far_out=False):
    many = isinstance(outs, tuple)
    one = HBM if far_out else VMEM
    return pl.pallas_call(
        body,
        out_shape=outs,
        in_specs=[VMEM] * len(args),
        out_specs=(one,) * len(outs) if many else one,
        scratch_shapes=scratch,
        input_output_aliases=alias or {},
        compiler_params=pltpu.CompilerParams(vmem_limit_bytes=32 * 1024 * 1024),
        cost_estimate=pl.CostEstimate(flops=flops, bytes_accessed=nbytes, transcendentals=0),
    )(*args)


def lat_shifts(x):
    lane = lax.broadcasted_iota(jnp.int32, x.shape, 1)
    before = jnp.where(lane == 0, 0.0, pltpu.roll(x, 1, 1))
    after = jnp.where(lane == LAT - 1, 0.0, pltpu.roll(x, LAT - 1, 1))
    return before, after


def edges_kernel(f_ref, sib_ref, nb_ref, xf):
    even = lax.axis_index("core") == 0
    for m in range(OWN):
        xf[...] = f_ref[m].astype(F32).reshape(CH * COLS, LAT)
        for s in range(2):
            left = xf[pl.ds(s, CH, stride=COLS), :]
            right = xf[pl.ds(COLS - 2 + s, CH, stride=COLS), :]
            sib_ref[m, s * CH : (s + 1) * CH] = jnp.where(even, right, left).astype(BF16)
            nb_ref[m, s * CH : (s + 1) * CH] = jnp.where(even, left, right).astype(BF16)


def conv_pairs(w, xs):
    width = 3 * CQ
    lane = lax.broadcasted_iota(jnp.int32, (width, LAT), 1)
    wide = jnp.dot(w, jnp.concatenate(xs, axis=1), preferred_element_type=F32)
    pairs = []
    for n in range(len(xs)):
        r = wide[:, n * LAT : (n + 1) * LAT]
        outs = []
        for s in range(2):
            y = [r[(3 * s + b) * width : (3 * s + b + 1) * width] for b in range(3)]
            outs.append(
                y[1]
                + jnp.where(lane == 0, 0.0, pltpu.roll(y[0], 1, 1))
                + jnp.where(lane == LAT - 1, 0.0, pltpu.roll(y[2], LAT - 1, 1))
            )
        pairs.append(outs)
    return pairs


def put_block(v0_ref, v1_ref, j, m, block):
    v0_ref[j, HEAD + m * 8 : HEAD + m * 8 + 8] = block[:8].astype(BF16)
    v1_ref[j, m] = block[8:].astype(BF16)


def put_pair(qk_ref, vs, m, p, outs):
    for s in range(2):
        col = 2 * p + s
        vs[s * CQ : (s + 1) * CQ] = outs[s][2 * CQ :]
        if 1 <= col <= COLS:
            for h in range(2):
                qk_ref[2 * (col - 1) + h, m] = outs[s][h * CQ : (h + 1) * CQ].astype(BF16)


def inner_kernel(
    f_ref, wq_ref, wk_ref, wv_ref, wo_ref, qk_ref, v0_ref, v1_ref, e_ref, wp_ref, wf_ref, ws, xf, xt, vs
):
    ws[0:HALF] = wq_ref[...].astype(F32)[:HALF]
    ws[HALF : 2 * HALF] = wk_ref[...].astype(F32)[:HALF]
    ws[2 * HALF : 3 * HALF] = wq_ref[...].astype(F32)[HALF:]
    ws[3 * HALF : 4 * HALF] = wk_ref[...].astype(F32)[HALF:]
    ws[2 * CQ :] = wv_ref[...].astype(F32)
    zero = jnp.zeros((3 * CQ, CH), F32)
    for b in range(3):
        taps = [ws[:, (3 * a + b) * CH : (3 * a + b + 1) * CH] for a in range(3)]
        for s in range(2):
            row = (3 * s + b) * 3 * CQ
            full = [zero] + taps if s else taps + [zero]
            wp_ref[row : row + 3 * CQ] = jnp.concatenate(full, axis=1).astype(BF16)
    wo = wo_ref[...].astype(F32)
    zero = jnp.zeros((CH, CQ), F32)
    for s in range(2):
        full = []
        for b in range(3):
            taps = [wo[:, (3 * a + b) * CQ : (3 * a + b + 1) * CQ] for a in range(3)]
            full += [zero] + taps if s else taps + [zero]
        wf_ref[s * CH : (s + 1) * CH] = jnp.concatenate(full, axis=1).astype(BF16)
    for m in range(OWN):
        xf[...] = f_ref[m].astype(F32).reshape(CH * COLS, LAT)
        for i in range(COLS):
            xt[m, i * CH : (i + 1) * CH] = xf[pl.ds(i, CH, stride=COLS), :].astype(BF16)
    units = [(m, p) for m in range(OWN) for p in range(1, EXT // 2 - 1)]
    for n in range(0, len(units), 2):
        two = units[n : n + 2]
        xs = [xt[m, 2 * (p - 1) * CH : 2 * (p + 1) * CH] for m, p in two]
        for (m, p), outs in zip(two, conv_pairs(wp_ref[...], xs)):
            put_pair(qk_ref, vs.at[m, pl.ds((p - 1) * 2 * CQ, 2 * CQ)], m, p, outs)
    for m in range(OWN):
        for j in range(4, 12):
            row = j * USED - 2 * CQ
            put_block(v0_ref, v1_ref, j, m, vs[m, row : row + ROWS])
        e_ref[m, 0:ROWS] = vs[m, 0:ROWS]
        e_ref[m, ROWS:] = vs[m, 6 * CQ - ROWS :]


def outer_kernel(
    iq_ref, i0_ref, i1_ref, e_ref, wp_ref, sib_ref, nb_ref, gs_ref, gn_ref,
    qk_ref, v0_ref, v1_ref, xl, xr, vl, vr
):
    core = lax.axis_index("core")
    near = 2 * CH

    @pl.when(core == 0)
    def _():
        xl[:, :near] = gn_ref[...]
        xl[:, near:] = nb_ref[...]
        xr[:, :near] = sib_ref[...]
        xr[:, near:] = gs_ref[1]

    @pl.when(core == 1)
    def _():
        xl[:, :near] = gs_ref[0]
        xl[:, near:] = sib_ref[...]
        xr[:, :near] = nb_ref[...]
        xr[:, near:] = gn_ref[...]

    for m in range(OWN):
        left, right = conv_pairs(wp_ref[...], [xl[m], xr[m]])
        put_pair(qk_ref, vl.at[pl.ds(0, 2 * CQ)], m, 0, left)
        put_pair(qk_ref, vr.at[pl.ds(ROWS, 2 * CQ)], m, EXT // 2 - 1, right)
        vl[2 * CQ :] = e_ref[m, 0:ROWS]
        vr[0:ROWS] = e_ref[m, ROWS:]
        vr[ROWS + 2 * CQ :] = jnp.zeros((8, LAT), F32)
        for j in range(4):
            put_block(v0_ref, v1_ref, j, m, vl[j * USED : j * USED + ROWS])
            row = (12 + j) * USED - (8 * CQ - ROWS)
            put_block(v0_ref, v1_ref, 12 + j, m, vr[row : row + ROWS])


def gram_kernel(x_ref, v0_ref, o_ref, xs, gs, ps):
    xs[...] = x_ref[...].astype(F32).reshape(TOTAL * CQ, LAT)
    pad = jnp.zeros((LAT - TOTAL, LAT), BF16)
    q, k = [], []
    for r in range(HALF):
        q.append(xs[pl.ds(r, TOTAL, stride=CQ), :].astype(BF16))
        k.append(jnp.concatenate([xs[pl.ds(HALF + r, TOTAL, stride=CQ), :].astype(BF16), pad], axis=0))
    gram = lax.dot_general(
        jnp.concatenate(q, axis=1),
        jnp.concatenate(k, axis=1),
        (((1,), (1,)), ((), ())),
        preferred_element_type=F32,
    )
    lane = lax.broadcasted_iota(jnp.int32, gram.shape, 1)
    gs[0] = gram
    gs[1] = jnp.where(lane < TOTAL, 0.0, pltpu.roll(gram, TOTAL, 1))
    gs[2] = jnp.where(lane < TOTAL, 0.0, pltpu.roll(gram, TOTAL - CUT, 1))
    rest = jnp.zeros((2, LAT), F32)
    for s in range(MEM):
        row = s * OWN
        free = [gs[1 + h, row + 4 : row + 5, :] for h in range(2)]
        ps[0, 4 * s : 4 * s + 4] = gs[0, row : row + 4, :] + jnp.concatenate(free + [rest], axis=0)
    for part in range(2):
        whole = ps[part]
        high = whole.astype(BF16).astype(F32)
        ps[part] = high
        ps[part + 1] = whole - high
    for s in range(MEM):
        for part in range(3):
            ps[3, 4 * part : 4 * part + 4] = ps[part, 4 * s : 4 * s + 4]
        ps[3, 12:HEAD] = jnp.zeros((HEAD - 12, LAT), F32)
        o_ref[s, 0:HEAD] = ps[3, 0:HEAD].astype(BF16)


def total_kernel(x_ref, o_ref):
    parts = jnp.sum(x_ref[:, 0:HEAD].astype(F32), axis=0)
    o_ref[...] = parts[0:4] + parts[4:8] + parts[8:12]


def spread_kernel(x_ref, o_ref):
    o_ref[...] = jnp.broadcast_to((x_ref[0] + x_ref[1])[None], o_ref.shape)


def softmax_kernel(scale, x_ref, v1_ref, o_ref, gs):
    gs[...] = jnp.zeros(gs.shape, F32)
    gs[0:4] = jnp.sum(x_ref[...], axis=0)
    gram = gs[...]
    head, tail = pltpu.roll(gram, LAT - TOTAL, 1), pltpu.roll(gram, LAT - TOTAL + CUT, 1)
    lane = lax.broadcasted_iota(jnp.int32, gram.shape, 1)
    gs[4:5] = jnp.where(lane[0:1] < CUT, head[0:1], tail[1:2])
    s = jnp.where(lane < TOTAL, gs[...] * scale, -jnp.inf)
    e = jnp.exp(s - jnp.max(s, axis=1, keepdims=True))
    w = e / jnp.sum(e, axis=1, keepdims=True)
    row = lax.broadcasted_iota(jnp.int32, (MEM, 8, LAT), 1)
    for m in range(OWN):
        block = v1_ref[:, m].astype(F32)
        o_ref[:, m] = jnp.where(row == USED - 8, w[m : m + 1][None], block).astype(BF16)


def mix_kernel(v0_ref, v1_ref, o_ref, vs, ms):
    vs[0] = v0_ref[:, HEAD:].astype(F32).reshape(TOTAL * 8, LAT)
    vs[1] = v1_ref[...].astype(F32).reshape(TOTAL * 8, LAT)
    rows = [vs[r // 8, pl.ds(r % 8, TOTAL, stride=8), :].astype(BF16) for r in range(ROWS)]
    w = rows[USED][:, :TOTAL]
    v = jnp.concatenate(rows[:USED], axis=1)
    mixed = jnp.dot(w, v, preferred_element_type=F32)
    for r in range(USED):
        ms[pl.ds(r, TOTAL, stride=ROWS), :] = mixed[:, r * LAT : (r + 1) * LAT]
    ms[pl.ds(USED, TOTAL, stride=ROWS), :] = jnp.zeros((TOTAL, LAT), F32)
    o_ref[...] = ms[...].astype(BF16).reshape(o_ref.shape)


def finish_kernel(x_ref, f_ref, w_ref, o_ref, mc, sh, br, ob, sem):
    copies = [pltpu.make_async_copy(ob.at[m], o_ref.at[m], sem.at[m]) for m in range(OWN)]
    for m in range(OWN):
        for j in range(MEM):
            mc[j * USED : j * USED + ROWS] = x_ref[j, m].astype(F32)
        whole = mc[0 : EXT * CQ]
        before, after = lat_shifts(whole)
        for b, x in enumerate((before, whole, after)):
            sh[b] = x.astype(BF16)
        for i in range(0, COLS, 4):
            patches = [
                jnp.concatenate([sh[b, p * CQ : (p + 4) * CQ] for b in range(3)], axis=0)
                for p in (i, i + 2)
            ]
            r = jnp.dot(w_ref[...], jnp.concatenate(patches, axis=1), preferred_element_type=F32)
            for n in range(4):
                rows, lanes = (n % 2) * CH, (n // 2) * LAT
                br[pl.ds(i + n, CH, stride=COLS), :] = r[rows : rows + CH, lanes : lanes + LAT]
        ob[m] = (f_ref[m].astype(F32) + br[...].reshape(CH, COLS, LAT)).astype(BF16)
        copies[m].start()
    for copy in copies:
        copy.wait()


def shards(fields, w_query, w_key, w_value, w_out):
    edge = jax.ShapeDtypeStruct((OWN, 2 * CH, LAT), BF16)
    plane = pltpu.VMEM((CH * COLS, LAT), F32)
    sib, nb = call(edges_kernel, (edge, edge), [plane], 0, 1_000_000, fields)
    swaps = [(i, (i - 1 if i % 2 == 0 else i + 1) % LON) for i in range(LON)]
    got_nb = lax.ppermute(nb, ("yhi", "x", "core"), swaps)
    got_sib = lax.all_gather(sib, "core", axis=0, tiled=False)
    qk_shape = jax.ShapeDtypeStruct((MEM, OWN, CQ, LAT), BF16)
    v0_shape = jax.ShapeDtypeStruct((MEM, HEAD + OWN * 8, LAT), BF16)
    v1_shape = jax.ShapeDtypeStruct((MEM, OWN, 8, LAT), BF16)
    ends = jax.ShapeDtypeStruct((OWN, 2 * ROWS, LAT), F32)
    pair = jax.ShapeDtypeStruct((18 * CQ, 4 * CH), BF16)
    pair_out = jax.ShapeDtypeStruct((2 * CH, 12 * CQ), BF16)
    qk, v0, v1, ends, w_pair, w_last = call(
        inner_kernel,
        (qk_shape, v0_shape, v1_shape, ends, pair, pair_out),
        [
            pltpu.VMEM((3 * CQ, 9 * CH), F32),
            plane,
            pltpu.VMEM((OWN, CH * COLS, LAT), BF16),
            pltpu.VMEM((OWN, 6 * CQ, LAT), F32),
        ],
        450_000_000,
        2_000_000,
        fields,
        w_query,
        w_key,
        w_value,
        w_out,
    )
    qk, v0, v1 = call(
        outer_kernel,
        (qk_shape, v0_shape, v1_shape),
        [pltpu.VMEM((OWN, 4 * CH, LAT), BF16)] * 2
        + [pltpu.VMEM((2 * CQ + ROWS, LAT), F32), pltpu.VMEM((2 * CQ + ROWS + 8, LAT), F32)],
        300_000_000,
        1_500_000,
        qk,
        v0,
        v1,
        ends,
        w_pair,
        sib,
        nb,
        got_sib,
        got_nb,
        alias={0: 0, 1: 1, 2: 2},
    )
    mem, lon = ("z", "ylo"), ("yhi", "x")
    qk = lax.all_to_all(qk, mem, 0, 0, tiled=True)
    v0 = call(
        gram_kernel,
        v0_shape,
        [
            pltpu.VMEM((TOTAL * CQ, LAT), F32),
            pltpu.VMEM((3, TOTAL, LAT), F32),
            pltpu.VMEM((4, 4 * MEM, LAT), F32),
        ],
        20_000_000,
        800_000,
        qk,
        v0,
        alias={1: 0},
    )
    v0 = lax.all_to_all(v0, mem, 0, 0, tiled=True)
    gram = call(total_kernel, jax.ShapeDtypeStruct((4, LAT), F32), [], 40_000, 200_000, v0)
    gram = lax.all_gather(gram, "core", axis=0, tiled=False)
    copies = jax.ShapeDtypeStruct((LON // 2, 4, LAT), F32)
    gram = call(spread_kernel, copies, [], 10_000, 40_000, gram)
    gram = lax.all_to_all(gram, lon, 0, 0, tiled=True)
    scale = 1.0 / math.sqrt(CQ * LAT * COLS * LON)
    v1 = call(
        functools.partial(softmax_kernel, scale),
        v1_shape,
        [pltpu.VMEM((8, LAT), F32)],
        40_000,
        400_000,
        gram,
        v1,
        alias={1: 0},
    )
    v1 = lax.all_to_all(v1, mem, 0, 0, tiled=True)
    mixed = call(
        mix_kernel,
        jax.ShapeDtypeStruct((MEM, OWN, ROWS, LAT), BF16),
        [pltpu.VMEM((2, TOTAL * 8, LAT), F32), pltpu.VMEM((TOTAL * ROWS, LAT), F32)],
        30_000_000,
        700_000,
        v0,
        v1,
    )
    mixed = lax.all_to_all(mixed, ("z", "ylo"), 0, 0, tiled=True)
    return call(
        finish_kernel,
        jax.ShapeDtypeStruct(fields.shape, BF16),
        [
            pltpu.VMEM((MEM * ROWS, LAT), F32),
            pltpu.VMEM((3, EXT * CQ, LAT), BF16),
            plane,
            pltpu.VMEM(fields.shape, BF16),
            pltpu.SemaphoreType.DMA((OWN,)),
        ],
        150_000_000,
        1_700_000,
        mixed,
        fields,
        w_last,
        far_out=True,
    )


def solution(mesh):
    fine = Mesh(mesh.devices.reshape(MEM // 2, 2, LON // 8, 4, 2), ("z", "ylo", "yhi", "x", "core"))
    spec = P(("z", "ylo"), None, ("yhi", "x", "core"), None)
    return jax.shard_map(
        shards,
        mesh=fine,
        in_specs=(spec, P(), P(), P(), P()),
        out_specs=spec,
        check_vma=False,
    )
```

```python
import functools
import math

import jax
import jax.numpy as jnp
from jax import lax
from jax.experimental import pallas as pl
from jax.experimental.pallas import tpu as pltpu
from jax.sharding import Mesh
from jax.sharding import PartitionSpec as P

CH, CQ, LAT = 64, 24, 128
HALF = CQ // 2
MEM, LON = 16, 32
OWN = 5
TOTAL = MEM * OWN
CUT = LAT - TOTAL
COLS = 8
EXT = COLS + 2
ROWS = 16
USED = EXT * CQ // MEM
HEAD = 8
F32, BF16 = jnp.float32, jnp.bfloat16
VMEM = pl.BlockSpec(memory_space=pltpu.VMEM)


HBM = pl.BlockSpec(memory_space=pl.ANY)


def call(body, outs, scratch, flops, nbytes, *args, alias=None, far_out=False):
    many = isinstance(outs, tuple)
    one = HBM if far_out else VMEM
    return pl.pallas_call(
        body,
        out_shape=outs,
        in_specs=[VMEM] * len(args),
        out_specs=(one,) * len(outs) if many else one,
        scratch_shapes=scratch,
        input_output_aliases=alias or {},
        compiler_params=pltpu.CompilerParams(vmem_limit_bytes=32 * 1024 * 1024),
        cost_estimate=pl.CostEstimate(flops=flops, bytes_accessed=nbytes, transcendentals=0),
    )(*args)


def lat_shifts(x):
    lane = lax.broadcasted_iota(jnp.int32, x.shape, 1)
    before = jnp.where(lane == 0, 0.0, pltpu.roll(x, 1, 1))
    after = jnp.where(lane == LAT - 1, 0.0, pltpu.roll(x, LAT - 1, 1))
    return before, after


def edges_kernel(f_ref, sib_ref, nb_ref, xf):
    even = lax.axis_index("core") == 0
    for m in range(OWN):
        xf[...] = f_ref[m].astype(F32).reshape(CH * COLS, LAT)
        for s in range(2):
            left = xf[pl.ds(s, CH, stride=COLS), :]
            right = xf[pl.ds(COLS - 2 + s, CH, stride=COLS), :]
            sib_ref[m, s * CH : (s + 1) * CH] = jnp.where(even, right, left).astype(BF16)
            nb_ref[m, s * CH : (s + 1) * CH] = jnp.where(even, left, right).astype(BF16)


def conv_pairs(w, xs):
    width = 3 * CQ
    lane = lax.broadcasted_iota(jnp.int32, (width, LAT), 1)
    wide = jnp.dot(w, jnp.concatenate(xs, axis=1), preferred_element_type=F32)
    pairs = []
    for n in range(len(xs)):
        r = wide[:, n * LAT : (n + 1) * LAT]
        outs = []
        for s in range(2):
            y = [r[(3 * s + b) * width : (3 * s + b + 1) * width] for b in range(3)]
            outs.append(
                y[1]
                + jnp.where(lane == 0, 0.0, pltpu.roll(y[0], 1, 1))
                + jnp.where(lane == LAT - 1, 0.0, pltpu.roll(y[2], LAT - 1, 1))
            )
        pairs.append(outs)
    return pairs


def put_block(v0_ref, v1_ref, j, m, block):
    v0_ref[j, HEAD + m * 8 : HEAD + m * 8 + 8] = block[:8].astype(BF16)
    v1_ref[j, m] = block[8:].astype(BF16)


def put_pair(qk_ref, vs, m, p, outs):
    for s in range(2):
        col = 2 * p + s
        vs[s * CQ : (s + 1) * CQ] = outs[s][2 * CQ :]
        if 1 <= col <= COLS:
            for h in range(2):
                qk_ref[2 * (col - 1) + h, m] = outs[s][h * CQ : (h + 1) * CQ].astype(BF16)


def inner_kernel(
    f_ref, wq_ref, wk_ref, wv_ref, wo_ref, qk_ref, v0_ref, v1_ref, e_ref, wp_ref, wf_ref, ws, xf, xt, vs
):
    ws[0:HALF] = wq_ref[...].astype(F32)[:HALF]
    ws[HALF : 2 * HALF] = wk_ref[...].astype(F32)[:HALF]
    ws[2 * HALF : 3 * HALF] = wq_ref[...].astype(F32)[HALF:]
    ws[3 * HALF : 4 * HALF] = wk_ref[...].astype(F32)[HALF:]
    ws[2 * CQ :] = wv_ref[...].astype(F32)
    zero = jnp.zeros((3 * CQ, CH), F32)
    for b in range(3):
        taps = [ws[:, (3 * a + b) * CH : (3 * a + b + 1) * CH] for a in range(3)]
        for s in range(2):
            row = (3 * s + b) * 3 * CQ
            full = [zero] + taps if s else taps + [zero]
            wp_ref[row : row + 3 * CQ] = jnp.concatenate(full, axis=1).astype(BF16)
    wo = wo_ref[...].astype(F32)
    zero = jnp.zeros((CH, CQ), F32)
    for s in range(2):
        full = []
        for b in range(3):
            taps = [wo[:, (3 * a + b) * CQ : (3 * a + b + 1) * CQ] for a in range(3)]
            full += [zero] + taps if s else taps + [zero]
        wf_ref[s * CH : (s + 1) * CH] = jnp.concatenate(full, axis=1).astype(BF16)
    for m in range(OWN):
        xf[...] = f_ref[m].astype(F32).reshape(CH * COLS, LAT)
        for i in range(COLS):
            xt[m, i * CH : (i + 1) * CH] = xf[pl.ds(i, CH, stride=COLS), :].astype(BF16)
    units = [(m, p) for m in range(OWN) for p in range(1, EXT // 2 - 1)]
    for n in range(0, len(units), 2):
        two = units[n : n + 2]
        xs = [xt[m, 2 * (p - 1) * CH : 2 * (p + 1) * CH] for m, p in two]
        for (m, p), outs in zip(two, conv_pairs(wp_ref[...], xs)):
            put_pair(qk_ref, vs.at[m, pl.ds((p - 1) * 2 * CQ, 2 * CQ)], m, p, outs)
    for m in range(OWN):
        for j in range(4, 12):
            row = j * USED - 2 * CQ
            put_block(v0_ref, v1_ref, j, m, vs[m, row : row + ROWS])
        e_ref[m, 0:ROWS] = vs[m, 0:ROWS]
        e_ref[m, ROWS:] = vs[m, 6 * CQ - ROWS :]


def outer_kernel(
    iq_ref, i0_ref, i1_ref, e_ref, wp_ref, sib_ref, nb_ref, gs_ref, gn_ref,
    qk_ref, v0_ref, v1_ref, xl, xr, vl, vr
):
    core = lax.axis_index("core")
    near = 2 * CH

    @pl.when(core == 0)
    def _():
        xl[:, :near] = gn_ref[...]
        xl[:, near:] = nb_ref[...]
        xr[:, :near] = sib_ref[...]
        xr[:, near:] = gs_ref[1]

    @pl.when(core == 1)
    def _():
        xl[:, :near] = gs_ref[0]
        xl[:, near:] = sib_ref[...]
        xr[:, :near] = nb_ref[...]
        xr[:, near:] = gn_ref[...]

    for m in range(OWN):
        left, right = conv_pairs(wp_ref[...], [xl[m], xr[m]])
        put_pair(qk_ref, vl.at[pl.ds(0, 2 * CQ)], m, 0, left)
        put_pair(qk_ref, vr.at[pl.ds(ROWS, 2 * CQ)], m, EXT // 2 - 1, right)
        vl[2 * CQ :] = e_ref[m, 0:ROWS]
        vr[0:ROWS] = e_ref[m, ROWS:]
        vr[ROWS + 2 * CQ :] = jnp.zeros((8, LAT), F32)
        for j in range(4):
            put_block(v0_ref, v1_ref, j, m, vl[j * USED : j * USED + ROWS])
            row = (12 + j) * USED - (8 * CQ - ROWS)
            put_block(v0_ref, v1_ref, 12 + j, m, vr[row : row + ROWS])


def gram_kernel(x_ref, v0_ref, o_ref, xs, gs, ps):
    xs[...] = x_ref[...].astype(F32).reshape(TOTAL * CQ, LAT)
    pad = jnp.zeros((LAT - TOTAL, LAT), BF16)
    q, k = [], []
    for r in range(HALF):
        q.append(xs[pl.ds(r, TOTAL, stride=CQ), :].astype(BF16))
        k.append(jnp.concatenate([xs[pl.ds(HALF + r, TOTAL, stride=CQ), :].astype(BF16), pad], axis=0))
    gram = lax.dot_general(
        jnp.concatenate(q, axis=1),
        jnp.concatenate(k, axis=1),
        (((1,), (1,)), ((), ())),
        preferred_element_type=F32,
    )
    lane = lax.broadcasted_iota(jnp.int32, gram.shape, 1)
    gs[0] = gram
    gs[1] = jnp.where(lane < TOTAL, 0.0, pltpu.roll(gram, TOTAL, 1))
    gs[2] = jnp.where(lane < TOTAL, 0.0, pltpu.roll(gram, TOTAL - CUT, 1))
    rest = jnp.zeros((2, LAT), F32)
    for s in range(MEM):
        row = s * OWN
        free = [gs[1 + h, row + 4 : row + 5, :] for h in range(2)]
        ps[0, 4 * s : 4 * s + 4] = gs[0, row : row + 4, :] + jnp.concatenate(free + [rest], axis=0)
    whole = ps[0]
    high = whole.astype(BF16).astype(F32)
    ps[0] = high
    ps[1] = whole - high
    for s in range(MEM):
        parts = [ps[part, 4 * s : 4 * s + 4] for part in range(2)]
        o_ref[s, 0:HEAD] = jnp.concatenate(parts, axis=0).astype(BF16)


def spread_kernel(x_ref, o_ref):
    parts = jnp.sum(x_ref[:, 0:HEAD].astype(F32), axis=0)
    o_ref[...] = jnp.broadcast_to((parts[0:4] + parts[4:8])[None], o_ref.shape)


def softmax_kernel(scale, x_ref, v1_ref, o_ref, gs):
    gs[...] = jnp.zeros(gs.shape, F32)
    gs[0:4] = jnp.sum(x_ref[...], axis=0)
    gram = gs[...]
    head, tail = pltpu.roll(gram, LAT - TOTAL, 1), pltpu.roll(gram, LAT - TOTAL + CUT, 1)
    lane = lax.broadcasted_iota(jnp.int32, gram.shape, 1)
    gs[4:5] = jnp.where(lane[0:1] < CUT, head[0:1], tail[1:2])
    s = jnp.where(lane < TOTAL, gs[...] * scale, -jnp.inf)
    e = jnp.exp(s - jnp.max(s, axis=1, keepdims=True))
    w = e / jnp.sum(e, axis=1, keepdims=True)
    row = lax.broadcasted_iota(jnp.int32, (MEM, 8, LAT), 1)
    for m in range(OWN):
        block = v1_ref[:, m].astype(F32)
        o_ref[:, m] = jnp.where(row == USED - 8, w[m : m + 1][None], block).astype(BF16)


def mix_kernel(v0_ref, v1_ref, o_ref, vs, ms):
    vs[0] = v0_ref[:, HEAD:].astype(F32).reshape(TOTAL * 8, LAT)
    vs[1] = v1_ref[...].astype(F32).reshape(TOTAL * 8, LAT)
    rows = [vs[r // 8, pl.ds(r % 8, TOTAL, stride=8), :].astype(BF16) for r in range(ROWS)]
    w = rows[USED][:, :TOTAL]
    v = jnp.concatenate(rows[:USED], axis=1)
    mixed = jnp.dot(w, v, preferred_element_type=F32)
    for r in range(USED):
        ms[pl.ds(r, TOTAL, stride=ROWS), :] = mixed[:, r * LAT : (r + 1) * LAT]
    ms[pl.ds(USED, TOTAL, stride=ROWS), :] = jnp.zeros((TOTAL, LAT), F32)
    o_ref[...] = ms[...].astype(BF16).reshape(o_ref.shape)


def finish_kernel(x_ref, f_ref, w_ref, o_ref, mc, sh, br, ob, sem):
    copies = [pltpu.make_async_copy(ob.at[m], o_ref.at[m], sem.at[m]) for m in range(OWN)]
    for m in range(OWN):
        for j in range(MEM):
            mc[j * USED : j * USED + ROWS] = x_ref[j, m].astype(F32)
        whole = mc[0 : EXT * CQ]
        before, after = lat_shifts(whole)
        for b, x in enumerate((before, whole, after)):
            sh[b] = x.astype(BF16)
        for i in range(0, COLS, 4):
            patches = [
                jnp.concatenate([sh[b, p * CQ : (p + 4) * CQ] for b in range(3)], axis=0)
                for p in (i, i + 2)
            ]
            r = jnp.dot(w_ref[...], jnp.concatenate(patches, axis=1), preferred_element_type=F32)
            for n in range(4):
                rows, lanes = (n % 2) * CH, (n // 2) * LAT
                br[pl.ds(i + n, CH, stride=COLS), :] = r[rows : rows + CH, lanes : lanes + LAT]
        ob[m] = (f_ref[m].astype(F32) + br[...].reshape(CH, COLS, LAT)).astype(BF16)
        copies[m].start()
    for copy in copies:
        copy.wait()


def shards(fields, w_query, w_key, w_value, w_out):
    edge = jax.ShapeDtypeStruct((OWN, 2 * CH, LAT), BF16)
    plane = pltpu.VMEM((CH * COLS, LAT), F32)
    sib, nb = call(edges_kernel, (edge, edge), [plane], 0, 1_000_000, fields)
    swaps = [(i, (i - 1 if i % 2 == 0 else i + 1) % LON) for i in range(LON)]
    got_nb = lax.ppermute(nb, ("yhi", "x", "core"), swaps)
    got_sib = lax.all_gather(sib, "core", axis=0, tiled=False)
    qk_shape = jax.ShapeDtypeStruct((MEM, OWN, CQ, LAT), BF16)
    v0_shape = jax.ShapeDtypeStruct((MEM, HEAD + OWN * 8, LAT), BF16)
    v1_shape = jax.ShapeDtypeStruct((MEM, OWN, 8, LAT), BF16)
    ends = jax.ShapeDtypeStruct((OWN, 2 * ROWS, LAT), F32)
    pair = jax.ShapeDtypeStruct((18 * CQ, 4 * CH), BF16)
    pair_out = jax.ShapeDtypeStruct((2 * CH, 12 * CQ), BF16)
    qk, v0, v1, ends, w_pair, w_last = call(
        inner_kernel,
        (qk_shape, v0_shape, v1_shape, ends, pair, pair_out),
        [
            pltpu.VMEM((3 * CQ, 9 * CH), F32),
            plane,
            pltpu.VMEM((OWN, CH * COLS, LAT), BF16),
            pltpu.VMEM((OWN, 6 * CQ, LAT), F32),
        ],
        450_000_000,
        2_000_000,
        fields,
        w_query,
        w_key,
        w_value,
        w_out,
    )
    qk, v0, v1 = call(
        outer_kernel,
        (qk_shape, v0_shape, v1_shape),
        [pltpu.VMEM((OWN, 4 * CH, LAT), BF16)] * 2
        + [pltpu.VMEM((2 * CQ + ROWS, LAT), F32), pltpu.VMEM((2 * CQ + ROWS + 8, LAT), F32)],
        300_000_000,
        1_500_000,
        qk,
        v0,
        v1,
        ends,
        w_pair,
        sib,
        nb,
        got_sib,
        got_nb,
        alias={0: 0, 1: 1, 2: 2},
    )
    mem, lon = ("z", "ylo"), ("yhi", "x", "core")
    qk = lax.all_to_all(qk, mem, 0, 0, tiled=True)
    v0 = call(
        gram_kernel,
        v0_shape,
        [
            pltpu.VMEM((TOTAL * CQ, LAT), F32),
            pltpu.VMEM((3, TOTAL, LAT), F32),
            pltpu.VMEM((2, 4 * MEM, LAT), F32),
        ],
        20_000_000,
        800_000,
        qk,
        v0,
        alias={1: 0},
    )
    v0 = lax.all_to_all(v0, mem, 0, 0, tiled=True)
    copies = jax.ShapeDtypeStruct((LON, 4, LAT), F32)
    gram = call(spread_kernel, copies, [], 40_000, 200_000, v0)
    gram = lax.all_to_all(gram, lon, 0, 0, tiled=True)
    scale = 1.0 / math.sqrt(CQ * LAT * COLS * LON)
    v1 = call(
        functools.partial(softmax_kernel, scale),
        v1_shape,
        [pltpu.VMEM((8, LAT), F32)],
        40_000,
        400_000,
        gram,
        v1,
        alias={1: 0},
    )
    v1 = lax.all_to_all(v1, mem, 0, 0, tiled=True)
    mixed = call(
        mix_kernel,
        jax.ShapeDtypeStruct((MEM, OWN, ROWS, LAT), BF16),
        [pltpu.VMEM((2, TOTAL * 8, LAT), F32), pltpu.VMEM((TOTAL * ROWS, LAT), F32)],
        30_000_000,
        700_000,
        v0,
        v1,
    )
    mixed = lax.all_to_all(mixed, ("z", "ylo"), 0, 0, tiled=True)
    return call(
        finish_kernel,
        jax.ShapeDtypeStruct(fields.shape, BF16),
        [
            pltpu.VMEM((MEM * ROWS, LAT), F32),
            pltpu.VMEM((3, EXT * CQ, LAT), BF16),
            plane,
            pltpu.VMEM(fields.shape, BF16),
            pltpu.SemaphoreType.DMA((OWN,)),
        ],
        150_000_000,
        1_700_000,
        mixed,
        fields,
        w_last,
        far_out=True,
    )


def solution(mesh):
    fine = Mesh(mesh.devices.reshape(MEM // 2, 2, LON // 8, 4, 2), ("z", "ylo", "yhi", "x", "core"))
    spec = P(("z", "ylo"), None, ("yhi", "x", "core"), None)
    return jax.shard_map(
        shards,
        mesh=fine,
        in_specs=(spec, P(), P(), P(), P()),
        out_specs=spec,
        check_vma=False,
    )
```

```python
import functools
import math

import jax
import jax.numpy as jnp
from jax import lax
from jax.experimental import pallas as pl
from jax.experimental.pallas import tpu as pltpu
from jax.sharding import Mesh
from jax.sharding import PartitionSpec as P

CH, CQ, LAT = 64, 24, 128
HALF = CQ // 2
MEM, LON = 16, 32
OWN = 5
TOTAL = MEM * OWN
CUT = LAT - TOTAL
COLS = 8
EXT = COLS + 2
ROWS = 16
USED = EXT * CQ // MEM
HEAD = 8
F32, BF16 = jnp.float32, jnp.bfloat16
VMEM = pl.BlockSpec(memory_space=pltpu.VMEM)


HBM = pl.BlockSpec(memory_space=pl.ANY)


def call(body, outs, scratch, flops, nbytes, *args, alias=None, far_out=False):
    many = isinstance(outs, tuple)
    one = HBM if far_out else VMEM
    return pl.pallas_call(
        body,
        out_shape=outs,
        in_specs=[VMEM] * len(args),
        out_specs=(one,) * len(outs) if many else one,
        scratch_shapes=scratch,
        input_output_aliases=alias or {},
        compiler_params=pltpu.CompilerParams(vmem_limit_bytes=32 * 1024 * 1024),
        cost_estimate=pl.CostEstimate(flops=flops, bytes_accessed=nbytes, transcendentals=0),
    )(*args)


def lat_shifts(x):
    lane = lax.broadcasted_iota(jnp.int32, x.shape, 1)
    before = jnp.where(lane == 0, 0.0, pltpu.roll(x, 1, 1))
    after = jnp.where(lane == LAT - 1, 0.0, pltpu.roll(x, LAT - 1, 1))
    return before, after


def edges_kernel(f_ref, sib_ref, nb_ref, xf):
    even = lax.axis_index("core") == 0
    for m in range(OWN):
        xf[...] = f_ref[m].astype(F32).reshape(CH * COLS, LAT)
        for s in range(2):
            left = xf[pl.ds(s, CH, stride=COLS), :]
            right = xf[pl.ds(COLS - 2 + s, CH, stride=COLS), :]
            sib_ref[m, s * CH : (s + 1) * CH] = jnp.where(even, right, left).astype(BF16)
            nb_ref[m, s * CH : (s + 1) * CH] = jnp.where(even, left, right).astype(BF16)


def conv_pairs(w, xs):
    width = 3 * CQ
    lane = lax.broadcasted_iota(jnp.int32, (width, LAT), 1)
    wide = jnp.dot(w, jnp.concatenate(xs, axis=1), preferred_element_type=F32)
    pairs = []
    for n in range(len(xs)):
        r = wide[:, n * LAT : (n + 1) * LAT]
        outs = []
        for s in range(2):
            y = [r[(3 * s + b) * width : (3 * s + b + 1) * width] for b in range(3)]
            outs.append(
                y[1]
                + jnp.where(lane == 0, 0.0, pltpu.roll(y[0], 1, 1))
                + jnp.where(lane == LAT - 1, 0.0, pltpu.roll(y[2], LAT - 1, 1))
            )
        pairs.append(outs)
    return pairs


def put_block(v0_ref, v1_ref, j, m, block):
    v0_ref[j, HEAD + m * 8 : HEAD + m * 8 + 8] = block[:8].astype(BF16)
    v1_ref[j, m] = block[8:].astype(BF16)


def put_pair(qk_ref, vs, m, p, outs):
    for s in range(2):
        col = 2 * p + s
        vs[s * CQ : (s + 1) * CQ] = outs[s][2 * CQ :]
        if 1 <= col <= COLS:
            for h in range(2):
                qk_ref[2 * (col - 1) + h, m] = outs[s][h * CQ : (h + 1) * CQ].astype(BF16)


def inner_kernel(
    f_ref, wq_ref, wk_ref, wv_ref, wo_ref, qk_ref, v0_ref, v1_ref, e_ref, wp_ref, wf_ref, ws, xf, xt, vs
):
    ws[0:HALF] = wq_ref[...].astype(F32)[:HALF]
    ws[HALF : 2 * HALF] = wk_ref[...].astype(F32)[:HALF]
    ws[2 * HALF : 3 * HALF] = wq_ref[...].astype(F32)[HALF:]
    ws[3 * HALF : 4 * HALF] = wk_ref[...].astype(F32)[HALF:]
    ws[2 * CQ :] = wv_ref[...].astype(F32)
    zero = jnp.zeros((3 * CQ, CH), F32)
    for b in range(3):
        taps = [ws[:, (3 * a + b) * CH : (3 * a + b + 1) * CH] for a in range(3)]
        for s in range(2):
            row = (3 * s + b) * 3 * CQ
            full = [zero] + taps if s else taps + [zero]
            wp_ref[row : row + 3 * CQ] = jnp.concatenate(full, axis=1).astype(BF16)
    wo = wo_ref[...].astype(F32)
    zero = jnp.zeros((CH, CQ), F32)
    for s in range(2):
        full = []
        for b in range(3):
            taps = [wo[:, (3 * a + b) * CQ : (3 * a + b + 1) * CQ] for a in range(3)]
            full += [zero] + taps if s else taps + [zero]
        wf_ref[s * CH : (s + 1) * CH] = jnp.concatenate(full, axis=1).astype(BF16)
    for m in range(OWN):
        xf[...] = f_ref[m].astype(F32).reshape(CH * COLS, LAT)
        for i in range(COLS):
            xt[m, i * CH : (i + 1) * CH] = xf[pl.ds(i, CH, stride=COLS), :].astype(BF16)
    units = [(m, p) for m in range(OWN) for p in range(1, EXT // 2 - 1)]
    for n in range(0, len(units), 2):
        two = units[n : n + 2]
        xs = [xt[m, 2 * (p - 1) * CH : 2 * (p + 1) * CH] for m, p in two]
        for (m, p), outs in zip(two, conv_pairs(wp_ref[...], xs)):
            put_pair(qk_ref, vs.at[m, pl.ds((p - 1) * 2 * CQ, 2 * CQ)], m, p, outs)
    for m in range(OWN):
        for j in range(4, 12):
            row = j * USED - 2 * CQ
            put_block(v0_ref, v1_ref, j, m, vs[m, row : row + ROWS])
        e_ref[m, 0:ROWS] = vs[m, 0:ROWS]
        e_ref[m, ROWS:] = vs[m, 6 * CQ - ROWS :]


def outer_kernel(
    iq_ref, i0_ref, i1_ref, e_ref, wp_ref, sib_ref, nb_ref, gs_ref, gn_ref,
    qk_ref, v0_ref, v1_ref, xl, xr, vl, vr
):
    core = lax.axis_index("core")
    near = 2 * CH

    @pl.when(core == 0)
    def _():
        xl[:, :near] = gn_ref[...]
        xl[:, near:] = nb_ref[...]
        xr[:, :near] = sib_ref[...]
        xr[:, near:] = gs_ref[1]

    @pl.when(core == 1)
    def _():
        xl[:, :near] = gs_ref[0]
        xl[:, near:] = sib_ref[...]
        xr[:, :near] = nb_ref[...]
        xr[:, near:] = gn_ref[...]

    for m in range(OWN):
        left, right = conv_pairs(wp_ref[...], [xl[m], xr[m]])
        put_pair(qk_ref, vl.at[pl.ds(0, 2 * CQ)], m, 0, left)
        put_pair(qk_ref, vr.at[pl.ds(ROWS, 2 * CQ)], m, EXT // 2 - 1, right)
        vl[2 * CQ :] = e_ref[m, 0:ROWS]
        vr[0:ROWS] = e_ref[m, ROWS:]
        vr[ROWS + 2 * CQ :] = jnp.zeros((8, LAT), F32)
        for j in range(4):
            put_block(v0_ref, v1_ref, j, m, vl[j * USED : j * USED + ROWS])
            row = (12 + j) * USED - (8 * CQ - ROWS)
            put_block(v0_ref, v1_ref, 12 + j, m, vr[row : row + ROWS])


def gram_kernel(x_ref, v0_ref, o_ref, xs, gs, ps):
    xs[...] = x_ref[...].astype(F32).reshape(TOTAL * CQ, LAT)
    pad = jnp.zeros((LAT - TOTAL, LAT), BF16)
    q, k = [], []
    for r in range(HALF):
        q.append(xs[pl.ds(r, TOTAL, stride=CQ), :].astype(BF16))
        k.append(jnp.concatenate([xs[pl.ds(HALF + r, TOTAL, stride=CQ), :].astype(BF16), pad], axis=0))
    gram = lax.dot_general(
        jnp.concatenate(q, axis=1),
        jnp.concatenate(k, axis=1),
        (((1,), (1,)), ((), ())),
        preferred_element_type=F32,
    )
    lane = lax.broadcasted_iota(jnp.int32, gram.shape, 1)
    gs[0] = gram
    gs[1] = jnp.where(lane < TOTAL, 0.0, pltpu.roll(gram, TOTAL, 1))
    gs[2] = jnp.where(lane < TOTAL, 0.0, pltpu.roll(gram, TOTAL - CUT, 1))
    rest = jnp.zeros((2, LAT), F32)
    for s in range(MEM):
        row = s * OWN
        free = [gs[1 + h, row + 4 : row + 5, :] for h in range(2)]
        ps[0, 4 * s : 4 * s + 4] = gs[0, row : row + 4, :] + jnp.concatenate(free + [rest], axis=0)
    whole = ps[0]
    high = whole.astype(BF16).astype(F32)
    ps[0] = high
    ps[1] = whole - high
    for s in range(MEM):
        parts = [ps[part, 4 * s : 4 * s + 4] for part in range(2)]
        o_ref[s, 0:HEAD] = jnp.concatenate(parts, axis=0).astype(BF16)


def total_kernel(x_ref, o_ref):
    parts = jnp.sum(x_ref[:, 0:HEAD].astype(F32), axis=0)
    o_ref[...] = parts[0:4] + parts[4:8]


def spread_kernel(x_ref, o_ref):
    o_ref[...] = jnp.broadcast_to((x_ref[0] + x_ref[1])[None], o_ref.shape)


def softmax_kernel(scale, x_ref, v1_ref, o_ref, gs):
    gs[...] = jnp.zeros(gs.shape, F32)
    gs[0:4] = jnp.sum(x_ref[...], axis=0)
    gram = gs[...]
    head, tail = pltpu.roll(gram, LAT - TOTAL, 1), pltpu.roll(gram, LAT - TOTAL + CUT, 1)
    lane = lax.broadcasted_iota(jnp.int32, gram.shape, 1)
    gs[4:5] = jnp.where(lane[0:1] < CUT, head[0:1], tail[1:2])
    s = jnp.where(lane < TOTAL, gs[...] * scale, -jnp.inf)
    e = jnp.exp(s - jnp.max(s, axis=1, keepdims=True))
    w = e / jnp.sum(e, axis=1, keepdims=True)
    row = lax.broadcasted_iota(jnp.int32, (MEM, 8, LAT), 1)
    for m in range(OWN):
        block = v1_ref[:, m].astype(F32)
        o_ref[:, m] = jnp.where(row == USED - 8, w[m : m + 1][None], block).astype(BF16)


def mix_kernel(v0_ref, v1_ref, o_ref, vs, ms):
    vs[0] = v0_ref[:, HEAD:].astype(F32).reshape(TOTAL * 8, LAT)
    vs[1] = v1_ref[...].astype(F32).reshape(TOTAL * 8, LAT)
    rows = [vs[r // 8, pl.ds(r % 8, TOTAL, stride=8), :].astype(BF16) for r in range(ROWS)]
    w = rows[USED][:, :TOTAL]
    v = jnp.concatenate(rows[:USED], axis=1)
    mixed = jnp.dot(w, v, preferred_element_type=F32)
    for r in range(USED):
        ms[pl.ds(r, TOTAL, stride=ROWS), :] = mixed[:, r * LAT : (r + 1) * LAT]
    ms[pl.ds(USED, TOTAL, stride=ROWS), :] = jnp.zeros((TOTAL, LAT), F32)
    o_ref[...] = ms[...].astype(BF16).reshape(o_ref.shape)


def finish_kernel(x_ref, f_ref, w_ref, o_ref, mc, sh, br, ob, sem):
    copies = [pltpu.make_async_copy(ob.at[m], o_ref.at[m], sem.at[m]) for m in range(OWN)]
    for m in range(OWN):
        for j in range(MEM):
            mc[j * USED : j * USED + ROWS] = x_ref[j, m].astype(F32)
        whole = mc[0 : EXT * CQ]
        before, after = lat_shifts(whole)
        for b, x in enumerate((before, whole, after)):
            sh[b] = x.astype(BF16)
        for i in range(0, COLS, 4):
            patches = [
                jnp.concatenate([sh[b, p * CQ : (p + 4) * CQ] for b in range(3)], axis=0)
                for p in (i, i + 2)
            ]
            r = jnp.dot(w_ref[...], jnp.concatenate(patches, axis=1), preferred_element_type=F32)
            for n in range(4):
                rows, lanes = (n % 2) * CH, (n // 2) * LAT
                br[pl.ds(i + n, CH, stride=COLS), :] = r[rows : rows + CH, lanes : lanes + LAT]
        ob[m] = (f_ref[m].astype(F32) + br[...].reshape(CH, COLS, LAT)).astype(BF16)
        copies[m].start()
    for copy in copies:
        copy.wait()


def shards(fields, w_query, w_key, w_value, w_out):
    edge = jax.ShapeDtypeStruct((OWN, 2 * CH, LAT), BF16)
    plane = pltpu.VMEM((CH * COLS, LAT), F32)
    sib, nb = call(edges_kernel, (edge, edge), [plane], 0, 1_000_000, fields)
    swaps = [(i, (i - 1 if i % 2 == 0 else i + 1) % LON) for i in range(LON)]
    got_nb = lax.ppermute(nb, ("yhi", "x", "core"), swaps)
    got_sib = lax.all_gather(sib, "core", axis=0, tiled=False)
    qk_shape = jax.ShapeDtypeStruct((MEM, OWN, CQ, LAT), BF16)
    v0_shape = jax.ShapeDtypeStruct((MEM, HEAD + OWN * 8, LAT), BF16)
    v1_shape = jax.ShapeDtypeStruct((MEM, OWN, 8, LAT), BF16)
    ends = jax.ShapeDtypeStruct((OWN, 2 * ROWS, LAT), F32)
    pair = jax.ShapeDtypeStruct((18 * CQ, 4 * CH), BF16)
    pair_out = jax.ShapeDtypeStruct((2 * CH, 12 * CQ), BF16)
    qk, v0, v1, ends, w_pair, w_last = call(
        inner_kernel,
        (qk_shape, v0_shape, v1_shape, ends, pair, pair_out),
        [
            pltpu.VMEM((3 * CQ, 9 * CH), F32),
            plane,
            pltpu.VMEM((OWN, CH * COLS, LAT), BF16),
            pltpu.VMEM((OWN, 6 * CQ, LAT), F32),
        ],
        450_000_000,
        2_000_000,
        fields,
        w_query,
        w_key,
        w_value,
        w_out,
    )
    qk, v0, v1 = call(
        outer_kernel,
        (qk_shape, v0_shape, v1_shape),
        [pltpu.VMEM((OWN, 4 * CH, LAT), BF16)] * 2
        + [pltpu.VMEM((2 * CQ + ROWS, LAT), F32), pltpu.VMEM((2 * CQ + ROWS + 8, LAT), F32)],
        300_000_000,
        1_500_000,
        qk,
        v0,
        v1,
        ends,
        w_pair,
        sib,
        nb,
        got_sib,
        got_nb,
        alias={0: 0, 1: 1, 2: 2},
    )
    mem, lon = ("z", "ylo"), ("yhi", "x")
    qk = lax.all_to_all(qk, mem, 0, 0, tiled=True)
    v0 = call(
        gram_kernel,
        v0_shape,
        [
            pltpu.VMEM((TOTAL * CQ, LAT), F32),
            pltpu.VMEM((3, TOTAL, LAT), F32),
            pltpu.VMEM((2, 4 * MEM, LAT), F32),
        ],
        20_000_000,
        800_000,
        qk,
        v0,
        alias={1: 0},
    )
    v0 = lax.all_to_all(v0, mem, 0, 0, tiled=True)
    gram = call(total_kernel, jax.ShapeDtypeStruct((4, LAT), F32), [], 40_000, 200_000, v0)
    gram = lax.all_gather(gram, "core", axis=0, tiled=False)
    copies = jax.ShapeDtypeStruct((LON // 2, 4, LAT), F32)
    gram = call(spread_kernel, copies, [], 10_000, 40_000, gram)
    gram = lax.all_to_all(gram, lon, 0, 0, tiled=True)
    scale = 1.0 / math.sqrt(CQ * LAT * COLS * LON)
    v1 = call(
        functools.partial(softmax_kernel, scale),
        v1_shape,
        [pltpu.VMEM((8, LAT), F32)],
        40_000,
        400_000,
        gram,
        v1,
        alias={1: 0},
    )
    v1 = lax.all_to_all(v1, mem, 0, 0, tiled=True)
    mixed = call(
        mix_kernel,
        jax.ShapeDtypeStruct((MEM, OWN, ROWS, LAT), BF16),
        [pltpu.VMEM((2, TOTAL * 8, LAT), F32), pltpu.VMEM((TOTAL * ROWS, LAT), F32)],
        30_000_000,
        700_000,
        v0,
        v1,
    )
    mixed = lax.all_to_all(mixed, ("z", "ylo"), 0, 0, tiled=True)
    return call(
        finish_kernel,
        jax.ShapeDtypeStruct(fields.shape, BF16),
        [
            pltpu.VMEM((MEM * ROWS, LAT), F32),
            pltpu.VMEM((3, EXT * CQ, LAT), BF16),
            plane,
            pltpu.VMEM(fields.shape, BF16),
            pltpu.SemaphoreType.DMA((OWN,)),
        ],
        150_000_000,
        1_700_000,
        mixed,
        fields,
        w_last,
        far_out=True,
    )


def solution(mesh):
    fine = Mesh(mesh.devices.reshape(MEM // 2, 2, LON // 8, 4, 2), ("z", "ylo", "yhi", "x", "core"))
    spec = P(("z", "ylo"), None, ("yhi", "x", "core"), None)
    return jax.shard_map(
        shards,
        mesh=fine,
        in_specs=(spec, P(), P(), P(), P()),
        out_specs=spec,
        check_vma=False,
    )
```

```python
import functools
import math

import jax
import jax.numpy as jnp
from jax import lax
from jax.experimental import pallas as pl
from jax.experimental.pallas import tpu as pltpu
from jax.sharding import Mesh
from jax.sharding import PartitionSpec as P

CH, CQ, LAT = 64, 24, 128
HALF = CQ // 2
MEM, LON = 16, 32
OWN = 5
TOTAL = MEM * OWN
CUT = LAT - TOTAL
COLS = 8
EXT = COLS + 2
ROWS = 16
USED = EXT * CQ // MEM
HEAD = 8
F32, BF16 = jnp.float32, jnp.bfloat16
VMEM = pl.BlockSpec(memory_space=pltpu.VMEM)


HBM = pl.BlockSpec(memory_space=pl.ANY)


def call(body, outs, scratch, flops, nbytes, *args, alias=None, far_out=False):
    many = isinstance(outs, tuple)
    one = HBM if far_out else VMEM
    return pl.pallas_call(
        body,
        out_shape=outs,
        in_specs=[VMEM] * len(args),
        out_specs=(one,) * len(outs) if many else one,
        scratch_shapes=scratch,
        input_output_aliases=alias or {},
        compiler_params=pltpu.CompilerParams(vmem_limit_bytes=32 * 1024 * 1024),
        cost_estimate=pl.CostEstimate(flops=flops, bytes_accessed=nbytes, transcendentals=0),
    )(*args)


def lat_shifts(x):
    lane = lax.broadcasted_iota(jnp.int32, x.shape, 1)
    before = jnp.where(lane == 0, 0.0, pltpu.roll(x, 1, 1))
    after = jnp.where(lane == LAT - 1, 0.0, pltpu.roll(x, LAT - 1, 1))
    return before, after


def edges_kernel(f_ref, sib_ref, nb_ref, xf):
    even = lax.axis_index("core") == 0
    for m in range(OWN):
        xf[...] = f_ref[m].astype(F32).reshape(CH * COLS, LAT)
        for s in range(2):
            left = xf[pl.ds(s, CH, stride=COLS), :]
            right = xf[pl.ds(COLS - 2 + s, CH, stride=COLS), :]
            sib_ref[m, s * CH : (s + 1) * CH] = jnp.where(even, right, left).astype(BF16)
            nb_ref[m, s * CH : (s + 1) * CH] = jnp.where(even, left, right).astype(BF16)


def conv_pairs(w, xs):
    width = 3 * CQ
    lane = lax.broadcasted_iota(jnp.int32, (width, LAT), 1)
    wide = jnp.dot(w, jnp.concatenate(xs, axis=1), preferred_element_type=F32)
    pairs = []
    for n in range(len(xs)):
        r = wide[:, n * LAT : (n + 1) * LAT]
        outs = []
        for s in range(2):
            y = [r[(3 * s + b) * width : (3 * s + b + 1) * width] for b in range(3)]
            outs.append(
                y[1]
                + jnp.where(lane == 0, 0.0, pltpu.roll(y[0], 1, 1))
                + jnp.where(lane == LAT - 1, 0.0, pltpu.roll(y[2], LAT - 1, 1))
            )
        pairs.append(outs)
    return pairs


def put_block(v0_ref, v1_ref, j, m, block):
    v0_ref[j, HEAD + m * 8 : HEAD + m * 8 + 8] = block[:8].astype(BF16)
    v1_ref[j, m] = block[8:].astype(BF16)


def put_pair(qk_ref, vs, m, p, outs):
    for s in range(2):
        col = 2 * p + s
        vs[s * CQ : (s + 1) * CQ] = outs[s][2 * CQ :]
        if 1 <= col <= COLS:
            for h in range(2):
                qk_ref[2 * (col - 1) + h, m] = outs[s][h * CQ : (h + 1) * CQ].astype(BF16)


def inner_kernel(
    f_ref, wq_ref, wk_ref, wv_ref, wo_ref,
    qk_ref, v0_ref, v1_ref, e_ref, wp_ref, wf_ref, xt, ws, xf, vs,
):
    ws[0:HALF] = wq_ref[...].astype(F32)[:HALF]
    ws[HALF : 2 * HALF] = wk_ref[...].astype(F32)[:HALF]
    ws[2 * HALF : 3 * HALF] = wq_ref[...].astype(F32)[HALF:]
    ws[3 * HALF : 4 * HALF] = wk_ref[...].astype(F32)[HALF:]
    ws[2 * CQ :] = wv_ref[...].astype(F32)
    zero = jnp.zeros((3 * CQ, CH), F32)
    for b in range(3):
        taps = [ws[:, (3 * a + b) * CH : (3 * a + b + 1) * CH] for a in range(3)]
        for s in range(2):
            row = (3 * s + b) * 3 * CQ
            full = [zero] + taps if s else taps + [zero]
            wp_ref[row : row + 3 * CQ] = jnp.concatenate(full, axis=1).astype(BF16)
    wo = wo_ref[...].astype(F32)
    zero = jnp.zeros((CH, CQ), F32)
    row = lax.broadcasted_iota(jnp.int32, (CH, 2 * CH), 0)
    lane = lax.broadcasted_iota(jnp.int32, (CH, 2 * CH), 1)
    for s in range(2):
        full = []
        for b in range(3):
            taps = [wo[:, (3 * a + b) * CQ : (3 * a + b + 1) * CQ] for a in range(3)]
            full += [zero] + taps if s else taps + [zero]
        full.append(jnp.where(lane == row + s * CH, 1.0, 0.0))
        wf_ref[s * CH : (s + 1) * CH] = jnp.concatenate(full, axis=1).astype(BF16)
    for m in range(OWN):
        xf[...] = f_ref[m].astype(F32).reshape(CH * COLS, LAT)
        for i in range(COLS):
            xt[m, i * CH : (i + 1) * CH] = xf[pl.ds(i, CH, stride=COLS), :].astype(BF16)
    units = [(m, p) for m in range(OWN) for p in range(1, EXT // 2 - 1)]
    for n in range(0, len(units), 2):
        two = units[n : n + 2]
        xs = [xt[m, 2 * (p - 1) * CH : 2 * (p + 1) * CH] for m, p in two]
        for (m, p), outs in zip(two, conv_pairs(wp_ref[...], xs)):
            put_pair(qk_ref, vs.at[m, pl.ds((p - 1) * 2 * CQ, 2 * CQ)], m, p, outs)
    for m in range(OWN):
        for j in range(4, 12):
            row = j * USED - 2 * CQ
            put_block(v0_ref, v1_ref, j, m, vs[m, row : row + ROWS])
        e_ref[m, 0:ROWS] = vs[m, 0:ROWS]
        e_ref[m, ROWS:] = vs[m, 6 * CQ - ROWS :]


def outer_kernel(
    iq_ref, i0_ref, i1_ref, e_ref, wp_ref, sib_ref, nb_ref, gs_ref, gn_ref,
    qk_ref, v0_ref, v1_ref, xl, xr, vl, vr
):
    core = lax.axis_index("core")
    near = 2 * CH

    @pl.when(core == 0)
    def _():
        xl[:, :near] = gn_ref[...]
        xl[:, near:] = nb_ref[...]
        xr[:, :near] = sib_ref[...]
        xr[:, near:] = gs_ref[1]

    @pl.when(core == 1)
    def _():
        xl[:, :near] = gs_ref[0]
        xl[:, near:] = sib_ref[...]
        xr[:, :near] = nb_ref[...]
        xr[:, near:] = gn_ref[...]

    for m in range(OWN):
        left, right = conv_pairs(wp_ref[...], [xl[m], xr[m]])
        put_pair(qk_ref, vl.at[pl.ds(0, 2 * CQ)], m, 0, left)
        put_pair(qk_ref, vr.at[pl.ds(ROWS, 2 * CQ)], m, EXT // 2 - 1, right)
        vl[2 * CQ :] = e_ref[m, 0:ROWS]
        vr[0:ROWS] = e_ref[m, ROWS:]
        vr[ROWS + 2 * CQ :] = jnp.zeros((8, LAT), F32)
        for j in range(4):
            put_block(v0_ref, v1_ref, j, m, vl[j * USED : j * USED + ROWS])
            row = (12 + j) * USED - (8 * CQ - ROWS)
            put_block(v0_ref, v1_ref, 12 + j, m, vr[row : row + ROWS])


def gram_kernel(x_ref, v0_ref, o_ref, xs, gs, ps):
    xs[...] = x_ref[...].astype(F32).reshape(TOTAL * CQ, LAT)
    pad = jnp.zeros((LAT - TOTAL, LAT), BF16)
    q, k = [], []
    for r in range(HALF):
        q.append(xs[pl.ds(r, TOTAL, stride=CQ), :].astype(BF16))
        k.append(jnp.concatenate([xs[pl.ds(HALF + r, TOTAL, stride=CQ), :].astype(BF16), pad], axis=0))
    gram = lax.dot_general(
        jnp.concatenate(q, axis=1),
        jnp.concatenate(k, axis=1),
        (((1,), (1,)), ((), ())),
        preferred_element_type=F32,
    )
    lane = lax.broadcasted_iota(jnp.int32, gram.shape, 1)
    gs[0] = gram
    gs[1] = jnp.where(lane < TOTAL, 0.0, pltpu.roll(gram, TOTAL, 1))
    gs[2] = jnp.where(lane < TOTAL, 0.0, pltpu.roll(gram, TOTAL - CUT, 1))
    rest = jnp.zeros((2, LAT), F32)
    for s in range(MEM):
        row = s * OWN
        free = [gs[1 + h, row + 4 : row + 5, :] for h in range(2)]
        ps[0, 4 * s : 4 * s + 4] = gs[0, row : row + 4, :] + jnp.concatenate(free + [rest], axis=0)
    whole = ps[0]
    high = whole.astype(BF16).astype(F32)
    ps[0] = high
    ps[1] = whole - high
    for s in range(MEM):
        parts = [ps[part, 4 * s : 4 * s + 4] for part in range(2)]
        o_ref[s, 0:HEAD] = jnp.concatenate(parts, axis=0).astype(BF16)


def total_kernel(x_ref, o_ref):
    parts = jnp.sum(x_ref[:, 0:HEAD].astype(F32), axis=0)
    o_ref[...] = parts[0:4] + parts[4:8]


def spread_kernel(x_ref, o_ref):
    o_ref[...] = jnp.broadcast_to((x_ref[0] + x_ref[1])[None], o_ref.shape)


def softmax_kernel(scale, x_ref, v1_ref, o_ref, gs):
    gs[...] = jnp.zeros(gs.shape, F32)
    gs[0:4] = jnp.sum(x_ref[...], axis=0)
    gram = gs[...]
    head, tail = pltpu.roll(gram, LAT - TOTAL, 1), pltpu.roll(gram, LAT - TOTAL + CUT, 1)
    lane = lax.broadcasted_iota(jnp.int32, gram.shape, 1)
    gs[4:5] = jnp.where(lane[0:1] < CUT, head[0:1], tail[1:2])
    s = jnp.where(lane < TOTAL, gs[...] * scale, -jnp.inf)
    e = jnp.exp(s - jnp.max(s, axis=1, keepdims=True))
    w = e / jnp.sum(e, axis=1, keepdims=True)
    row = lax.broadcasted_iota(jnp.int32, (MEM, 8, LAT), 1)
    for m in range(OWN):
        block = v1_ref[:, m].astype(F32)
        o_ref[:, m] = jnp.where(row == USED - 8, w[m : m + 1][None], block).astype(BF16)


def mix_kernel(v0_ref, v1_ref, o_ref, vs, ms):
    vs[0] = v0_ref[:, HEAD:].astype(F32).reshape(TOTAL * 8, LAT)
    vs[1] = v1_ref[...].astype(F32).reshape(TOTAL * 8, LAT)
    rows = [vs[r // 8, pl.ds(r % 8, TOTAL, stride=8), :].astype(BF16) for r in range(ROWS)]
    w = rows[USED][:, :TOTAL]
    v = jnp.concatenate(rows[:USED], axis=1)
    mixed = jnp.dot(w, v, preferred_element_type=F32)
    for r in range(USED):
        ms[pl.ds(r, TOTAL, stride=ROWS), :] = mixed[:, r * LAT : (r + 1) * LAT]
    ms[pl.ds(USED, TOTAL, stride=ROWS), :] = jnp.zeros((TOTAL, LAT), F32)
    o_ref[...] = ms[...].astype(BF16).reshape(o_ref.shape)


def finish_kernel(x_ref, xt_ref, w_ref, o_ref, mc, sh, br, ob, sem):
    copies = [pltpu.make_async_copy(ob.at[m], o_ref.at[m], sem.at[m]) for m in range(OWN)]
    for m in range(OWN):
        for j in range(MEM):
            mc[j * USED : j * USED + ROWS] = x_ref[j, m].astype(F32)
        whole = mc[0 : EXT * CQ]
        before, after = lat_shifts(whole)
        for b, x in enumerate((before, whole, after)):
            sh[b] = x.astype(BF16)
        for i in range(0, COLS, 4):
            patches = []
            for p in (i, i + 2):
                parts = [sh[b, p * CQ : (p + 4) * CQ] for b in range(3)]
                parts.append(xt_ref[m, p * CH : (p + 2) * CH])
                patches.append(jnp.concatenate(parts, axis=0))
            r = jnp.dot(w_ref[...], jnp.concatenate(patches, axis=1), preferred_element_type=F32)
            for n in range(4):
                rows, lanes = (n % 2) * CH, (n // 2) * LAT
                br[pl.ds(i + n, CH, stride=COLS), :] = r[rows : rows + CH, lanes : lanes + LAT]
        ob[m] = br[...].reshape(CH, COLS, LAT).astype(BF16)
        copies[m].start()
    for copy in copies:
        copy.wait()


def shards(fields, w_query, w_key, w_value, w_out):
    edge = jax.ShapeDtypeStruct((OWN, 2 * CH, LAT), BF16)
    plane = pltpu.VMEM((CH * COLS, LAT), F32)
    sib, nb = call(edges_kernel, (edge, edge), [plane], 0, 1_000_000, fields)
    swaps = [(i, (i - 1 if i % 2 == 0 else i + 1) % LON) for i in range(LON)]
    got_nb = lax.ppermute(nb, ("yhi", "x", "core"), swaps)
    got_sib = lax.all_gather(sib, "core", axis=0, tiled=False)
    qk_shape = jax.ShapeDtypeStruct((MEM, OWN, CQ, LAT), BF16)
    v0_shape = jax.ShapeDtypeStruct((MEM, HEAD + OWN * 8, LAT), BF16)
    v1_shape = jax.ShapeDtypeStruct((MEM, OWN, 8, LAT), BF16)
    ends = jax.ShapeDtypeStruct((OWN, 2 * ROWS, LAT), F32)
    pair = jax.ShapeDtypeStruct((18 * CQ, 4 * CH), BF16)
    pair_out = jax.ShapeDtypeStruct((2 * CH, 12 * CQ + 2 * CH), BF16)
    turned = jax.ShapeDtypeStruct((OWN, CH * COLS, LAT), BF16)
    qk, v0, v1, ends, w_pair, w_last, turned = call(
        inner_kernel,
        (qk_shape, v0_shape, v1_shape, ends, pair, pair_out, turned),
        [
            pltpu.VMEM((3 * CQ, 9 * CH), F32),
            plane,
            pltpu.VMEM((OWN, 6 * CQ, LAT), F32),
        ],
        450_000_000,
        2_000_000,
        fields,
        w_query,
        w_key,
        w_value,
        w_out,
    )
    qk, v0, v1 = call(
        outer_kernel,
        (qk_shape, v0_shape, v1_shape),
        [pltpu.VMEM((OWN, 4 * CH, LAT), BF16)] * 2
        + [pltpu.VMEM((2 * CQ + ROWS, LAT), F32), pltpu.VMEM((2 * CQ + ROWS + 8, LAT), F32)],
        300_000_000,
        1_500_000,
        qk,
        v0,
        v1,
        ends,
        w_pair,
        sib,
        nb,
        got_sib,
        got_nb,
        alias={0: 0, 1: 1, 2: 2},
    )
    mem, lon = ("z", "ylo"), ("yhi", "x")
    qk = lax.all_to_all(qk, mem, 0, 0, tiled=True)
    v0 = call(
        gram_kernel,
        v0_shape,
        [
            pltpu.VMEM((TOTAL * CQ, LAT), F32),
            pltpu.VMEM((3, TOTAL, LAT), F32),
            pltpu.VMEM((2, 4 * MEM, LAT), F32),
        ],
        20_000_000,
        800_000,
        qk,
        v0,
        alias={1: 0},
    )
    v0 = lax.all_to_all(v0, mem, 0, 0, tiled=True)
    gram = call(total_kernel, jax.ShapeDtypeStruct((4, LAT), F32), [], 40_000, 200_000, v0)
    gram = lax.all_gather(gram, "core", axis=0, tiled=False)
    copies = jax.ShapeDtypeStruct((LON // 2, 4, LAT), F32)
    gram = call(spread_kernel, copies, [], 10_000, 40_000, gram)
    gram = lax.all_to_all(gram, lon, 0, 0, tiled=True)
    scale = 1.0 / math.sqrt(CQ * LAT * COLS * LON)
    v1 = call(
        functools.partial(softmax_kernel, scale),
        v1_shape,
        [pltpu.VMEM((8, LAT), F32)],
        40_000,
        400_000,
        gram,
        v1,
        alias={1: 0},
    )
    v1 = lax.all_to_all(v1, mem, 0, 0, tiled=True)
    mixed = call(
        mix_kernel,
        jax.ShapeDtypeStruct((MEM, OWN, ROWS, LAT), BF16),
        [pltpu.VMEM((2, TOTAL * 8, LAT), F32), pltpu.VMEM((TOTAL * ROWS, LAT), F32)],
        30_000_000,
        700_000,
        v0,
        v1,
    )
    mixed = lax.all_to_all(mixed, ("z", "ylo"), 0, 0, tiled=True)
    return call(
        finish_kernel,
        jax.ShapeDtypeStruct(fields.shape, BF16),
        [
            pltpu.VMEM((MEM * ROWS, LAT), F32),
            pltpu.VMEM((3, EXT * CQ, LAT), BF16),
            plane,
            pltpu.VMEM(fields.shape, BF16),
            pltpu.SemaphoreType.DMA((OWN,)),
        ],
        150_000_000,
        1_700_000,
        mixed,
        turned,
        w_last,
        far_out=True,
    )


def solution(mesh):
    fine = Mesh(mesh.devices.reshape(MEM // 2, 2, LON // 8, 4, 2), ("z", "ylo", "yhi", "x", "core"))
    spec = P(("z", "ylo"), None, ("yhi", "x", "core"), None)
    return jax.shard_map(
        shards,
        mesh=fine,
        in_specs=(spec, P(), P(), P(), P()),
        out_specs=spec,
        check_vma=False,
    )
```

```python
import functools
import math

import jax
import jax.numpy as jnp
from jax import lax
from jax.experimental import pallas as pl
from jax.experimental.pallas import tpu as pltpu
from jax.sharding import Mesh
from jax.sharding import PartitionSpec as P

CH, CQ, LAT = 64, 24, 128
HALF = CQ // 2
MEM, LON = 16, 32
OWN = 5
TOTAL = MEM * OWN
CUT = LAT - TOTAL
COLS = 8
EXT = COLS + 2
ROWS = 16
USED = EXT * CQ // MEM
F32, BF16 = jnp.float32, jnp.bfloat16
VMEM = pl.BlockSpec(memory_space=pltpu.VMEM)


HBM = pl.BlockSpec(memory_space=pl.ANY)


def call(body, outs, scratch, flops, nbytes, *args, alias=None, far_out=False):
    many = isinstance(outs, tuple)
    one = HBM if far_out else VMEM
    return pl.pallas_call(
        body,
        out_shape=outs,
        in_specs=[VMEM] * len(args),
        out_specs=(one,) * len(outs) if many else one,
        scratch_shapes=scratch,
        input_output_aliases=alias or {},
        compiler_params=pltpu.CompilerParams(vmem_limit_bytes=32 * 1024 * 1024),
        cost_estimate=pl.CostEstimate(flops=flops, bytes_accessed=nbytes, transcendentals=0),
    )(*args)


def lat_shifts(x):
    lane = lax.broadcasted_iota(jnp.int32, x.shape, 1)
    before = jnp.where(lane == 0, 0.0, pltpu.roll(x, 1, 1))
    after = jnp.where(lane == LAT - 1, 0.0, pltpu.roll(x, LAT - 1, 1))
    return before, after


def edges_kernel(f_ref, sib_ref, nb_ref, xf):
    even = lax.axis_index("core") == 0
    for m in range(OWN):
        xf[...] = f_ref[m].astype(F32).reshape(CH * COLS, LAT)
        for s in range(2):
            left = xf[pl.ds(s, CH, stride=COLS), :]
            right = xf[pl.ds(COLS - 2 + s, CH, stride=COLS), :]
            sib_ref[m, s * CH : (s + 1) * CH] = jnp.where(even, right, left).astype(BF16)
            nb_ref[m, s * CH : (s + 1) * CH] = jnp.where(even, left, right).astype(BF16)


def conv_pairs(w, xs):
    width = 3 * CQ
    lane = lax.broadcasted_iota(jnp.int32, (width, LAT), 1)
    wide = jnp.dot(w, jnp.concatenate(xs, axis=1), preferred_element_type=F32)
    pairs = []
    for n in range(len(xs)):
        r = wide[:, n * LAT : (n + 1) * LAT]
        outs = []
        for s in range(2):
            y = [r[(3 * s + b) * width : (3 * s + b + 1) * width] for b in range(3)]
            outs.append(
                y[1]
                + jnp.where(lane == 0, 0.0, pltpu.roll(y[0], 1, 1))
                + jnp.where(lane == LAT - 1, 0.0, pltpu.roll(y[2], LAT - 1, 1))
            )
        pairs.append(outs)
    return pairs


def put_pair(qk_ref, vs, m, p, outs):
    for s in range(2):
        col = 2 * p + s
        vs[s * CQ : (s + 1) * CQ] = outs[s][2 * CQ :]
        if 1 <= col <= COLS:
            for h in range(2):
                qk_ref[2 * (col - 1) + h, m] = outs[s][h * CQ : (h + 1) * CQ].astype(BF16)


def inner_kernel(
    f_ref, wq_ref, wk_ref, wv_ref, wo_ref,
    qk_ref, v_ref, e_ref, wp_ref, wf_ref, xt, ws, xf, vs,
):
    ws[0:HALF] = wq_ref[...].astype(F32)[:HALF]
    ws[HALF : 2 * HALF] = wk_ref[...].astype(F32)[:HALF]
    ws[2 * HALF : 3 * HALF] = wq_ref[...].astype(F32)[HALF:]
    ws[3 * HALF : 4 * HALF] = wk_ref[...].astype(F32)[HALF:]
    ws[2 * CQ :] = wv_ref[...].astype(F32)
    zero = jnp.zeros((3 * CQ, CH), F32)
    for b in range(3):
        taps = [ws[:, (3 * a + b) * CH : (3 * a + b + 1) * CH] for a in range(3)]
        for s in range(2):
            row = (3 * s + b) * 3 * CQ
            full = [zero] + taps if s else taps + [zero]
            wp_ref[row : row + 3 * CQ] = jnp.concatenate(full, axis=1).astype(BF16)
    wo = wo_ref[...].astype(F32)
    zero = jnp.zeros((CH, CQ), F32)
    row = lax.broadcasted_iota(jnp.int32, (CH, 2 * CH), 0)
    lane = lax.broadcasted_iota(jnp.int32, (CH, 2 * CH), 1)
    for s in range(2):
        full = []
        for b in range(3):
            taps = [wo[:, (3 * a + b) * CQ : (3 * a + b + 1) * CQ] for a in range(3)]
            full += [zero] + taps if s else taps + [zero]
        full.append(jnp.where(lane == row + s * CH, 1.0, 0.0))
        wf_ref[s * CH : (s + 1) * CH] = jnp.concatenate(full, axis=1).astype(BF16)
    for m in range(OWN):
        xf[...] = f_ref[m].astype(F32).reshape(CH * COLS, LAT)
        for i in range(COLS):
            xt[m, i * CH : (i + 1) * CH] = xf[pl.ds(i, CH, stride=COLS), :].astype(BF16)
    units = [(m, p) for m in range(OWN) for p in range(1, EXT // 2 - 1)]
    for n in range(0, len(units), 2):
        two = units[n : n + 2]
        xs = [xt[m, 2 * (p - 1) * CH : 2 * (p + 1) * CH] for m, p in two]
        for (m, p), outs in zip(two, conv_pairs(wp_ref[...], xs)):
            put_pair(qk_ref, vs.at[m, pl.ds((p - 1) * 2 * CQ, 2 * CQ)], m, p, outs)
    for m in range(OWN):
        for j in range(4, 12):
            row = j * USED - 2 * CQ
            v_ref[j, m] = vs[m, row : row + ROWS].astype(BF16)
        e_ref[m, 0:ROWS] = vs[m, 0:ROWS]
        e_ref[m, ROWS:] = vs[m, 6 * CQ - ROWS :]


def outer_kernel(
    iq_ref, iv_ref, e_ref, wp_ref, sib_ref, nb_ref, gs_ref, gn_ref,
    qk_ref, v_ref, xl, xr, vl, vr
):
    core = lax.axis_index("core")
    near = 2 * CH

    @pl.when(core == 0)
    def _():
        xl[:, :near] = gn_ref[...]
        xl[:, near:] = nb_ref[...]
        xr[:, :near] = sib_ref[...]
        xr[:, near:] = gs_ref[1]

    @pl.when(core == 1)
    def _():
        xl[:, :near] = gs_ref[0]
        xl[:, near:] = sib_ref[...]
        xr[:, :near] = nb_ref[...]
        xr[:, near:] = gn_ref[...]

    for m in range(OWN):
        left, right = conv_pairs(wp_ref[...], [xl[m], xr[m]])
        put_pair(qk_ref, vl.at[pl.ds(0, 2 * CQ)], m, 0, left)
        put_pair(qk_ref, vr.at[pl.ds(ROWS, 2 * CQ)], m, EXT // 2 - 1, right)
        vl[2 * CQ :] = e_ref[m, 0:ROWS]
        vr[0:ROWS] = e_ref[m, ROWS:]
        vr[ROWS + 2 * CQ :] = jnp.zeros((8, LAT), F32)
        for j in range(4):
            v_ref[j, m] = vl[j * USED : j * USED + ROWS].astype(BF16)
            row = (12 + j) * USED - (8 * CQ - ROWS)
            v_ref[12 + j, m] = vr[row : row + ROWS].astype(BF16)


def gram_kernel(x_ref, g_ref, xs, gs):
    xs[...] = x_ref[...].astype(F32).reshape(TOTAL * CQ, LAT)
    pad = jnp.zeros((LAT - TOTAL, LAT), BF16)
    q, k = [], []
    for r in range(HALF):
        q.append(xs[pl.ds(r, TOTAL, stride=CQ), :].astype(BF16))
        k.append(jnp.concatenate([xs[pl.ds(HALF + r, TOTAL, stride=CQ), :].astype(BF16), pad], axis=0))
    gram = lax.dot_general(
        jnp.concatenate(q, axis=1),
        jnp.concatenate(k, axis=1),
        (((1,), (1,)), ((), ())),
        preferred_element_type=F32,
    )
    lane = lax.broadcasted_iota(jnp.int32, gram.shape, 1)
    gs[0] = gram
    gs[1] = jnp.where(lane < TOTAL, 0.0, pltpu.roll(gram, TOTAL, 1))
    gs[2] = jnp.where(lane < TOTAL, 0.0, pltpu.roll(gram, TOTAL - CUT, 1))
    rest = jnp.zeros((2, LAT), F32)
    for s in range(MEM):
        row = s * OWN
        free = [gs[1 + h, row + 4 : row + 5, :] for h in range(2)]
        g_ref[s] = gs[0, row : row + 4, :] + jnp.concatenate(free + [rest], axis=0)


def total_kernel(x_ref, o_ref):
    o_ref[...] = jnp.sum(x_ref[...], axis=0)


def spread_kernel(x_ref, o_ref):
    o_ref[...] = jnp.broadcast_to((x_ref[0] + x_ref[1])[None], o_ref.shape)


def softmax_kernel(scale, x_ref, v_ref, o_ref, gs):
    gs[...] = jnp.zeros(gs.shape, F32)
    gs[0:4] = jnp.sum(x_ref[...], axis=0)
    gram = gs[...]
    head, tail = pltpu.roll(gram, LAT - TOTAL, 1), pltpu.roll(gram, LAT - TOTAL + CUT, 1)
    lane = lax.broadcasted_iota(jnp.int32, gram.shape, 1)
    gs[4:5] = jnp.where(lane[0:1] < CUT, head[0:1], tail[1:2])
    s = jnp.where(lane < TOTAL, gs[...] * scale, -jnp.inf)
    e = jnp.exp(s - jnp.max(s, axis=1, keepdims=True))
    w = e / jnp.sum(e, axis=1, keepdims=True)
    row = lax.broadcasted_iota(jnp.int32, (MEM, ROWS, LAT), 1)
    for m in range(OWN):
        block = v_ref[:, m].astype(F32)
        o_ref[:, m] = jnp.where(row == USED, w[m : m + 1][None], block).astype(BF16)


def mix_kernel(x_ref, o_ref, vs, ms):
    vs[...] = x_ref[...].astype(F32).reshape(TOTAL * ROWS, LAT)
    w = vs[pl.ds(USED, TOTAL, stride=ROWS), :].astype(BF16)[:, :TOTAL]
    v = jnp.concatenate([vs[pl.ds(r, TOTAL, stride=ROWS), :].astype(BF16) for r in range(USED)], axis=1)
    mixed = jnp.dot(w, v, preferred_element_type=F32)
    for r in range(USED):
        ms[pl.ds(r, TOTAL, stride=ROWS), :] = mixed[:, r * LAT : (r + 1) * LAT]
    ms[pl.ds(USED, TOTAL, stride=ROWS), :] = jnp.zeros((TOTAL, LAT), F32)
    o_ref[...] = ms[...].astype(BF16).reshape(o_ref.shape)


def finish_kernel(x_ref, xt_ref, w_ref, o_ref, mc, sh, br, ob, sem):
    copies = [pltpu.make_async_copy(ob.at[m], o_ref.at[m], sem.at[m]) for m in range(OWN)]
    for m in range(OWN):
        for j in range(MEM):
            mc[j * USED : j * USED + ROWS] = x_ref[j, m].astype(F32)
        whole = mc[0 : EXT * CQ]
        before, after = lat_shifts(whole)
        for b, x in enumerate((before, whole, after)):
            sh[b] = x.astype(BF16)
        for i in range(0, COLS, 4):
            patches = []
            for p in (i, i + 2):
                parts = [sh[b, p * CQ : (p + 4) * CQ] for b in range(3)]
                parts.append(xt_ref[m, p * CH : (p + 2) * CH])
                patches.append(jnp.concatenate(parts, axis=0))
            r = jnp.dot(w_ref[...], jnp.concatenate(patches, axis=1), preferred_element_type=F32)
            for n in range(4):
                rows, lanes = (n % 2) * CH, (n // 2) * LAT
                br[pl.ds(i + n, CH, stride=COLS), :] = r[rows : rows + CH, lanes : lanes + LAT]
        ob[m] = br[...].reshape(CH, COLS, LAT).astype(BF16)
        copies[m].start()
    for copy in copies:
        copy.wait()


def shards(fields, w_query, w_key, w_value, w_out):
    edge = jax.ShapeDtypeStruct((OWN, 2 * CH, LAT), BF16)
    plane = pltpu.VMEM((CH * COLS, LAT), F32)
    sib, nb = call(edges_kernel, (edge, edge), [plane], 0, 1_000_000, fields)
    swaps = [(i, (i - 1 if i % 2 == 0 else i + 1) % LON) for i in range(LON)]
    got_nb = lax.ppermute(nb, ("yhi", "x", "core"), swaps)
    got_sib = lax.all_gather(sib, "core", axis=0, tiled=False)
    qk_shape = jax.ShapeDtypeStruct((MEM, OWN, CQ, LAT), BF16)
    v_shape = jax.ShapeDtypeStruct((MEM, OWN, ROWS, LAT), BF16)
    ends = jax.ShapeDtypeStruct((OWN, 2 * ROWS, LAT), F32)
    pair = jax.ShapeDtypeStruct((18 * CQ, 4 * CH), BF16)
    pair_out = jax.ShapeDtypeStruct((2 * CH, 12 * CQ + 2 * CH), BF16)
    turned = jax.ShapeDtypeStruct((OWN, CH * COLS, LAT), BF16)
    qk, v, ends, w_pair, w_last, turned = call(
        inner_kernel,
        (qk_shape, v_shape, ends, pair, pair_out, turned),
        [
            pltpu.VMEM((3 * CQ, 9 * CH), F32),
            plane,
            pltpu.VMEM((OWN, 6 * CQ, LAT), F32),
        ],
        450_000_000,
        2_000_000,
        fields,
        w_query,
        w_key,
        w_value,
        w_out,
    )
    qk, v = call(
        outer_kernel,
        (qk_shape, v_shape),
        [pltpu.VMEM((OWN, 4 * CH, LAT), BF16)] * 2
        + [pltpu.VMEM((2 * CQ + ROWS, LAT), F32), pltpu.VMEM((2 * CQ + ROWS + 8, LAT), F32)],
        300_000_000,
        1_500_000,
        qk,
        v,
        ends,
        w_pair,
        sib,
        nb,
        got_sib,
        got_nb,
        alias={0: 0, 1: 1},
    )
    mem, lon = ("z", "ylo"), ("yhi", "x")
    qk = lax.all_to_all(qk, mem, 0, 0, tiled=True)
    gram = call(
        gram_kernel,
        jax.ShapeDtypeStruct((MEM, 4, LAT), F32),
        [pltpu.VMEM((TOTAL * CQ, LAT), F32), pltpu.VMEM((3, TOTAL, LAT), F32)],
        20_000_000,
        600_000,
        qk,
    )
    gram = lax.all_to_all(gram, mem, 0, 0, tiled=True)
    gram = call(total_kernel, jax.ShapeDtypeStruct((4, LAT), F32), [], 10_000, 40_000, gram)
    gram = lax.all_gather(gram, "core", axis=0, tiled=False)
    copies = jax.ShapeDtypeStruct((LON // 2, 4, LAT), F32)
    gram = call(spread_kernel, copies, [], 10_000, 40_000, gram)
    gram = lax.all_to_all(gram, lon, 0, 0, tiled=True)
    scale = 1.0 / math.sqrt(CQ * LAT * COLS * LON)
    v = call(
        functools.partial(softmax_kernel, scale),
        v_shape,
        [pltpu.VMEM((8, LAT), F32)],
        40_000,
        700_000,
        gram,
        v,
        alias={1: 0},
    )
    v = lax.all_to_all(v, mem, 0, 0, tiled=True)
    mixed = call(
        mix_kernel,
        v_shape,
        [pltpu.VMEM((TOTAL * ROWS, LAT), F32)] * 2,
        30_000_000,
        700_000,
        v,
    )
    mixed = lax.all_to_all(mixed, ("z", "ylo"), 0, 0, tiled=True)
    return call(
        finish_kernel,
        jax.ShapeDtypeStruct(fields.shape, BF16),
        [
            pltpu.VMEM((MEM * ROWS, LAT), F32),
            pltpu.VMEM((3, EXT * CQ, LAT), BF16),
            plane,
            pltpu.VMEM(fields.shape, BF16),
            pltpu.SemaphoreType.DMA((OWN,)),
        ],
        150_000_000,
        1_700_000,
        mixed,
        turned,
        w_last,
        far_out=True,
    )


def solution(mesh):
    fine = Mesh(mesh.devices.reshape(MEM // 2, 2, LON // 8, 4, 2), ("z", "ylo", "yhi", "x", "core"))
    spec = P(("z", "ylo"), None, ("yhi", "x", "core"), None)
    return jax.shard_map(
        shards,
        mesh=fine,
        in_specs=(spec, P(), P(), P(), P()),
        out_specs=spec,
        check_vma=False,
    )
```

```python
import functools
import math

import jax
import jax.numpy as jnp
from jax import lax
from jax.experimental import pallas as pl
from jax.experimental.pallas import tpu as pltpu
from jax.sharding import Mesh
from jax.sharding import PartitionSpec as P

CH, CQ, LAT = 64, 24, 128
HALF = CQ // 2
MEM, LON = 16, 32
OWN = 5
TOTAL = MEM * OWN
CUT = LAT - TOTAL
COLS = 8
EXT = COLS + 2
ROWS = 16
USED = EXT * CQ // MEM
HEAD = 8
F32, BF16 = jnp.float32, jnp.bfloat16
VMEM = pl.BlockSpec(memory_space=pltpu.VMEM)


HBM = pl.BlockSpec(memory_space=pl.ANY)


def call(body, outs, scratch, flops, nbytes, *args, alias=None, far_out=False):
    many = isinstance(outs, tuple)
    one = HBM if far_out else VMEM
    return pl.pallas_call(
        body,
        out_shape=outs,
        in_specs=[VMEM] * len(args),
        out_specs=(one,) * len(outs) if many else one,
        scratch_shapes=scratch,
        input_output_aliases=alias or {},
        compiler_params=pltpu.CompilerParams(vmem_limit_bytes=32 * 1024 * 1024),
        cost_estimate=pl.CostEstimate(flops=flops, bytes_accessed=nbytes, transcendentals=0),
    )(*args)


def lat_shifts(x):
    lane = lax.broadcasted_iota(jnp.int32, x.shape, 1)
    before = jnp.where(lane == 0, 0.0, pltpu.roll(x, 1, 1))
    after = jnp.where(lane == LAT - 1, 0.0, pltpu.roll(x, LAT - 1, 1))
    return before, after


def edges_kernel(f_ref, sib_ref, nb_ref, xf):
    even = lax.axis_index("core") == 0
    for m in range(OWN):
        xf[...] = f_ref[m].astype(F32).reshape(CH * COLS, LAT)
        for s in range(2):
            left = xf[pl.ds(s, CH, stride=COLS), :]
            right = xf[pl.ds(COLS - 2 + s, CH, stride=COLS), :]
            sib_ref[m, s * CH : (s + 1) * CH] = jnp.where(even, right, left).astype(BF16)
            nb_ref[m, s * CH : (s + 1) * CH] = jnp.where(even, left, right).astype(BF16)


def conv_pairs(w, xs):
    width = 3 * CQ
    lane = lax.broadcasted_iota(jnp.int32, (width, LAT), 1)
    wide = jnp.dot(w, jnp.concatenate(xs, axis=1), preferred_element_type=F32)
    pairs = []
    for n in range(len(xs)):
        r = wide[:, n * LAT : (n + 1) * LAT]
        outs = []
        for s in range(2):
            y = [r[(3 * s + b) * width : (3 * s + b + 1) * width] for b in range(3)]
            outs.append(
                y[1]
                + jnp.where(lane == 0, 0.0, pltpu.roll(y[0], 1, 1))
                + jnp.where(lane == LAT - 1, 0.0, pltpu.roll(y[2], LAT - 1, 1))
            )
        pairs.append(outs)
    return pairs


def put_block(v0_ref, v1_ref, j, m, block):
    v0_ref[j, HEAD + m * 8 : HEAD + m * 8 + 8] = block[:8].astype(BF16)
    v1_ref[j, m] = block[8:].astype(BF16)


def put_pair(qk_ref, vs, m, p, outs):
    for s in range(2):
        col = 2 * p + s
        vs[s * CQ : (s + 1) * CQ] = outs[s][2 * CQ :]
        if 1 <= col <= COLS:
            for h in range(2):
                qk_ref[2 * (col - 1) + h, m] = outs[s][h * CQ : (h + 1) * CQ].astype(BF16)


def inner_kernel(
    f_ref, wq_ref, wk_ref, wv_ref, wo_ref,
    qk_ref, v0_ref, v1_ref, e_ref, wp_ref, wf_ref, xt, ws, xf, vs,
):
    ws[0:HALF] = wq_ref[...].astype(F32)[:HALF]
    ws[HALF : 2 * HALF] = wk_ref[...].astype(F32)[:HALF]
    ws[2 * HALF : 3 * HALF] = wq_ref[...].astype(F32)[HALF:]
    ws[3 * HALF : 4 * HALF] = wk_ref[...].astype(F32)[HALF:]
    ws[2 * CQ :] = wv_ref[...].astype(F32)
    zero = jnp.zeros((3 * CQ, CH), F32)
    for b in range(3):
        taps = [ws[:, (3 * a + b) * CH : (3 * a + b + 1) * CH] for a in range(3)]
        for s in range(2):
            row = (3 * s + b) * 3 * CQ
            full = [zero] + taps if s else taps + [zero]
            wp_ref[row : row + 3 * CQ] = jnp.concatenate(full, axis=1).astype(BF16)
    wo = wo_ref[...].astype(F32)
    zero = jnp.zeros((CH, CQ), F32)
    row = lax.broadcasted_iota(jnp.int32, (CH, 2 * CH), 0)
    lane = lax.broadcasted_iota(jnp.int32, (CH, 2 * CH), 1)
    for s in range(2):
        full = []
        for b in range(3):
            taps = [wo[:, (3 * a + b) * CQ : (3 * a + b + 1) * CQ] for a in range(3)]
            full += [zero] + taps if s else taps + [zero]
        full.append(jnp.where(lane == row + s * CH, 1.0, 0.0))
        wf_ref[s * CH : (s + 1) * CH] = jnp.concatenate(full, axis=1).astype(BF16)
    for m in range(OWN):
        xf[...] = f_ref[m].astype(F32).reshape(CH * COLS, LAT)
        for i in range(COLS):
            xt[m, i * CH : (i + 1) * CH] = xf[pl.ds(i, CH, stride=COLS), :].astype(BF16)
    units = [(m, p) for m in range(OWN) for p in range(1, EXT // 2 - 1)]
    for n in range(0, len(units), 2):
        two = units[n : n + 2]
        xs = [xt[m, 2 * (p - 1) * CH : 2 * (p + 1) * CH] for m, p in two]
        for (m, p), outs in zip(two, conv_pairs(wp_ref[...], xs)):
            put_pair(qk_ref, vs.at[m, pl.ds((p - 1) * 2 * CQ, 2 * CQ)], m, p, outs)
    for m in range(OWN):
        for j in range(4, 12):
            row = j * USED - 2 * CQ
            put_block(v0_ref, v1_ref, j, m, vs[m, row : row + ROWS])
        e_ref[m, 0:ROWS] = vs[m, 0:ROWS]
        e_ref[m, ROWS:] = vs[m, 6 * CQ - ROWS :]


def outer_kernel(
    iq_ref, i0_ref, i1_ref, e_ref, wp_ref, sib_ref, nb_ref, gs_ref, gn_ref,
    qk_ref, v0_ref, v1_ref, xl, xr, vl, vr
):
    core = lax.axis_index("core")
    near = 2 * CH

    @pl.when(core == 0)
    def _():
        xl[:, :near] = gn_ref[...]
        xl[:, near:] = nb_ref[...]
        xr[:, :near] = sib_ref[...]
        xr[:, near:] = gs_ref[1]

    @pl.when(core == 1)
    def _():
        xl[:, :near] = gs_ref[0]
        xl[:, near:] = sib_ref[...]
        xr[:, :near] = nb_ref[...]
        xr[:, near:] = gn_ref[...]

    for m in range(OWN):
        left, right = conv_pairs(wp_ref[...], [xl[m], xr[m]])
        put_pair(qk_ref, vl.at[pl.ds(0, 2 * CQ)], m, 0, left)
        put_pair(qk_ref, vr.at[pl.ds(ROWS, 2 * CQ)], m, EXT // 2 - 1, right)
        vl[2 * CQ :] = e_ref[m, 0:ROWS]
        vr[0:ROWS] = e_ref[m, ROWS:]
        vr[ROWS + 2 * CQ :] = jnp.zeros((8, LAT), F32)
        for j in range(4):
            put_block(v0_ref, v1_ref, j, m, vl[j * USED : j * USED + ROWS])
            row = (12 + j) * USED - (8 * CQ - ROWS)
            put_block(v0_ref, v1_ref, 12 + j, m, vr[row : row + ROWS])


def gram_kernel(x_ref, g_ref, xs, gs):
    xs[...] = x_ref[...].astype(F32).reshape(TOTAL * CQ, LAT)
    pad = jnp.zeros((LAT - TOTAL, LAT), BF16)
    q, k = [], []
    for r in range(HALF):
        q.append(xs[pl.ds(r, TOTAL, stride=CQ), :].astype(BF16))
        k.append(jnp.concatenate([xs[pl.ds(HALF + r, TOTAL, stride=CQ), :].astype(BF16), pad], axis=0))
    gram = lax.dot_general(
        jnp.concatenate(q, axis=1),
        jnp.concatenate(k, axis=1),
        (((1,), (1,)), ((), ())),
        preferred_element_type=F32,
    )
    lane = lax.broadcasted_iota(jnp.int32, gram.shape, 1)
    gs[0] = gram
    gs[1] = jnp.where(lane < TOTAL, 0.0, pltpu.roll(gram, TOTAL, 1))
    gs[2] = jnp.where(lane < TOTAL, 0.0, pltpu.roll(gram, TOTAL - CUT, 1))
    rest = jnp.zeros((2, LAT), F32)
    for s in range(MEM):
        row = s * OWN
        free = [gs[1 + h, row + 4 : row + 5, :] for h in range(2)]
        g_ref[4 * s : 4 * s + 4] = gs[0, row : row + 4, :] + jnp.concatenate(free + [rest], axis=0)


def header_kernel(g_ref, v0_ref, o_ref, ps):
    whole = g_ref[0] + g_ref[1]
    high = whole.astype(BF16).astype(F32)
    ps[0] = high
    ps[1] = whole - high
    for s in range(MEM):
        parts = [ps[part, 4 * s : 4 * s + 4] for part in range(2)]
        o_ref[s, 0:HEAD] = jnp.concatenate(parts, axis=0).astype(BF16)


def spread_kernel(x_ref, o_ref):
    parts = jnp.sum(x_ref[:, 0:HEAD].astype(F32), axis=0)
    o_ref[...] = jnp.broadcast_to((parts[0:4] + parts[4:8])[None], o_ref.shape)


def softmax_kernel(scale, x_ref, v1_ref, o_ref, gs):
    gs[...] = jnp.zeros(gs.shape, F32)
    gs[0:4] = jnp.sum(x_ref[...], axis=0)
    gram = gs[...]
    head, tail = pltpu.roll(gram, LAT - TOTAL, 1), pltpu.roll(gram, LAT - TOTAL + CUT, 1)
    lane = lax.broadcasted_iota(jnp.int32, gram.shape, 1)
    gs[4:5] = jnp.where(lane[0:1] < CUT, head[0:1], tail[1:2])
    s = jnp.where(lane < TOTAL, gs[...] * scale, -jnp.inf)
    e = jnp.exp(s - jnp.max(s, axis=1, keepdims=True))
    w = e / jnp.sum(e, axis=1, keepdims=True)
    row = lax.broadcasted_iota(jnp.int32, (MEM, 8, LAT), 1)
    for m in range(OWN):
        block = v1_ref[:, m].astype(F32)
        o_ref[:, m] = jnp.where(row == USED - 8, w[m : m + 1][None], block).astype(BF16)


def mix_kernel(v0_ref, v1_ref, o_ref, vs, ms):
    vs[0] = v0_ref[:, HEAD:].astype(F32).reshape(TOTAL * 8, LAT)
    vs[1] = v1_ref[...].astype(F32).reshape(TOTAL * 8, LAT)
    rows = [vs[r // 8, pl.ds(r % 8, TOTAL, stride=8), :].astype(BF16) for r in range(ROWS)]
    w = rows[USED][:, :TOTAL]
    v = jnp.concatenate(rows[:USED], axis=1)
    mixed = jnp.dot(w, v, preferred_element_type=F32)
    for r in range(USED):
        ms[pl.ds(r, TOTAL, stride=ROWS), :] = mixed[:, r * LAT : (r + 1) * LAT]
    ms[pl.ds(USED, TOTAL, stride=ROWS), :] = jnp.zeros((TOTAL, LAT), F32)
    o_ref[...] = ms[...].astype(BF16).reshape(o_ref.shape)


def finish_kernel(x_ref, xt_ref, w_ref, o_ref, mc, sh, br, ob, sem):
    copies = [pltpu.make_async_copy(ob.at[m], o_ref.at[m], sem.at[m]) for m in range(OWN)]
    for m in range(OWN):
        for j in range(MEM):
            mc[j * USED : j * USED + ROWS] = x_ref[j, m].astype(F32)
        whole = mc[0 : EXT * CQ]
        before, after = lat_shifts(whole)
        for b, x in enumerate((before, whole, after)):
            sh[b] = x.astype(BF16)
        for i in range(0, COLS, 4):
            patches = []
            for p in (i, i + 2):
                parts = [sh[b, p * CQ : (p + 4) * CQ] for b in range(3)]
                parts.append(xt_ref[m, p * CH : (p + 2) * CH])
                patches.append(jnp.concatenate(parts, axis=0))
            r = jnp.dot(w_ref[...], jnp.concatenate(patches, axis=1), preferred_element_type=F32)
            for n in range(4):
                rows, lanes = (n % 2) * CH, (n // 2) * LAT
                br[pl.ds(i + n, CH, stride=COLS), :] = r[rows : rows + CH, lanes : lanes + LAT]
        ob[m] = br[...].reshape(CH, COLS, LAT).astype(BF16)
        copies[m].start()
    for copy in copies:
        copy.wait()


def shards(fields, w_query, w_key, w_value, w_out):
    edge = jax.ShapeDtypeStruct((OWN, 2 * CH, LAT), BF16)
    plane = pltpu.VMEM((CH * COLS, LAT), F32)
    sib, nb = call(edges_kernel, (edge, edge), [plane], 0, 1_000_000, fields)
    swaps = [(i, (i - 1 if i % 2 == 0 else i + 1) % LON) for i in range(LON)]
    got_nb = lax.ppermute(nb, ("yhi", "x", "core"), swaps)
    got_sib = lax.all_gather(sib, "core", axis=0, tiled=False)
    qk_shape = jax.ShapeDtypeStruct((MEM, OWN, CQ, LAT), BF16)
    v0_shape = jax.ShapeDtypeStruct((MEM, HEAD + OWN * 8, LAT), BF16)
    v1_shape = jax.ShapeDtypeStruct((MEM, OWN, 8, LAT), BF16)
    ends = jax.ShapeDtypeStruct((OWN, 2 * ROWS, LAT), F32)
    pair = jax.ShapeDtypeStruct((18 * CQ, 4 * CH), BF16)
    pair_out = jax.ShapeDtypeStruct((2 * CH, 12 * CQ + 2 * CH), BF16)
    turned = jax.ShapeDtypeStruct((OWN, CH * COLS, LAT), BF16)
    qk, v0, v1, ends, w_pair, w_last, turned = call(
        inner_kernel,
        (qk_shape, v0_shape, v1_shape, ends, pair, pair_out, turned),
        [
            pltpu.VMEM((3 * CQ, 9 * CH), F32),
            plane,
            pltpu.VMEM((OWN, 6 * CQ, LAT), F32),
        ],
        450_000_000,
        2_000_000,
        fields,
        w_query,
        w_key,
        w_value,
        w_out,
    )
    qk, v0, v1 = call(
        outer_kernel,
        (qk_shape, v0_shape, v1_shape),
        [pltpu.VMEM((OWN, 4 * CH, LAT), BF16)] * 2
        + [pltpu.VMEM((2 * CQ + ROWS, LAT), F32), pltpu.VMEM((2 * CQ + ROWS + 8, LAT), F32)],
        300_000_000,
        1_500_000,
        qk,
        v0,
        v1,
        ends,
        w_pair,
        sib,
        nb,
        got_sib,
        got_nb,
        alias={0: 0, 1: 1, 2: 2},
    )
    mem, lon = ("z", "ylo"), ("yhi", "x")
    qk = lax.all_to_all(qk, mem, 0, 0, tiled=True)
    gram = call(
        gram_kernel,
        jax.ShapeDtypeStruct((4 * MEM, LAT), F32),
        [pltpu.VMEM((TOTAL * CQ, LAT), F32), pltpu.VMEM((3, TOTAL, LAT), F32)],
        20_000_000,
        600_000,
        qk,
    )
    gram = lax.all_gather(gram, "core", axis=0, tiled=False)
    v0 = call(
        header_kernel,
        v0_shape,
        [pltpu.VMEM((2, 4 * MEM, LAT), F32)],
        20_000,
        100_000,
        gram,
        v0,
        alias={1: 0},
    )
    v0 = lax.all_to_all(v0, mem, 0, 0, tiled=True)
    copies = jax.ShapeDtypeStruct((LON // 2, 4, LAT), F32)
    gram = call(spread_kernel, copies, [], 40_000, 200_000, v0)
    gram = lax.all_to_all(gram, lon, 0, 0, tiled=True)
    scale = 1.0 / math.sqrt(CQ * LAT * COLS * LON)
    v1 = call(
        functools.partial(softmax_kernel, scale),
        v1_shape,
        [pltpu.VMEM((8, LAT), F32)],
        40_000,
        400_000,
        gram,
        v1,
        alias={1: 0},
    )
    v1 = lax.all_to_all(v1, mem, 0, 0, tiled=True)
    mixed = call(
        mix_kernel,
        jax.ShapeDtypeStruct((MEM, OWN, ROWS, LAT), BF16),
        [pltpu.VMEM((2, TOTAL * 8, LAT), F32), pltpu.VMEM((TOTAL * ROWS, LAT), F32)],
        30_000_000,
        700_000,
        v0,
        v1,
    )
    mixed = lax.all_to_all(mixed, ("z", "ylo"), 0, 0, tiled=True)
    return call(
        finish_kernel,
        jax.ShapeDtypeStruct(fields.shape, BF16),
        [
            pltpu.VMEM((MEM * ROWS, LAT), F32),
            pltpu.VMEM((3, EXT * CQ, LAT), BF16),
            plane,
            pltpu.VMEM(fields.shape, BF16),
            pltpu.SemaphoreType.DMA((OWN,)),
        ],
        150_000_000,
        1_700_000,
        mixed,
        turned,
        w_last,
        far_out=True,
    )


def solution(mesh):
    fine = Mesh(mesh.devices.reshape(MEM // 2, 2, LON // 8, 4, 2), ("z", "ylo", "yhi", "x", "core"))
    spec = P(("z", "ylo"), None, ("yhi", "x", "core"), None)
    return jax.shard_map(
        shards,
        mesh=fine,
        in_specs=(spec, P(), P(), P(), P()),
        out_specs=spec,
        check_vma=False,
    )
```

```python
import functools
import math

import jax
import jax.numpy as jnp
from jax import lax
from jax.experimental import pallas as pl
from jax.experimental.pallas import tpu as pltpu
from jax.sharding import Mesh
from jax.sharding import PartitionSpec as P

CH, CQ, LAT = 64, 24, 128
HALF = CQ // 2
MEM, LON = 16, 32
OWN = 5
TOTAL = MEM * OWN
CUT = LAT - TOTAL
COLS = 8
EXT = COLS + 2
ROWS = 16
USED = EXT * CQ // MEM
HEAD = 8
F32, BF16 = jnp.float32, jnp.bfloat16
VMEM = pl.BlockSpec(memory_space=pltpu.VMEM)


HBM = pl.BlockSpec(memory_space=pl.ANY)


def call(body, outs, scratch, flops, nbytes, *args, alias=None, far_out=False):
    many = isinstance(outs, tuple)
    one = HBM if far_out else VMEM
    return pl.pallas_call(
        body,
        out_shape=outs,
        in_specs=[VMEM] * len(args),
        out_specs=(one,) * len(outs) if many else one,
        scratch_shapes=scratch,
        input_output_aliases=alias or {},
        compiler_params=pltpu.CompilerParams(vmem_limit_bytes=32 * 1024 * 1024),
        cost_estimate=pl.CostEstimate(flops=flops, bytes_accessed=nbytes, transcendentals=0),
    )(*args)


def lat_shifts(x):
    lane = lax.broadcasted_iota(jnp.int32, x.shape, 1)
    before = jnp.where(lane == 0, 0.0, pltpu.roll(x, 1, 1))
    after = jnp.where(lane == LAT - 1, 0.0, pltpu.roll(x, LAT - 1, 1))
    return before, after


def edges_kernel(f_ref, sib_ref, nb_ref, xf):
    even = lax.axis_index("core") == 0
    for m in range(OWN):
        xf[...] = f_ref[m].astype(F32).reshape(CH * COLS, LAT)
        for s in range(2):
            left = xf[pl.ds(s, CH, stride=COLS), :]
            right = xf[pl.ds(COLS - 2 + s, CH, stride=COLS), :]
            sib_ref[m, s * CH : (s + 1) * CH] = jnp.where(even, right, left).astype(BF16)
            nb_ref[m, s * CH : (s + 1) * CH] = jnp.where(even, left, right).astype(BF16)


def conv_pairs(w, xs):
    width = 3 * CQ
    lane = lax.broadcasted_iota(jnp.int32, (width, LAT), 1)
    wide = jnp.dot(w, jnp.concatenate(xs, axis=1), preferred_element_type=F32)
    pairs = []
    for n in range(len(xs)):
        r = wide[:, n * LAT : (n + 1) * LAT]
        outs = []
        for s in range(2):
            y = [r[(3 * s + b) * width : (3 * s + b + 1) * width] for b in range(3)]
            outs.append(
                y[1]
                + jnp.where(lane == 0, 0.0, pltpu.roll(y[0], 1, 1))
                + jnp.where(lane == LAT - 1, 0.0, pltpu.roll(y[2], LAT - 1, 1))
            )
        pairs.append(outs)
    return pairs


def put_block(v0_ref, v1_ref, j, m, block):
    v0_ref[j, HEAD + m * 8 : HEAD + m * 8 + 8] = block[:8].astype(BF16)
    v1_ref[j, m] = block[8:].astype(BF16)


def put_pair(qk_ref, vs, m, p, outs):
    for s in range(2):
        col = 2 * p + s
        vs[s * CQ : (s + 1) * CQ] = outs[s][2 * CQ :]
        if 1 <= col <= COLS:
            for h in range(2):
                qk_ref[2 * (col - 1) + h, m] = outs[s][h * CQ : (h + 1) * CQ].astype(BF16)


def inner_kernel(
    f_ref, wq_ref, wk_ref, wv_ref, wo_ref,
    qk_ref, v0_ref, v1_ref, e_ref, wp_ref, wf_ref, xt, ws, xf, vs,
):
    ws[0:HALF] = wq_ref[...].astype(F32)[:HALF]
    ws[HALF : 2 * HALF] = wk_ref[...].astype(F32)[:HALF]
    ws[2 * HALF : 3 * HALF] = wq_ref[...].astype(F32)[HALF:]
    ws[3 * HALF : 4 * HALF] = wk_ref[...].astype(F32)[HALF:]
    ws[2 * CQ :] = wv_ref[...].astype(F32)
    zero = jnp.zeros((3 * CQ, CH), F32)
    for b in range(3):
        taps = [ws[:, (3 * a + b) * CH : (3 * a + b + 1) * CH] for a in range(3)]
        for s in range(2):
            row = (3 * s + b) * 3 * CQ
            full = [zero] + taps if s else taps + [zero]
            wp_ref[row : row + 3 * CQ] = jnp.concatenate(full, axis=1).astype(BF16)
    wo = wo_ref[...].astype(F32)
    zero = jnp.zeros((CH, CQ), F32)
    row = lax.broadcasted_iota(jnp.int32, (CH, 2 * CH), 0)
    lane = lax.broadcasted_iota(jnp.int32, (CH, 2 * CH), 1)
    for s in range(2):
        full = []
        for b in range(3):
            taps = [wo[:, (3 * a + b) * CQ : (3 * a + b + 1) * CQ] for a in range(3)]
            full += [zero] + taps if s else taps + [zero]
        full.append(jnp.where(lane == row + s * CH, 1.0, 0.0))
        wf_ref[s * CH : (s + 1) * CH] = jnp.concatenate(full, axis=1).astype(BF16)
    for m in range(OWN):
        xf[...] = f_ref[m].astype(F32).reshape(CH * COLS, LAT)
        for i in range(COLS):
            xt[m, i * CH : (i + 1) * CH] = xf[pl.ds(i, CH, stride=COLS), :].astype(BF16)
    units = [(m, p) for m in range(OWN) for p in range(1, EXT // 2 - 1)]
    for n in range(0, len(units), 2):
        two = units[n : n + 2]
        xs = [xt[m, 2 * (p - 1) * CH : 2 * (p + 1) * CH] for m, p in two]
        for (m, p), outs in zip(two, conv_pairs(wp_ref[...], xs)):
            put_pair(qk_ref, vs.at[m, pl.ds((p - 1) * 2 * CQ, 2 * CQ)], m, p, outs)
    for m in range(OWN):
        for j in range(4, 12):
            row = j * USED - 2 * CQ
            put_block(v0_ref, v1_ref, j, m, vs[m, row : row + ROWS])
        e_ref[m, 0:ROWS] = vs[m, 0:ROWS]
        e_ref[m, ROWS:] = vs[m, 6 * CQ - ROWS :]


def outer_kernel(
    iq_ref, i0_ref, i1_ref, e_ref, wp_ref, sib_ref, nb_ref, gs_ref, gn_ref,
    qk_ref, v0_ref, v1_ref, xl, xr, vl, vr
):
    core = lax.axis_index("core")
    near = 2 * CH

    @pl.when(core == 0)
    def _():
        xl[:, :near] = gn_ref[...]
        xl[:, near:] = nb_ref[...]
        xr[:, :near] = sib_ref[...]
        xr[:, near:] = gs_ref[1]

    @pl.when(core == 1)
    def _():
        xl[:, :near] = gs_ref[0]
        xl[:, near:] = sib_ref[...]
        xr[:, :near] = nb_ref[...]
        xr[:, near:] = gn_ref[...]

    for m in range(OWN):
        left, right = conv_pairs(wp_ref[...], [xl[m], xr[m]])
        put_pair(qk_ref, vl.at[pl.ds(0, 2 * CQ)], m, 0, left)
        put_pair(qk_ref, vr.at[pl.ds(ROWS, 2 * CQ)], m, EXT // 2 - 1, right)
        vl[2 * CQ :] = e_ref[m, 0:ROWS]
        vr[0:ROWS] = e_ref[m, ROWS:]
        vr[ROWS + 2 * CQ :] = jnp.zeros((8, LAT), F32)
        for j in range(4):
            put_block(v0_ref, v1_ref, j, m, vl[j * USED : j * USED + ROWS])
            row = (12 + j) * USED - (8 * CQ - ROWS)
            put_block(v0_ref, v1_ref, 12 + j, m, vr[row : row + ROWS])


def gram_kernel(x_ref, v0_ref, o_ref, xs, gs, ps):
    xs[...] = x_ref[...].astype(F32).reshape(TOTAL * CQ, LAT)
    pad = jnp.zeros((LAT - TOTAL, LAT), BF16)
    q, k = [], []
    for r in range(HALF):
        q.append(xs[pl.ds(r, TOTAL, stride=CQ), :].astype(BF16))
        k.append(jnp.concatenate([xs[pl.ds(HALF + r, TOTAL, stride=CQ), :].astype(BF16), pad], axis=0))
    gram = lax.dot_general(
        jnp.concatenate(q, axis=1),
        jnp.concatenate(k, axis=1),
        (((1,), (1,)), ((), ())),
        preferred_element_type=F32,
    )
    lane = lax.broadcasted_iota(jnp.int32, gram.shape, 1)
    gs[0] = gram
    gs[1] = jnp.where(lane < TOTAL, 0.0, pltpu.roll(gram, TOTAL, 1))
    gs[2] = jnp.where(lane < TOTAL, 0.0, pltpu.roll(gram, TOTAL - CUT, 1))
    rest = jnp.zeros((2, LAT), F32)
    for s in range(MEM):
        row = s * OWN
        free = [gs[1 + h, row + 4 : row + 5, :] for h in range(2)]
        ps[0, 4 * s : 4 * s + 4] = gs[0, row : row + 4, :] + jnp.concatenate(free + [rest], axis=0)
    whole = ps[0]
    high = whole.astype(BF16).astype(F32)
    ps[0] = high
    ps[1] = whole - high
    for s in range(MEM):
        parts = [ps[part, 4 * s : 4 * s + 4] for part in range(2)]
        o_ref[s, 0:HEAD] = jnp.concatenate(parts, axis=0).astype(BF16)


def total_kernel(x_ref, o_ref):
    parts = jnp.sum(x_ref[:, 0:HEAD].astype(F32), axis=0)
    o_ref[...] = parts[0:4] + parts[4:8]


def spread_kernel(x_ref, o_ref):
    o_ref[...] = jnp.broadcast_to((x_ref[0] + x_ref[1])[None], o_ref.shape)


def softmax_kernel(scale, x_ref, v1_ref, o_ref, gs):
    gs[...] = jnp.zeros(gs.shape, F32)
    gs[0:4] = jnp.sum(x_ref[...], axis=0)
    gram = gs[...]
    head, tail = pltpu.roll(gram, LAT - TOTAL, 1), pltpu.roll(gram, LAT - TOTAL + CUT, 1)
    lane = lax.broadcasted_iota(jnp.int32, gram.shape, 1)
    gs[4:5] = jnp.where(lane[0:1] < CUT, head[0:1], tail[1:2])
    s = jnp.where(lane < TOTAL, gs[...] * scale, -jnp.inf)
    e = jnp.exp(s - jnp.max(s, axis=1, keepdims=True))
    w = e / jnp.sum(e, axis=1, keepdims=True)
    for m in range(OWN):
        o_ref[:, m, USED - 8 : USED - 7, :] = jnp.broadcast_to(
            w[m : m + 1].astype(BF16)[None], (MEM, 1, LAT)
        )


def mix_kernel(v0_ref, v1_ref, o_ref, vs, ms):
    vs[0] = v0_ref[:, HEAD:].astype(F32).reshape(TOTAL * 8, LAT)
    vs[1] = v1_ref[...].astype(F32).reshape(TOTAL * 8, LAT)
    rows = [vs[r // 8, pl.ds(r % 8, TOTAL, stride=8), :].astype(BF16) for r in range(ROWS)]
    w = rows[USED][:, :TOTAL]
    v = jnp.concatenate(rows[:USED], axis=1)
    mixed = jnp.dot(w, v, preferred_element_type=F32)
    for r in range(USED):
        ms[pl.ds(r, TOTAL, stride=ROWS), :] = mixed[:, r * LAT : (r + 1) * LAT]
    ms[pl.ds(USED, TOTAL, stride=ROWS), :] = jnp.zeros((TOTAL, LAT), F32)
    o_ref[...] = ms[...].astype(BF16).reshape(o_ref.shape)


def finish_kernel(x_ref, xt_ref, w_ref, o_ref, mc, sh, br, ob, sem):
    copies = [pltpu.make_async_copy(ob.at[m], o_ref.at[m], sem.at[m]) for m in range(OWN)]
    for m in range(OWN):
        for j in range(MEM):
            mc[j * USED : j * USED + ROWS] = x_ref[j, m].astype(F32)
        whole = mc[0 : EXT * CQ]
        before, after = lat_shifts(whole)
        for b, x in enumerate((before, whole, after)):
            sh[b] = x.astype(BF16)
        for i in range(0, COLS, 4):
            patches = []
            for p in (i, i + 2):
                parts = [sh[b, p * CQ : (p + 4) * CQ] for b in range(3)]
                parts.append(xt_ref[m, p * CH : (p + 2) * CH])
                patches.append(jnp.concatenate(parts, axis=0))
            r = jnp.dot(w_ref[...], jnp.concatenate(patches, axis=1), preferred_element_type=F32)
            for n in range(4):
                rows, lanes = (n % 2) * CH, (n // 2) * LAT
                br[pl.ds(i + n, CH, stride=COLS), :] = r[rows : rows + CH, lanes : lanes + LAT]
        ob[m] = br[...].reshape(CH, COLS, LAT).astype(BF16)
        copies[m].start()
    for copy in copies:
        copy.wait()


def shards(fields, w_query, w_key, w_value, w_out):
    edge = jax.ShapeDtypeStruct((OWN, 2 * CH, LAT), BF16)
    plane = pltpu.VMEM((CH * COLS, LAT), F32)
    sib, nb = call(edges_kernel, (edge, edge), [plane], 0, 1_000_000, fields)
    swaps = [(i, (i - 1 if i % 2 == 0 else i + 1) % LON) for i in range(LON)]
    got_nb = lax.ppermute(nb, ("yhi", "x", "core"), swaps)
    got_sib = lax.all_gather(sib, "core", axis=0, tiled=False)
    qk_shape = jax.ShapeDtypeStruct((MEM, OWN, CQ, LAT), BF16)
    v0_shape = jax.ShapeDtypeStruct((MEM, HEAD + OWN * 8, LAT), BF16)
    v1_shape = jax.ShapeDtypeStruct((MEM, OWN, 8, LAT), BF16)
    ends = jax.ShapeDtypeStruct((OWN, 2 * ROWS, LAT), F32)
    pair = jax.ShapeDtypeStruct((18 * CQ, 4 * CH), BF16)
    pair_out = jax.ShapeDtypeStruct((2 * CH, 12 * CQ + 2 * CH), BF16)
    turned = jax.ShapeDtypeStruct((OWN, CH * COLS, LAT), BF16)
    qk, v0, v1, ends, w_pair, w_last, turned = call(
        inner_kernel,
        (qk_shape, v0_shape, v1_shape, ends, pair, pair_out, turned),
        [
            pltpu.VMEM((3 * CQ, 9 * CH), F32),
            plane,
            pltpu.VMEM((OWN, 6 * CQ, LAT), F32),
        ],
        450_000_000,
        2_000_000,
        fields,
        w_query,
        w_key,
        w_value,
        w_out,
    )
    qk, v0, v1 = call(
        outer_kernel,
        (qk_shape, v0_shape, v1_shape),
        [pltpu.VMEM((OWN, 4 * CH, LAT), BF16)] * 2
        + [pltpu.VMEM((2 * CQ + ROWS, LAT), F32), pltpu.VMEM((2 * CQ + ROWS + 8, LAT), F32)],
        300_000_000,
        1_500_000,
        qk,
        v0,
        v1,
        ends,
        w_pair,
        sib,
        nb,
        got_sib,
        got_nb,
        alias={0: 0, 1: 1, 2: 2},
    )
    mem, lon = ("z", "ylo"), ("yhi", "x")
    qk = lax.all_to_all(qk, mem, 0, 0, tiled=True)
    v0 = call(
        gram_kernel,
        v0_shape,
        [
            pltpu.VMEM((TOTAL * CQ, LAT), F32),
            pltpu.VMEM((3, TOTAL, LAT), F32),
            pltpu.VMEM((2, 4 * MEM, LAT), F32),
        ],
        20_000_000,
        800_000,
        qk,
        v0,
        alias={1: 0},
    )
    v0 = lax.all_to_all(v0, mem, 0, 0, tiled=True)
    gram = call(total_kernel, jax.ShapeDtypeStruct((4, LAT), F32), [], 40_000, 200_000, v0)
    gram = lax.all_gather(gram, "core", axis=0, tiled=False)
    copies = jax.ShapeDtypeStruct((LON // 2, 4, LAT), F32)
    gram = call(spread_kernel, copies, [], 10_000, 40_000, gram)
    gram = lax.all_to_all(gram, lon, 0, 0, tiled=True)
    scale = 1.0 / math.sqrt(CQ * LAT * COLS * LON)
    v1 = call(
        functools.partial(softmax_kernel, scale),
        v1_shape,
        [pltpu.VMEM((8, LAT), F32)],
        40_000,
        400_000,
        gram,
        v1,
        alias={1: 0},
    )
    v1 = lax.all_to_all(v1, mem, 0, 0, tiled=True)
    mixed = call(
        mix_kernel,
        jax.ShapeDtypeStruct((MEM, OWN, ROWS, LAT), BF16),
        [pltpu.VMEM((2, TOTAL * 8, LAT), F32), pltpu.VMEM((TOTAL * ROWS, LAT), F32)],
        30_000_000,
        700_000,
        v0,
        v1,
    )
    mixed = lax.all_to_all(mixed, ("z", "ylo"), 0, 0, tiled=True)
    return call(
        finish_kernel,
        jax.ShapeDtypeStruct(fields.shape, BF16),
        [
            pltpu.VMEM((MEM * ROWS, LAT), F32),
            pltpu.VMEM((3, EXT * CQ, LAT), BF16),
            plane,
            pltpu.VMEM(fields.shape, BF16),
            pltpu.SemaphoreType.DMA((OWN,)),
        ],
        150_000_000,
        1_700_000,
        mixed,
        turned,
        w_last,
        far_out=True,
    )


def solution(mesh):
    fine = Mesh(mesh.devices.reshape(MEM // 2, 2, LON // 8, 4, 2), ("z", "ylo", "yhi", "x", "core"))
    spec = P(("z", "ylo"), None, ("yhi", "x", "core"), None)
    return jax.shard_map(
        shards,
        mesh=fine,
        in_specs=(spec, P(), P(), P(), P()),
        out_specs=spec,
        check_vma=False,
    )
```

```python
import functools
import math

import jax
import jax.numpy as jnp
from jax import lax
from jax.experimental import pallas as pl
from jax.experimental.pallas import tpu as pltpu
from jax.sharding import Mesh
from jax.sharding import PartitionSpec as P

CH, CQ, LAT = 64, 24, 128
HALF = CQ // 2
MEM, LON = 16, 32
OWN = 5
TOTAL = MEM * OWN
CUT = LAT - TOTAL
COLS = 8
EXT = COLS + 2
ROWS = 16
USED = EXT * CQ // MEM
EARLY = 3
HEAD = 8
F32, BF16 = jnp.float32, jnp.bfloat16
VMEM = pl.BlockSpec(memory_space=pltpu.VMEM)


HBM = pl.BlockSpec(memory_space=pl.ANY)


def call(body, outs, scratch, flops, nbytes, *args, alias=None, far_out=False):
    many = isinstance(outs, tuple)
    one = HBM if far_out else VMEM
    return pl.pallas_call(
        body,
        out_shape=outs,
        in_specs=[VMEM] * len(args),
        out_specs=(one,) * len(outs) if many else one,
        scratch_shapes=scratch,
        input_output_aliases=alias or {},
        compiler_params=pltpu.CompilerParams(vmem_limit_bytes=32 * 1024 * 1024),
        cost_estimate=pl.CostEstimate(flops=flops, bytes_accessed=nbytes, transcendentals=0),
    )(*args)


def lat_shifts(x):
    lane = lax.broadcasted_iota(jnp.int32, x.shape, 1)
    before = jnp.where(lane == 0, 0.0, pltpu.roll(x, 1, 1))
    after = jnp.where(lane == LAT - 1, 0.0, pltpu.roll(x, LAT - 1, 1))
    return before, after


def edges_kernel(f_ref, sib_ref, nb_ref, xf):
    even = lax.axis_index("core") == 0
    for m in range(OWN):
        xf[...] = f_ref[m].astype(F32).reshape(CH * COLS, LAT)
        for s in range(2):
            left = xf[pl.ds(s, CH, stride=COLS), :]
            right = xf[pl.ds(COLS - 2 + s, CH, stride=COLS), :]
            sib_ref[m, s * CH : (s + 1) * CH] = jnp.where(even, right, left).astype(BF16)
            nb_ref[m, s * CH : (s + 1) * CH] = jnp.where(even, left, right).astype(BF16)


def conv_pairs(w, xs):
    width = 3 * CQ
    lane = lax.broadcasted_iota(jnp.int32, (width, LAT), 1)
    wide = jnp.dot(w, jnp.concatenate(xs, axis=1), preferred_element_type=F32)
    pairs = []
    for n in range(len(xs)):
        r = wide[:, n * LAT : (n + 1) * LAT]
        outs = []
        for s in range(2):
            y = [r[(3 * s + b) * width : (3 * s + b + 1) * width] for b in range(3)]
            outs.append(
                y[1]
                + jnp.where(lane == 0, 0.0, pltpu.roll(y[0], 1, 1))
                + jnp.where(lane == LAT - 1, 0.0, pltpu.roll(y[2], LAT - 1, 1))
            )
        pairs.append(outs)
    return pairs


def put_block(v0_ref, v1_ref, j, m, block):
    low = block[:8].astype(BF16)
    if m < EARLY:
        v0_ref[j, HEAD + m * 8 : HEAD + m * 8 + 8] = low
    else:
        v1_ref[j, (OWN + m - EARLY) * 8 : (OWN + m - EARLY + 1) * 8] = low
    v1_ref[j, m * 8 : m * 8 + 8] = block[8:].astype(BF16)


def put_pair(qk_ref, vs, m, p, outs):
    for s in range(2):
        col = 2 * p + s
        vs[s * CQ : (s + 1) * CQ] = outs[s][2 * CQ :]
        if 1 <= col <= COLS:
            for h in range(2):
                qk_ref[2 * (col - 1) + h, m] = outs[s][h * CQ : (h + 1) * CQ].astype(BF16)


def inner_kernel(
    f_ref, wq_ref, wk_ref, wv_ref, wo_ref,
    qk_ref, v0_ref, v1_ref, e_ref, wp_ref, wf_ref, xt, ws, xf, vs,
):
    ws[0:HALF] = wq_ref[...].astype(F32)[:HALF]
    ws[HALF : 2 * HALF] = wk_ref[...].astype(F32)[:HALF]
    ws[2 * HALF : 3 * HALF] = wq_ref[...].astype(F32)[HALF:]
    ws[3 * HALF : 4 * HALF] = wk_ref[...].astype(F32)[HALF:]
    ws[2 * CQ :] = wv_ref[...].astype(F32)
    zero = jnp.zeros((3 * CQ, CH), F32)
    for b in range(3):
        taps = [ws[:, (3 * a + b) * CH : (3 * a + b + 1) * CH] for a in range(3)]
        for s in range(2):
            row = (3 * s + b) * 3 * CQ
            full = [zero] + taps if s else taps + [zero]
            wp_ref[row : row + 3 * CQ] = jnp.concatenate(full, axis=1).astype(BF16)
    wo = wo_ref[...].astype(F32)
    zero = jnp.zeros((CH, CQ), F32)
    row = lax.broadcasted_iota(jnp.int32, (CH, 2 * CH), 0)
    lane = lax.broadcasted_iota(jnp.int32, (CH, 2 * CH), 1)
    for s in range(2):
        full = []
        for b in range(3):
            taps = [wo[:, (3 * a + b) * CQ : (3 * a + b + 1) * CQ] for a in range(3)]
            full += [zero] + taps if s else taps + [zero]
        full.append(jnp.where(lane == row + s * CH, 1.0, 0.0))
        wf_ref[s * CH : (s + 1) * CH] = jnp.concatenate(full, axis=1).astype(BF16)
    for m in range(OWN):
        xf[...] = f_ref[m].astype(F32).reshape(CH * COLS, LAT)
        for i in range(COLS):
            xt[m, i * CH : (i + 1) * CH] = xf[pl.ds(i, CH, stride=COLS), :].astype(BF16)
    units = [(m, p) for m in range(OWN) for p in range(1, EXT // 2 - 1)]
    for n in range(0, len(units), 2):
        two = units[n : n + 2]
        xs = [xt[m, 2 * (p - 1) * CH : 2 * (p + 1) * CH] for m, p in two]
        for (m, p), outs in zip(two, conv_pairs(wp_ref[...], xs)):
            put_pair(qk_ref, vs.at[m, pl.ds((p - 1) * 2 * CQ, 2 * CQ)], m, p, outs)
    for m in range(OWN):
        for j in range(4, 12):
            row = j * USED - 2 * CQ
            put_block(v0_ref, v1_ref, j, m, vs[m, row : row + ROWS])
        e_ref[m, 0:ROWS] = vs[m, 0:ROWS]
        e_ref[m, ROWS:] = vs[m, 6 * CQ - ROWS :]


def outer_kernel(
    iq_ref, i0_ref, i1_ref, e_ref, wp_ref, sib_ref, nb_ref, gs_ref, gn_ref,
    qk_ref, v0_ref, v1_ref, xl, xr, vl, vr
):
    core = lax.axis_index("core")
    near = 2 * CH

    @pl.when(core == 0)
    def _():
        xl[:, :near] = gn_ref[...]
        xl[:, near:] = nb_ref[...]
        xr[:, :near] = sib_ref[...]
        xr[:, near:] = gs_ref[1]

    @pl.when(core == 1)
    def _():
        xl[:, :near] = gs_ref[0]
        xl[:, near:] = sib_ref[...]
        xr[:, :near] = nb_ref[...]
        xr[:, near:] = gn_ref[...]

    for m in range(OWN):
        left, right = conv_pairs(wp_ref[...], [xl[m], xr[m]])
        put_pair(qk_ref, vl.at[pl.ds(0, 2 * CQ)], m, 0, left)
        put_pair(qk_ref, vr.at[pl.ds(ROWS, 2 * CQ)], m, EXT // 2 - 1, right)
        vl[2 * CQ :] = e_ref[m, 0:ROWS]
        vr[0:ROWS] = e_ref[m, ROWS:]
        vr[ROWS + 2 * CQ :] = jnp.zeros((8, LAT), F32)
        for j in range(4):
            put_block(v0_ref, v1_ref, j, m, vl[j * USED : j * USED + ROWS])
            row = (12 + j) * USED - (8 * CQ - ROWS)
            put_block(v0_ref, v1_ref, 12 + j, m, vr[row : row + ROWS])


def gram_kernel(x_ref, v0_ref, o_ref, xs, gs, ps):
    xs[...] = x_ref[...].astype(F32).reshape(TOTAL * CQ, LAT)
    pad = jnp.zeros((LAT - TOTAL, LAT), BF16)
    q, k = [], []
    for r in range(HALF):
        q.append(xs[pl.ds(r, TOTAL, stride=CQ), :].astype(BF16))
        k.append(jnp.concatenate([xs[pl.ds(HALF + r, TOTAL, stride=CQ), :].astype(BF16), pad], axis=0))
    gram = lax.dot_general(
        jnp.concatenate(q, axis=1),
        jnp.concatenate(k, axis=1),
        (((1,), (1,)), ((), ())),
        preferred_element_type=F32,
    )
    lane = lax.broadcasted_iota(jnp.int32, gram.shape, 1)
    gs[0] = gram
    gs[1] = jnp.where(lane < TOTAL, 0.0, pltpu.roll(gram, TOTAL, 1))
    gs[2] = jnp.where(lane < TOTAL, 0.0, pltpu.roll(gram, TOTAL - CUT, 1))
    rest = jnp.zeros((2, LAT), F32)
    for s in range(MEM):
        row = s * OWN
        free = [gs[1 + h, row + 4 : row + 5, :] for h in range(2)]
        ps[0, 4 * s : 4 * s + 4] = gs[0, row : row + 4, :] + jnp.concatenate(free + [rest], axis=0)
    whole = ps[0]
    high = whole.astype(BF16).astype(F32)
    ps[0] = high
    ps[1] = whole - high
    for s in range(MEM):
        parts = [ps[part, 4 * s : 4 * s + 4] for part in range(2)]
        o_ref[s, 0:HEAD] = jnp.concatenate(parts, axis=0).astype(BF16)


def total_kernel(x_ref, o_ref):
    parts = jnp.sum(x_ref[:, 0:HEAD].astype(F32), axis=0)
    o_ref[...] = parts[0:4] + parts[4:8]


def spread_kernel(x_ref, o_ref):
    o_ref[...] = jnp.broadcast_to((x_ref[0] + x_ref[1])[None], o_ref.shape)


def softmax_kernel(scale, x_ref, v1_ref, o_ref, gs):
    gs[...] = jnp.zeros(gs.shape, F32)
    gs[0:4] = jnp.sum(x_ref[...], axis=0)
    gram = gs[...]
    head, tail = pltpu.roll(gram, LAT - TOTAL, 1), pltpu.roll(gram, LAT - TOTAL + CUT, 1)
    lane = lax.broadcasted_iota(jnp.int32, gram.shape, 1)
    gs[4:5] = jnp.where(lane[0:1] < CUT, head[0:1], tail[1:2])
    s = jnp.where(lane < TOTAL, gs[...] * scale, -jnp.inf)
    e = jnp.exp(s - jnp.max(s, axis=1, keepdims=True))
    w = e / jnp.sum(e, axis=1, keepdims=True)
    for m in range(OWN):
        row = m * 8 + USED - 8
        o_ref[:, row : row + 1, :] = jnp.broadcast_to(
            w[m : m + 1].astype(BF16)[None], (MEM, 1, LAT)
        )


def mix_kernel(v0_ref, v1_ref, o_ref, vs, ms):
    low = [v0_ref[:, HEAD:].astype(F32), v1_ref[:, OWN * 8 :].astype(F32)]
    vs[0] = jnp.concatenate(low, axis=1).reshape(TOTAL * 8, LAT)
    vs[1] = v1_ref[:, : OWN * 8].astype(F32).reshape(TOTAL * 8, LAT)
    rows = [vs[r // 8, pl.ds(r % 8, TOTAL, stride=8), :].astype(BF16) for r in range(ROWS)]
    w = rows[USED][:, :TOTAL]
    v = jnp.concatenate(rows[:USED], axis=1)
    mixed = jnp.dot(w, v, preferred_element_type=F32)
    for r in range(USED):
        ms[pl.ds(r, TOTAL, stride=ROWS), :] = mixed[:, r * LAT : (r + 1) * LAT]
    ms[pl.ds(USED, TOTAL, stride=ROWS), :] = jnp.zeros((TOTAL, LAT), F32)
    o_ref[...] = ms[...].astype(BF16).reshape(o_ref.shape)


def finish_kernel(x_ref, xt_ref, w_ref, o_ref, mc, sh, br, ob, sem):
    copies = [pltpu.make_async_copy(ob.at[m], o_ref.at[m], sem.at[m]) for m in range(OWN)]
    for m in range(OWN):
        for j in range(MEM):
            mc[j * USED : j * USED + ROWS] = x_ref[j, m].astype(F32)
        whole = mc[0 : EXT * CQ]
        before, after = lat_shifts(whole)
        for b, x in enumerate((before, whole, after)):
            sh[b] = x.astype(BF16)
        for i in range(0, COLS, 4):
            patches = []
            for p in (i, i + 2):
                parts = [sh[b, p * CQ : (p + 4) * CQ] for b in range(3)]
                parts.append(xt_ref[m, p * CH : (p + 2) * CH])
                patches.append(jnp.concatenate(parts, axis=0))
            r = jnp.dot(w_ref[...], jnp.concatenate(patches, axis=1), preferred_element_type=F32)
            for n in range(4):
                rows, lanes = (n % 2) * CH, (n // 2) * LAT
                br[pl.ds(i + n, CH, stride=COLS), :] = r[rows : rows + CH, lanes : lanes + LAT]
        ob[m] = br[...].reshape(CH, COLS, LAT).astype(BF16)
        copies[m].start()
    for copy in copies:
        copy.wait()


def shards(fields, w_query, w_key, w_value, w_out):
    edge = jax.ShapeDtypeStruct((OWN, 2 * CH, LAT), BF16)
    plane = pltpu.VMEM((CH * COLS, LAT), F32)
    sib, nb = call(edges_kernel, (edge, edge), [plane], 0, 1_000_000, fields)
    swaps = [(i, (i - 1 if i % 2 == 0 else i + 1) % LON) for i in range(LON)]
    got_nb = lax.ppermute(nb, ("yhi", "x", "core"), swaps)
    got_sib = lax.all_gather(sib, "core", axis=0, tiled=False)
    qk_shape = jax.ShapeDtypeStruct((MEM, OWN, CQ, LAT), BF16)
    v0_shape = jax.ShapeDtypeStruct((MEM, HEAD + EARLY * 8, LAT), BF16)
    v1_shape = jax.ShapeDtypeStruct((MEM, (2 * OWN - EARLY) * 8, LAT), BF16)
    ends = jax.ShapeDtypeStruct((OWN, 2 * ROWS, LAT), F32)
    pair = jax.ShapeDtypeStruct((18 * CQ, 4 * CH), BF16)
    pair_out = jax.ShapeDtypeStruct((2 * CH, 12 * CQ + 2 * CH), BF16)
    turned = jax.ShapeDtypeStruct((OWN, CH * COLS, LAT), BF16)
    qk, v0, v1, ends, w_pair, w_last, turned = call(
        inner_kernel,
        (qk_shape, v0_shape, v1_shape, ends, pair, pair_out, turned),
        [
            pltpu.VMEM((3 * CQ, 9 * CH), F32),
            plane,
            pltpu.VMEM((OWN, 6 * CQ, LAT), F32),
        ],
        450_000_000,
        2_000_000,
        fields,
        w_query,
        w_key,
        w_value,
        w_out,
    )
    qk, v0, v1 = call(
        outer_kernel,
        (qk_shape, v0_shape, v1_shape),
        [pltpu.VMEM((OWN, 4 * CH, LAT), BF16)] * 2
        + [pltpu.VMEM((2 * CQ + ROWS, LAT), F32), pltpu.VMEM((2 * CQ + ROWS + 8, LAT), F32)],
        300_000_000,
        1_500_000,
        qk,
        v0,
        v1,
        ends,
        w_pair,
        sib,
        nb,
        got_sib,
        got_nb,
        alias={0: 0, 1: 1, 2: 2},
    )
    mem, lon = ("z", "ylo"), ("yhi", "x")
    qk = lax.all_to_all(qk, mem, 0, 0, tiled=True)
    v0 = call(
        gram_kernel,
        v0_shape,
        [
            pltpu.VMEM((TOTAL * CQ, LAT), F32),
            pltpu.VMEM((3, TOTAL, LAT), F32),
            pltpu.VMEM((2, 4 * MEM, LAT), F32),
        ],
        20_000_000,
        800_000,
        qk,
        v0,
        alias={1: 0},
    )
    v0 = lax.all_to_all(v0, mem, 0, 0, tiled=True)
    gram = call(total_kernel, jax.ShapeDtypeStruct((4, LAT), F32), [], 40_000, 200_000, v0)
    gram = lax.all_gather(gram, "core", axis=0, tiled=False)
    copies = jax.ShapeDtypeStruct((LON // 2, 4, LAT), F32)
    gram = call(spread_kernel, copies, [], 10_000, 40_000, gram)
    gram = lax.all_to_all(gram, lon, 0, 0, tiled=True)
    scale = 1.0 / math.sqrt(CQ * LAT * COLS * LON)
    v1 = call(
        functools.partial(softmax_kernel, scale),
        v1_shape,
        [pltpu.VMEM((8, LAT), F32)],
        40_000,
        400_000,
        gram,
        v1,
        alias={1: 0},
    )
    v1 = lax.all_to_all(v1, mem, 0, 0, tiled=True)
    mixed = call(
        mix_kernel,
        jax.ShapeDtypeStruct((MEM, OWN, ROWS, LAT), BF16),
        [pltpu.VMEM((2, TOTAL * 8, LAT), F32), pltpu.VMEM((TOTAL * ROWS, LAT), F32)],
        30_000_000,
        700_000,
        v0,
        v1,
    )
    mixed = lax.all_to_all(mixed, ("z", "ylo"), 0, 0, tiled=True)
    return call(
        finish_kernel,
        jax.ShapeDtypeStruct(fields.shape, BF16),
        [
            pltpu.VMEM((MEM * ROWS, LAT), F32),
            pltpu.VMEM((3, EXT * CQ, LAT), BF16),
            plane,
            pltpu.VMEM(fields.shape, BF16),
            pltpu.SemaphoreType.DMA((OWN,)),
        ],
        150_000_000,
        1_700_000,
        mixed,
        turned,
        w_last,
        far_out=True,
    )


def solution(mesh):
    fine = Mesh(mesh.devices.reshape(MEM // 2, 2, LON // 8, 4, 2), ("z", "ylo", "yhi", "x", "core"))
    spec = P(("z", "ylo"), None, ("yhi", "x", "core"), None)
    return jax.shard_map(
        shards,
        mesh=fine,
        in_specs=(spec, P(), P(), P(), P()),
        out_specs=spec,
        check_vma=False,
    )
```

```python
import functools
import math

import jax
import jax.numpy as jnp
from jax import lax
from jax.experimental import pallas as pl
from jax.experimental.pallas import tpu as pltpu
from jax.sharding import Mesh
from jax.sharding import PartitionSpec as P

CH, CQ, LAT = 64, 24, 128
HALF = CQ // 2
MEM, LON = 16, 32
OWN = 5
TOTAL = MEM * OWN
CUT = LAT - TOTAL
COLS = 8
EXT = COLS + 2
ROWS = 16
USED = EXT * CQ // MEM
LATE = 3
HEAD = 8
F32, BF16 = jnp.float32, jnp.bfloat16
VMEM = pl.BlockSpec(memory_space=pltpu.VMEM)


HBM = pl.BlockSpec(memory_space=pl.ANY)


def call(body, outs, scratch, flops, nbytes, *args, alias=None, far_out=False):
    many = isinstance(outs, tuple)
    one = HBM if far_out else VMEM
    return pl.pallas_call(
        body,
        out_shape=outs,
        in_specs=[VMEM] * len(args),
        out_specs=(one,) * len(outs) if many else one,
        scratch_shapes=scratch,
        input_output_aliases=alias or {},
        compiler_params=pltpu.CompilerParams(vmem_limit_bytes=32 * 1024 * 1024),
        cost_estimate=pl.CostEstimate(flops=flops, bytes_accessed=nbytes, transcendentals=0),
    )(*args)


def lat_shifts(x):
    lane = lax.broadcasted_iota(jnp.int32, x.shape, 1)
    before = jnp.where(lane == 0, 0.0, pltpu.roll(x, 1, 1))
    after = jnp.where(lane == LAT - 1, 0.0, pltpu.roll(x, LAT - 1, 1))
    return before, after


def edges_kernel(f_ref, sib_ref, nb_ref, xf):
    even = lax.axis_index("core") == 0
    for m in range(OWN):
        xf[...] = f_ref[m].astype(F32).reshape(CH * COLS, LAT)
        for s in range(2):
            left = xf[pl.ds(s, CH, stride=COLS), :]
            right = xf[pl.ds(COLS - 2 + s, CH, stride=COLS), :]
            sib_ref[m, s * CH : (s + 1) * CH] = jnp.where(even, right, left).astype(BF16)
            nb_ref[m, s * CH : (s + 1) * CH] = jnp.where(even, left, right).astype(BF16)


def conv_pairs(w, xs):
    width = 3 * CQ
    lane = lax.broadcasted_iota(jnp.int32, (width, LAT), 1)
    wide = jnp.dot(w, jnp.concatenate(xs, axis=1), preferred_element_type=F32)
    pairs = []
    for n in range(len(xs)):
        r = wide[:, n * LAT : (n + 1) * LAT]
        outs = []
        for s in range(2):
            y = [r[(3 * s + b) * width : (3 * s + b + 1) * width] for b in range(3)]
            outs.append(
                y[1]
                + jnp.where(lane == 0, 0.0, pltpu.roll(y[0], 1, 1))
                + jnp.where(lane == LAT - 1, 0.0, pltpu.roll(y[2], LAT - 1, 1))
            )
        pairs.append(outs)
    return pairs


def put_block(v0_ref, v1_ref, j, m, block):
    v0_ref[j, HEAD + m * 8 : HEAD + m * 8 + 8] = block[:8].astype(BF16)
    high = block[8:].astype(BF16)
    if m < LATE:
        v1_ref[j, m * 8 : m * 8 + 8] = high
    else:
        row = HEAD + (OWN + m - LATE) * 8
        v0_ref[j, row : row + 8] = high


def put_pair(qk_ref, vs, m, p, outs):
    for s in range(2):
        col = 2 * p + s
        vs[s * CQ : (s + 1) * CQ] = outs[s][2 * CQ :]
        if 1 <= col <= COLS:
            for h in range(2):
                qk_ref[2 * (col - 1) + h, m] = outs[s][h * CQ : (h + 1) * CQ].astype(BF16)


def inner_kernel(
    f_ref, wq_ref, wk_ref, wv_ref, wo_ref,
    qk_ref, v0_ref, v1_ref, e_ref, wp_ref, wf_ref, xt, ws, xf, vs,
):
    ws[0:HALF] = wq_ref[...].astype(F32)[:HALF]
    ws[HALF : 2 * HALF] = wk_ref[...].astype(F32)[:HALF]
    ws[2 * HALF : 3 * HALF] = wq_ref[...].astype(F32)[HALF:]
    ws[3 * HALF : 4 * HALF] = wk_ref[...].astype(F32)[HALF:]
    ws[2 * CQ :] = wv_ref[...].astype(F32)
    zero = jnp.zeros((3 * CQ, CH), F32)
    for b in range(3):
        taps = [ws[:, (3 * a + b) * CH : (3 * a + b + 1) * CH] for a in range(3)]
        for s in range(2):
            row = (3 * s + b) * 3 * CQ
            full = [zero] + taps if s else taps + [zero]
            wp_ref[row : row + 3 * CQ] = jnp.concatenate(full, axis=1).astype(BF16)
    wo = wo_ref[...].astype(F32)
    zero = jnp.zeros((CH, CQ), F32)
    row = lax.broadcasted_iota(jnp.int32, (CH, 2 * CH), 0)
    lane = lax.broadcasted_iota(jnp.int32, (CH, 2 * CH), 1)
    for s in range(2):
        full = []
        for b in range(3):
            taps = [wo[:, (3 * a + b) * CQ : (3 * a + b + 1) * CQ] for a in range(3)]
            full += [zero] + taps if s else taps + [zero]
        full.append(jnp.where(lane == row + s * CH, 1.0, 0.0))
        wf_ref[s * CH : (s + 1) * CH] = jnp.concatenate(full, axis=1).astype(BF16)
    for m in range(OWN):
        xf[...] = f_ref[m].astype(F32).reshape(CH * COLS, LAT)
        for i in range(COLS):
            xt[m, i * CH : (i + 1) * CH] = xf[pl.ds(i, CH, stride=COLS), :].astype(BF16)
    units = [(m, p) for m in range(OWN) for p in range(1, EXT // 2 - 1)]
    for n in range(0, len(units), 2):
        two = units[n : n + 2]
        xs = [xt[m, 2 * (p - 1) * CH : 2 * (p + 1) * CH] for m, p in two]
        for (m, p), outs in zip(two, conv_pairs(wp_ref[...], xs)):
            put_pair(qk_ref, vs.at[m, pl.ds((p - 1) * 2 * CQ, 2 * CQ)], m, p, outs)
    for m in range(OWN):
        for j in range(4, 12):
            row = j * USED - 2 * CQ
            put_block(v0_ref, v1_ref, j, m, vs[m, row : row + ROWS])
        e_ref[m, 0:ROWS] = vs[m, 0:ROWS]
        e_ref[m, ROWS:] = vs[m, 6 * CQ - ROWS :]


def outer_kernel(
    iq_ref, i0_ref, i1_ref, e_ref, wp_ref, sib_ref, nb_ref, gs_ref, gn_ref,
    qk_ref, v0_ref, v1_ref, xl, xr, vl, vr
):
    core = lax.axis_index("core")
    near = 2 * CH

    @pl.when(core == 0)
    def _():
        xl[:, :near] = gn_ref[...]
        xl[:, near:] = nb_ref[...]
        xr[:, :near] = sib_ref[...]
        xr[:, near:] = gs_ref[1]

    @pl.when(core == 1)
    def _():
        xl[:, :near] = gs_ref[0]
        xl[:, near:] = sib_ref[...]
        xr[:, :near] = nb_ref[...]
        xr[:, near:] = gn_ref[...]

    for m in range(OWN):
        left, right = conv_pairs(wp_ref[...], [xl[m], xr[m]])
        put_pair(qk_ref, vl.at[pl.ds(0, 2 * CQ)], m, 0, left)
        put_pair(qk_ref, vr.at[pl.ds(ROWS, 2 * CQ)], m, EXT // 2 - 1, right)
        vl[2 * CQ :] = e_ref[m, 0:ROWS]
        vr[0:ROWS] = e_ref[m, ROWS:]
        vr[ROWS + 2 * CQ :] = jnp.zeros((8, LAT), F32)
        for j in range(4):
            put_block(v0_ref, v1_ref, j, m, vl[j * USED : j * USED + ROWS])
            row = (12 + j) * USED - (8 * CQ - ROWS)
            put_block(v0_ref, v1_ref, 12 + j, m, vr[row : row + ROWS])


def gram_kernel(x_ref, v0_ref, o_ref, xs, gs, ps):
    xs[...] = x_ref[...].astype(F32).reshape(TOTAL * CQ, LAT)
    pad = jnp.zeros((LAT - TOTAL, LAT), BF16)
    q, k = [], []
    for r in range(HALF):
        q.append(xs[pl.ds(r, TOTAL, stride=CQ), :].astype(BF16))
        k.append(jnp.concatenate([xs[pl.ds(HALF + r, TOTAL, stride=CQ), :].astype(BF16), pad], axis=0))
    gram = lax.dot_general(
        jnp.concatenate(q, axis=1),
        jnp.concatenate(k, axis=1),
        (((1,), (1,)), ((), ())),
        preferred_element_type=F32,
    )
    lane = lax.broadcasted_iota(jnp.int32, gram.shape, 1)
    gs[0] = gram
    gs[1] = jnp.where(lane < TOTAL, 0.0, pltpu.roll(gram, TOTAL, 1))
    gs[2] = jnp.where(lane < TOTAL, 0.0, pltpu.roll(gram, TOTAL - CUT, 1))
    rest = jnp.zeros((2, LAT), F32)
    for s in range(MEM):
        row = s * OWN
        free = [gs[1 + h, row + 4 : row + 5, :] for h in range(2)]
        ps[0, 4 * s : 4 * s + 4] = gs[0, row : row + 4, :] + jnp.concatenate(free + [rest], axis=0)
    whole = ps[0]
    high = whole.astype(BF16).astype(F32)
    ps[0] = high
    ps[1] = whole - high
    for s in range(MEM):
        parts = [ps[part, 4 * s : 4 * s + 4] for part in range(2)]
        o_ref[s, 0:HEAD] = jnp.concatenate(parts, axis=0).astype(BF16)


def total_kernel(x_ref, o_ref):
    parts = jnp.sum(x_ref[:, 0:HEAD].astype(F32), axis=0)
    o_ref[...] = parts[0:4] + parts[4:8]


def spread_kernel(x_ref, o_ref):
    o_ref[...] = jnp.broadcast_to((x_ref[0] + x_ref[1])[None], o_ref.shape)


def softmax_kernel(scale, x_ref, v1_ref, o_ref, gs):
    gs[...] = jnp.zeros(gs.shape, F32)
    gs[0:4] = jnp.sum(x_ref[...], axis=0)
    gram = gs[...]
    head, tail = pltpu.roll(gram, LAT - TOTAL, 1), pltpu.roll(gram, LAT - TOTAL + CUT, 1)
    lane = lax.broadcasted_iota(jnp.int32, gram.shape, 1)
    gs[4:5] = jnp.where(lane[0:1] < CUT, head[0:1], tail[1:2])
    s = jnp.where(lane < TOTAL, gs[...] * scale, -jnp.inf)
    e = jnp.exp(s - jnp.max(s, axis=1, keepdims=True))
    w = e / jnp.sum(e, axis=1, keepdims=True)
    o_ref[:, LATE * 8 :] = jnp.broadcast_to(w.astype(BF16)[None], (MEM, 8, LAT))


def mix_kernel(v0_ref, v1_ref, o_ref, ws, vs, ms):
    for s in range(MEM):
        ws[s * OWN : (s + 1) * OWN] = v1_ref[s, LATE * 8 :].astype(F32)[:OWN]
    w = ws[...].astype(BF16)[:, :TOTAL]
    vs[0] = v0_ref[:, HEAD : HEAD + OWN * 8].astype(F32).reshape(TOTAL * 8, LAT)
    high = [v1_ref[:, : LATE * 8].astype(F32), v0_ref[:, HEAD + OWN * 8 :].astype(F32)]
    vs[1] = jnp.concatenate(high, axis=1).reshape(TOTAL * 8, LAT)
    rows = [vs[r // 8, pl.ds(r % 8, TOTAL, stride=8), :].astype(BF16) for r in range(USED)]
    v = jnp.concatenate(rows, axis=1)
    mixed = jnp.dot(w, v, preferred_element_type=F32)
    for r in range(USED):
        ms[pl.ds(r, TOTAL, stride=ROWS), :] = mixed[:, r * LAT : (r + 1) * LAT]
    ms[pl.ds(USED, TOTAL, stride=ROWS), :] = jnp.zeros((TOTAL, LAT), F32)
    o_ref[...] = ms[...].astype(BF16).reshape(o_ref.shape)


def finish_kernel(x_ref, xt_ref, w_ref, o_ref, mc, sh, br, ob, sem):
    copies = [pltpu.make_async_copy(ob.at[m], o_ref.at[m], sem.at[m]) for m in range(OWN)]
    for m in range(OWN):
        for j in range(MEM):
            mc[j * USED : j * USED + ROWS] = x_ref[j, m].astype(F32)
        whole = mc[0 : EXT * CQ]
        before, after = lat_shifts(whole)
        for b, x in enumerate((before, whole, after)):
            sh[b] = x.astype(BF16)
        for i in range(0, COLS, 4):
            patches = []
            for p in (i, i + 2):
                parts = [sh[b, p * CQ : (p + 4) * CQ] for b in range(3)]
                parts.append(xt_ref[m, p * CH : (p + 2) * CH])
                patches.append(jnp.concatenate(parts, axis=0))
            r = jnp.dot(w_ref[...], jnp.concatenate(patches, axis=1), preferred_element_type=F32)
            for n in range(4):
                rows, lanes = (n % 2) * CH, (n // 2) * LAT
                br[pl.ds(i + n, CH, stride=COLS), :] = r[rows : rows + CH, lanes : lanes + LAT]
        ob[m] = br[...].reshape(CH, COLS, LAT).astype(BF16)
        copies[m].start()
    for copy in copies:
        copy.wait()


def shards(fields, w_query, w_key, w_value, w_out):
    edge = jax.ShapeDtypeStruct((OWN, 2 * CH, LAT), BF16)
    plane = pltpu.VMEM((CH * COLS, LAT), F32)
    sib, nb = call(edges_kernel, (edge, edge), [plane], 0, 1_000_000, fields)
    swaps = [(i, (i - 1 if i % 2 == 0 else i + 1) % LON) for i in range(LON)]
    got_nb = lax.ppermute(nb, ("yhi", "x", "core"), swaps)
    got_sib = lax.all_gather(sib, "core", axis=0, tiled=False)
    qk_shape = jax.ShapeDtypeStruct((MEM, OWN, CQ, LAT), BF16)
    v0_shape = jax.ShapeDtypeStruct((MEM, HEAD + (2 * OWN - LATE) * 8, LAT), BF16)
    v1_shape = jax.ShapeDtypeStruct((MEM, LATE * 8 + 8, LAT), BF16)
    ends = jax.ShapeDtypeStruct((OWN, 2 * ROWS, LAT), F32)
    pair = jax.ShapeDtypeStruct((18 * CQ, 4 * CH), BF16)
    pair_out = jax.ShapeDtypeStruct((2 * CH, 12 * CQ + 2 * CH), BF16)
    turned = jax.ShapeDtypeStruct((OWN, CH * COLS, LAT), BF16)
    qk, v0, v1, ends, w_pair, w_last, turned = call(
        inner_kernel,
        (qk_shape, v0_shape, v1_shape, ends, pair, pair_out, turned),
        [
            pltpu.VMEM((3 * CQ, 9 * CH), F32),
            plane,
            pltpu.VMEM((OWN, 6 * CQ, LAT), F32),
        ],
        450_000_000,
        2_000_000,
        fields,
        w_query,
        w_key,
        w_value,
        w_out,
    )
    qk, v0, v1 = call(
        outer_kernel,
        (qk_shape, v0_shape, v1_shape),
        [pltpu.VMEM((OWN, 4 * CH, LAT), BF16)] * 2
        + [pltpu.VMEM((2 * CQ + ROWS, LAT), F32), pltpu.VMEM((2 * CQ + ROWS + 8, LAT), F32)],
        300_000_000,
        1_500_000,
        qk,
        v0,
        v1,
        ends,
        w_pair,
        sib,
        nb,
        got_sib,
        got_nb,
        alias={0: 0, 1: 1, 2: 2},
    )
    mem, lon = ("z", "ylo"), ("yhi", "x")
    qk = lax.all_to_all(qk, mem, 0, 0, tiled=True)
    v0 = call(
        gram_kernel,
        v0_shape,
        [
            pltpu.VMEM((TOTAL * CQ, LAT), F32),
            pltpu.VMEM((3, TOTAL, LAT), F32),
            pltpu.VMEM((2, 4 * MEM, LAT), F32),
        ],
        20_000_000,
        800_000,
        qk,
        v0,
        alias={1: 0},
    )
    v0 = lax.all_to_all(v0, mem, 0, 0, tiled=True)
    gram = call(total_kernel, jax.ShapeDtypeStruct((4, LAT), F32), [], 40_000, 200_000, v0)
    gram = lax.all_gather(gram, "core", axis=0, tiled=False)
    copies = jax.ShapeDtypeStruct((LON // 2, 4, LAT), F32)
    gram = call(spread_kernel, copies, [], 10_000, 40_000, gram)
    gram = lax.all_to_all(gram, lon, 0, 0, tiled=True)
    scale = 1.0 / math.sqrt(CQ * LAT * COLS * LON)
    v1 = call(
        functools.partial(softmax_kernel, scale),
        v1_shape,
        [pltpu.VMEM((8, LAT), F32)],
        40_000,
        400_000,
        gram,
        v1,
        alias={1: 0},
    )
    v1 = lax.all_to_all(v1, mem, 0, 0, tiled=True)
    mixed = call(
        mix_kernel,
        jax.ShapeDtypeStruct((MEM, OWN, ROWS, LAT), BF16),
        [
            pltpu.VMEM((TOTAL, LAT), F32),
            pltpu.VMEM((2, TOTAL * 8, LAT), F32),
            pltpu.VMEM((TOTAL * ROWS, LAT), F32),
        ],
        30_000_000,
        700_000,
        v0,
        v1,
    )
    mixed = lax.all_to_all(mixed, ("z", "ylo"), 0, 0, tiled=True)
    return call(
        finish_kernel,
        jax.ShapeDtypeStruct(fields.shape, BF16),
        [
            pltpu.VMEM((MEM * ROWS, LAT), F32),
            pltpu.VMEM((3, EXT * CQ, LAT), BF16),
            plane,
            pltpu.VMEM(fields.shape, BF16),
            pltpu.SemaphoreType.DMA((OWN,)),
        ],
        150_000_000,
        1_700_000,
        mixed,
        turned,
        w_last,
        far_out=True,
    )


def solution(mesh):
    fine = Mesh(mesh.devices.reshape(MEM // 2, 2, LON // 8, 4, 2), ("z", "ylo", "yhi", "x", "core"))
    spec = P(("z", "ylo"), None, ("yhi", "x", "core"), None)
    return jax.shard_map(
        shards,
        mesh=fine,
        in_specs=(spec, P(), P(), P(), P()),
        out_specs=spec,
        check_vma=False,
    )
```

```python
import functools
import math

import jax
import jax.numpy as jnp
from jax import lax
from jax.experimental import pallas as pl
from jax.experimental.pallas import tpu as pltpu
from jax.sharding import Mesh
from jax.sharding import PartitionSpec as P

CH, CQ, LAT = 64, 24, 128
HALF = CQ // 2
MEM, LON = 16, 32
OWN = 5
TOTAL = MEM * OWN
CUT = LAT - TOTAL
COLS = 8
EXT = COLS + 2
ROWS = 16
USED = EXT * CQ // MEM
HEAD = 8
F32, BF16 = jnp.float32, jnp.bfloat16
VMEM = pl.BlockSpec(memory_space=pltpu.VMEM)


HBM = pl.BlockSpec(memory_space=pl.ANY)


def call(body, outs, scratch, flops, nbytes, *args, alias=None, far_out=False):
    many = isinstance(outs, tuple)
    one = HBM if far_out else VMEM
    return pl.pallas_call(
        body,
        out_shape=outs,
        in_specs=[VMEM] * len(args),
        out_specs=(one,) * len(outs) if many else one,
        scratch_shapes=scratch,
        input_output_aliases=alias or {},
        compiler_params=pltpu.CompilerParams(vmem_limit_bytes=32 * 1024 * 1024),
        cost_estimate=pl.CostEstimate(flops=flops, bytes_accessed=nbytes, transcendentals=0),
    )(*args)


def lat_shifts(x):
    lane = lax.broadcasted_iota(jnp.int32, x.shape, 1)
    before = jnp.where(lane == 0, 0.0, pltpu.roll(x, 1, 1))
    after = jnp.where(lane == LAT - 1, 0.0, pltpu.roll(x, LAT - 1, 1))
    return before, after


def edges_kernel(f_ref, sib_ref, nb_ref, xf):
    even = lax.axis_index("core") == 0
    for m in range(OWN):
        xf[...] = f_ref[m].astype(F32).reshape(CH * COLS, LAT)
        for s in range(2):
            left = xf[pl.ds(s, CH, stride=COLS), :]
            right = xf[pl.ds(COLS - 2 + s, CH, stride=COLS), :]
            sib_ref[m, s * CH : (s + 1) * CH] = jnp.where(even, right, left).astype(BF16)
            nb_ref[m, s * CH : (s + 1) * CH] = jnp.where(even, left, right).astype(BF16)


def conv_pairs(w, xs):
    width = 3 * CQ
    lane = lax.broadcasted_iota(jnp.int32, (width, LAT), 1)
    wide = jnp.dot(w, jnp.concatenate(xs, axis=1), preferred_element_type=F32)
    pairs = []
    for n in range(len(xs)):
        r = wide[:, n * LAT : (n + 1) * LAT]
        outs = []
        for s in range(2):
            y = [r[(3 * s + b) * width : (3 * s + b + 1) * width] for b in range(3)]
            outs.append(
                y[1]
                + jnp.where(lane == 0, 0.0, pltpu.roll(y[0], 1, 1))
                + jnp.where(lane == LAT - 1, 0.0, pltpu.roll(y[2], LAT - 1, 1))
            )
        pairs.append(outs)
    return pairs


def put_block(v0_ref, v1_ref, j, m, block):
    v0_ref[j, HEAD + m * 8 : HEAD + m * 8 + 8] = block[:8].astype(BF16)
    v1_ref[j, m] = block[8:].astype(BF16)


def put_pair(qk_ref, vs, m, p, outs):
    for s in range(2):
        col = 2 * p + s
        vs[s * CQ : (s + 1) * CQ] = outs[s][2 * CQ :]
        if 1 <= col <= COLS:
            for h in range(2):
                qk_ref[2 * (col - 1) + h, m] = outs[s][h * CQ : (h + 1) * CQ].astype(BF16)


def inner_kernel(
    f_ref, wq_ref, wk_ref, wv_ref, wo_ref,
    qk_ref, v0_ref, v1_ref, e_ref, wp_ref, wf_ref, xt, ws, xf, vs,
):
    ws[0:HALF] = wq_ref[...].astype(F32)[:HALF]
    ws[HALF : 2 * HALF] = wk_ref[...].astype(F32)[:HALF]
    ws[2 * HALF : 3 * HALF] = wq_ref[...].astype(F32)[HALF:]
    ws[3 * HALF : 4 * HALF] = wk_ref[...].astype(F32)[HALF:]
    ws[2 * CQ :] = wv_ref[...].astype(F32)
    zero = jnp.zeros((3 * CQ, CH), F32)
    for b in range(3):
        taps = [ws[:, (3 * a + b) * CH : (3 * a + b + 1) * CH] for a in range(3)]
        for s in range(2):
            row = (3 * s + b) * 3 * CQ
            full = [zero] + taps if s else taps + [zero]
            wp_ref[row : row + 3 * CQ] = jnp.concatenate(full, axis=1).astype(BF16)
    wo = wo_ref[...].astype(F32)
    zero = jnp.zeros((CH, CQ), F32)
    row = lax.broadcasted_iota(jnp.int32, (CH, 2 * CH), 0)
    lane = lax.broadcasted_iota(jnp.int32, (CH, 2 * CH), 1)
    for s in range(2):
        full = []
        for b in range(3):
            taps = [wo[:, (3 * a + b) * CQ : (3 * a + b + 1) * CQ] for a in range(3)]
            full += [zero] + taps if s else taps + [zero]
        full.append(jnp.where(lane == row + s * CH, 1.0, 0.0))
        wf_ref[s * CH : (s + 1) * CH] = jnp.concatenate(full, axis=1).astype(BF16)
    for m in range(OWN):
        xf[...] = f_ref[m].astype(F32).reshape(CH * COLS, LAT)
        for i in range(COLS):
            xt[m, i * CH : (i + 1) * CH] = xf[pl.ds(i, CH, stride=COLS), :].astype(BF16)
    units = [(m, p) for m in range(OWN) for p in range(1, EXT // 2 - 1)]
    for n in range(0, len(units), 2):
        two = units[n : n + 2]
        xs = [xt[m, 2 * (p - 1) * CH : 2 * (p + 1) * CH] for m, p in two]
        for (m, p), outs in zip(two, conv_pairs(wp_ref[...], xs)):
            put_pair(qk_ref, vs.at[m, pl.ds((p - 1) * 2 * CQ, 2 * CQ)], m, p, outs)
    for m in range(OWN):
        for j in range(4, 12):
            row = j * USED - 2 * CQ
            put_block(v0_ref, v1_ref, j, m, vs[m, row : row + ROWS])
        e_ref[m, 0:ROWS] = vs[m, 0:ROWS]
        e_ref[m, ROWS:] = vs[m, 6 * CQ - ROWS :]


def outer_kernel(
    iq_ref, i0_ref, i1_ref, e_ref, wp_ref, sib_ref, nb_ref, gs_ref, gn_ref,
    qk_ref, v0_ref, v1_ref, xl, xr, vl, vr
):
    core = lax.axis_index("core")
    near = 2 * CH

    @pl.when(core == 0)
    def _():
        xl[:, :near] = gn_ref[...]
        xl[:, near:] = nb_ref[...]
        xr[:, :near] = sib_ref[...]
        xr[:, near:] = gs_ref[1]

    @pl.when(core == 1)
    def _():
        xl[:, :near] = gs_ref[0]
        xl[:, near:] = sib_ref[...]
        xr[:, :near] = nb_ref[...]
        xr[:, near:] = gn_ref[...]

    for m in range(OWN):
        left, right = conv_pairs(wp_ref[...], [xl[m], xr[m]])
        put_pair(qk_ref, vl.at[pl.ds(0, 2 * CQ)], m, 0, left)
        put_pair(qk_ref, vr.at[pl.ds(ROWS, 2 * CQ)], m, EXT // 2 - 1, right)
        vl[2 * CQ :] = e_ref[m, 0:ROWS]
        vr[0:ROWS] = e_ref[m, ROWS:]
        vr[ROWS + 2 * CQ :] = jnp.zeros((8, LAT), F32)
        for j in range(4):
            put_block(v0_ref, v1_ref, j, m, vl[j * USED : j * USED + ROWS])
            row = (12 + j) * USED - (8 * CQ - ROWS)
            put_block(v0_ref, v1_ref, 12 + j, m, vr[row : row + ROWS])


def gram_kernel(x_ref, g_ref, xs, gs):
    xs[...] = x_ref[...].astype(F32).reshape(TOTAL * CQ, LAT)
    pad = jnp.zeros((LAT - TOTAL, LAT), BF16)
    q, k = [], []
    for r in range(HALF):
        q.append(xs[pl.ds(r, TOTAL, stride=CQ), :].astype(BF16))
        k.append(jnp.concatenate([xs[pl.ds(HALF + r, TOTAL, stride=CQ), :].astype(BF16), pad], axis=0))
    gram = lax.dot_general(
        jnp.concatenate(q, axis=1),
        jnp.concatenate(k, axis=1),
        (((1,), (1,)), ((), ())),
        preferred_element_type=F32,
    )
    lane = lax.broadcasted_iota(jnp.int32, gram.shape, 1)
    gs[0] = gram
    gs[1] = jnp.where(lane < TOTAL, 0.0, pltpu.roll(gram, TOTAL, 1))
    gs[2] = jnp.where(lane < TOTAL, 0.0, pltpu.roll(gram, TOTAL - CUT, 1))
    rest = jnp.zeros((2, LAT), F32)
    for s in range(MEM):
        row = s * OWN
        free = [gs[1 + h, row + 4 : row + 5, :] for h in range(2)]
        g_ref[4 * s : 4 * s + 4] = gs[0, row : row + 4, :] + jnp.concatenate(free + [rest], axis=0)


def header_kernel(g_ref, v0_ref, o_ref, ps):
    whole = g_ref[0] + g_ref[1]
    high = whole.astype(BF16).astype(F32)
    ps[0] = high
    ps[1] = whole - high
    for s in range(MEM):
        parts = [ps[part, 4 * s : 4 * s + 4] for part in range(2)]
        o_ref[s, 0:HEAD] = jnp.concatenate(parts, axis=0).astype(BF16)


def spread_kernel(x_ref, o_ref):
    parts = jnp.sum(x_ref[:, 0:HEAD].astype(F32), axis=0)
    o_ref[...] = jnp.broadcast_to((parts[0:4] + parts[4:8])[None], o_ref.shape)


def softmax_kernel(scale, x_ref, v1_ref, o_ref, gs):
    gs[...] = jnp.zeros(gs.shape, F32)
    gs[0:4] = jnp.sum(x_ref[...], axis=0)
    gram = gs[...]
    head, tail = pltpu.roll(gram, LAT - TOTAL, 1), pltpu.roll(gram, LAT - TOTAL + CUT, 1)
    lane = lax.broadcasted_iota(jnp.int32, gram.shape, 1)
    gs[4:5] = jnp.where(lane[0:1] < CUT, head[0:1], tail[1:2])
    s = jnp.where(lane < TOTAL, gs[...] * scale, -jnp.inf)
    e = jnp.exp(s - jnp.max(s, axis=1, keepdims=True))
    w = e / jnp.sum(e, axis=1, keepdims=True)
    for m in range(OWN):
        o_ref[:, m, USED - 8 : USED - 7, :] = jnp.broadcast_to(
            w[m : m + 1].astype(BF16)[None], (MEM, 1, LAT)
        )


def mix_kernel(v0_ref, v1_ref, o_ref, vs, ms):
    vs[0] = v0_ref[:, HEAD:].astype(F32).reshape(TOTAL * 8, LAT)
    vs[1] = v1_ref[...].astype(F32).reshape(TOTAL * 8, LAT)
    rows = [vs[r // 8, pl.ds(r % 8, TOTAL, stride=8), :].astype(BF16) for r in range(ROWS)]
    w = rows[USED][:, :TOTAL]
    v = jnp.concatenate(rows[:USED], axis=1)
    mixed = jnp.dot(w, v, preferred_element_type=F32)
    for r in range(USED):
        ms[pl.ds(r, TOTAL, stride=ROWS), :] = mixed[:, r * LAT : (r + 1) * LAT]
    ms[pl.ds(USED, TOTAL, stride=ROWS), :] = jnp.zeros((TOTAL, LAT), F32)
    o_ref[...] = ms[...].astype(BF16).reshape(o_ref.shape)


def finish_kernel(x_ref, xt_ref, w_ref, o_ref, mc, sh, br, ob, sem):
    copies = [pltpu.make_async_copy(ob.at[m], o_ref.at[m], sem.at[m]) for m in range(OWN)]
    for m in range(OWN):
        for j in range(MEM):
            mc[j * USED : j * USED + ROWS] = x_ref[j, m].astype(F32)
        whole = mc[0 : EXT * CQ]
        before, after = lat_shifts(whole)
        for b, x in enumerate((before, whole, after)):
            sh[b] = x.astype(BF16)
        for i in range(0, COLS, 4):
            patches = []
            for p in (i, i + 2):
                parts = [sh[b, p * CQ : (p + 4) * CQ] for b in range(3)]
                parts.append(xt_ref[m, p * CH : (p + 2) * CH])
                patches.append(jnp.concatenate(parts, axis=0))
            r = jnp.dot(w_ref[...], jnp.concatenate(patches, axis=1), preferred_element_type=F32)
            for n in range(4):
                rows, lanes = (n % 2) * CH, (n // 2) * LAT
                br[pl.ds(i + n, CH, stride=COLS), :] = r[rows : rows + CH, lanes : lanes + LAT]
        ob[m] = br[...].reshape(CH, COLS, LAT).astype(BF16)
        copies[m].start()
    for copy in copies:
        copy.wait()


def shards(fields, w_query, w_key, w_value, w_out):
    edge = jax.ShapeDtypeStruct((OWN, 2 * CH, LAT), BF16)
    plane = pltpu.VMEM((CH * COLS, LAT), F32)
    sib, nb = call(edges_kernel, (edge, edge), [plane], 0, 1_000_000, fields)
    swaps = [(i, (i - 1 if i % 2 == 0 else i + 1) % LON) for i in range(LON)]
    got_nb = lax.ppermute(nb, ("yhi", "x", "core"), swaps)
    got_sib = lax.all_gather(sib, "core", axis=0, tiled=False)
    qk_shape = jax.ShapeDtypeStruct((MEM, OWN, CQ, LAT), BF16)
    v0_shape = jax.ShapeDtypeStruct((MEM, HEAD + OWN * 8, LAT), BF16)
    v1_shape = jax.ShapeDtypeStruct((MEM, OWN, 8, LAT), BF16)
    ends = jax.ShapeDtypeStruct((OWN, 2 * ROWS, LAT), F32)
    pair = jax.ShapeDtypeStruct((18 * CQ, 4 * CH), BF16)
    pair_out = jax.ShapeDtypeStruct((2 * CH, 12 * CQ + 2 * CH), BF16)
    turned = jax.ShapeDtypeStruct((OWN, CH * COLS, LAT), BF16)
    qk, v0, v1, ends, w_pair, w_last, turned = call(
        inner_kernel,
        (qk_shape, v0_shape, v1_shape, ends, pair, pair_out, turned),
        [
            pltpu.VMEM((3 * CQ, 9 * CH), F32),
            plane,
            pltpu.VMEM((OWN, 6 * CQ, LAT), F32),
        ],
        450_000_000,
        2_000_000,
        fields,
        w_query,
        w_key,
        w_value,
        w_out,
    )
    qk, v0, v1 = call(
        outer_kernel,
        (qk_shape, v0_shape, v1_shape),
        [pltpu.VMEM((OWN, 4 * CH, LAT), BF16)] * 2
        + [pltpu.VMEM((2 * CQ + ROWS, LAT), F32), pltpu.VMEM((2 * CQ + ROWS + 8, LAT), F32)],
        300_000_000,
        1_500_000,
        qk,
        v0,
        v1,
        ends,
        w_pair,
        sib,
        nb,
        got_sib,
        got_nb,
        alias={0: 0, 1: 1, 2: 2},
    )
    mem, lon = ("z", "ylo"), ("yhi", "x")
    qk = lax.all_to_all(qk, mem, 0, 0, tiled=True)
    gram = call(
        gram_kernel,
        jax.ShapeDtypeStruct((4 * MEM, LAT), F32),
        [pltpu.VMEM((TOTAL * CQ, LAT), F32), pltpu.VMEM((3, TOTAL, LAT), F32)],
        20_000_000,
        600_000,
        qk,
    )
    gram = lax.all_gather(gram, "core", axis=0, tiled=False)
    v0 = call(
        header_kernel,
        v0_shape,
        [pltpu.VMEM((2, 4 * MEM, LAT), F32)],
        20_000,
        100_000,
        gram,
        v0,
        alias={1: 0},
    )
    v0 = lax.all_to_all(v0, mem, 0, 0, tiled=True)
    copies = jax.ShapeDtypeStruct((LON // 2, 4, LAT), F32)
    gram = call(spread_kernel, copies, [], 40_000, 200_000, v0)
    gram = lax.all_to_all(gram, lon, 0, 0, tiled=True)
    scale = 1.0 / math.sqrt(CQ * LAT * COLS * LON)
    v1 = call(
        functools.partial(softmax_kernel, scale),
        v1_shape,
        [pltpu.VMEM((8, LAT), F32)],
        40_000,
        400_000,
        gram,
        v1,
        alias={1: 0},
    )
    v1 = lax.all_to_all(v1, mem, 0, 0, tiled=True)
    mixed = call(
        mix_kernel,
        jax.ShapeDtypeStruct((MEM, OWN, ROWS, LAT), BF16),
        [pltpu.VMEM((2, TOTAL * 8, LAT), F32), pltpu.VMEM((TOTAL * ROWS, LAT), F32)],
        30_000_000,
        700_000,
        v0,
        v1,
    )
    mixed = lax.all_to_all(mixed, ("z", "ylo"), 0, 0, tiled=True)
    return call(
        finish_kernel,
        jax.ShapeDtypeStruct(fields.shape, BF16),
        [
            pltpu.VMEM((MEM * ROWS, LAT), F32),
            pltpu.VMEM((3, EXT * CQ, LAT), BF16),
            plane,
            pltpu.VMEM(fields.shape, BF16),
            pltpu.SemaphoreType.DMA((OWN,)),
        ],
        150_000_000,
        1_700_000,
        mixed,
        turned,
        w_last,
        far_out=True,
    )


def solution(mesh):
    fine = Mesh(mesh.devices.reshape(MEM // 2, 2, LON // 8, 4, 2), ("z", "ylo", "yhi", "x", "core"))
    spec = P(("z", "ylo"), None, ("yhi", "x", "core"), None)
    return jax.shard_map(
        shards,
        mesh=fine,
        in_specs=(spec, P(), P(), P(), P()),
        out_specs=spec,
        check_vma=False,
    )
```

```python
import functools
import math

import jax
import jax.numpy as jnp
from jax import lax
from jax.experimental import pallas as pl
from jax.experimental.pallas import tpu as pltpu
from jax.sharding import Mesh
from jax.sharding import PartitionSpec as P

CH, CQ, LAT = 64, 24, 128
HALF = CQ // 2
MEM, LON = 16, 32
OWN = 5
TOTAL = MEM * OWN
CUT = LAT - TOTAL
COLS = 8
EXT = COLS + 2
ROWS = 16
USED = EXT * CQ // MEM
HEAD = 8
F32, BF16 = jnp.float32, jnp.bfloat16
VMEM = pl.BlockSpec(memory_space=pltpu.VMEM)


HBM = pl.BlockSpec(memory_space=pl.ANY)


def call(body, outs, scratch, flops, nbytes, *args, alias=None, far_out=False):
    many = isinstance(outs, tuple)
    one = HBM if far_out else VMEM
    return pl.pallas_call(
        body,
        out_shape=outs,
        in_specs=[VMEM] * len(args),
        out_specs=(one,) * len(outs) if many else one,
        scratch_shapes=scratch,
        input_output_aliases=alias or {},
        compiler_params=pltpu.CompilerParams(vmem_limit_bytes=32 * 1024 * 1024),
        cost_estimate=pl.CostEstimate(flops=flops, bytes_accessed=nbytes, transcendentals=0),
    )(*args)


def lat_shifts(x):
    lane = lax.broadcasted_iota(jnp.int32, x.shape, 1)
    before = jnp.where(lane == 0, 0.0, pltpu.roll(x, 1, 1))
    after = jnp.where(lane == LAT - 1, 0.0, pltpu.roll(x, LAT - 1, 1))
    return before, after


def edges_kernel(f_ref, sib_ref, nb_ref, xf):
    even = lax.axis_index("core") == 0
    for m in range(OWN):
        xf[...] = f_ref[m].astype(F32).reshape(CH * COLS, LAT)
        for s in range(2):
            left = xf[pl.ds(s, CH, stride=COLS), :]
            right = xf[pl.ds(COLS - 2 + s, CH, stride=COLS), :]
            sib_ref[m, s * CH : (s + 1) * CH] = jnp.where(even, right, left).astype(BF16)
            nb_ref[m, s * CH : (s + 1) * CH] = jnp.where(even, left, right).astype(BF16)


def conv_pairs(w, xs):
    width = 3 * CQ
    lane = lax.broadcasted_iota(jnp.int32, (width, LAT), 1)
    wide = jnp.dot(w, jnp.concatenate(xs, axis=1), preferred_element_type=F32)
    pairs = []
    for n in range(len(xs)):
        r = wide[:, n * LAT : (n + 1) * LAT]
        outs = []
        for s in range(2):
            y = [r[(3 * s + b) * width : (3 * s + b + 1) * width] for b in range(3)]
            outs.append(
                y[1]
                + jnp.where(lane == 0, 0.0, pltpu.roll(y[0], 1, 1))
                + jnp.where(lane == LAT - 1, 0.0, pltpu.roll(y[2], LAT - 1, 1))
            )
        pairs.append(outs)
    return pairs


def put_block(v0_ref, v1_ref, j, m, block):
    v0_ref[j, HEAD + m * 8 : HEAD + m * 8 + 8] = block[:8].astype(BF16)
    v1_ref[j, m] = block[8:].astype(BF16)


def put_pair(qk_ref, vs, m, p, outs):
    for s in range(2):
        col = 2 * p + s
        vs[s * CQ : (s + 1) * CQ] = outs[s][2 * CQ :]
        if 1 <= col <= COLS:
            for h in range(2):
                qk_ref[2 * (col - 1) + h, m] = outs[s][h * CQ : (h + 1) * CQ].astype(BF16)


def inner_kernel(
    f_ref, wq_ref, wk_ref, wv_ref, wo_ref,
    qk_ref, v0_ref, v1_ref, e_ref, wp_ref, wf_ref, xt, ws, xf, vs,
):
    ws[0:HALF] = wq_ref[...].astype(F32)[:HALF]
    ws[HALF : 2 * HALF] = wk_ref[...].astype(F32)[:HALF]
    ws[2 * HALF : 3 * HALF] = wq_ref[...].astype(F32)[HALF:]
    ws[3 * HALF : 4 * HALF] = wk_ref[...].astype(F32)[HALF:]
    ws[2 * CQ :] = wv_ref[...].astype(F32)
    zero = jnp.zeros((3 * CQ, CH), F32)
    for b in range(3):
        taps = [ws[:, (3 * a + b) * CH : (3 * a + b + 1) * CH] for a in range(3)]
        for s in range(2):
            row = (3 * s + b) * 3 * CQ
            full = [zero] + taps if s else taps + [zero]
            wp_ref[row : row + 3 * CQ] = jnp.concatenate(full, axis=1).astype(BF16)
    wo = wo_ref[...].astype(F32)
    zero = jnp.zeros((CH, CQ), F32)
    row = lax.broadcasted_iota(jnp.int32, (CH, 2 * CH), 0)
    lane = lax.broadcasted_iota(jnp.int32, (CH, 2 * CH), 1)
    for s in range(2):
        full = []
        for b in range(3):
            taps = [wo[:, (3 * a + b) * CQ : (3 * a + b + 1) * CQ] for a in range(3)]
            full += [zero] + taps if s else taps + [zero]
        full.append(jnp.where(lane == row + s * CH, 1.0, 0.0))
        wf_ref[s * CH : (s + 1) * CH] = jnp.concatenate(full, axis=1).astype(BF16)
    for m in range(OWN):
        xf[...] = f_ref[m].astype(F32).reshape(CH * COLS, LAT)
        for i in range(COLS):
            xt[m, i * CH : (i + 1) * CH] = xf[pl.ds(i, CH, stride=COLS), :].astype(BF16)
    units = [(m, p) for m in range(OWN) for p in range(1, EXT // 2 - 1)]
    for n in range(0, len(units), 2):
        two = units[n : n + 2]
        xs = [xt[m, 2 * (p - 1) * CH : 2 * (p + 1) * CH] for m, p in two]
        for (m, p), outs in zip(two, conv_pairs(wp_ref[...], xs)):
            put_pair(qk_ref, vs.at[m, pl.ds((p - 1) * 2 * CQ, 2 * CQ)], m, p, outs)
    for m in range(OWN):
        for j in range(4, 12):
            row = j * USED - 2 * CQ
            put_block(v0_ref, v1_ref, j, m, vs[m, row : row + ROWS])
        e_ref[m, 0:ROWS] = vs[m, 0:ROWS]
        e_ref[m, ROWS:] = vs[m, 6 * CQ - ROWS :]


def outer_kernel(
    iq_ref, i0_ref, i1_ref, e_ref, wp_ref, sib_ref, nb_ref, gs_ref, gn_ref,
    qk_ref, v0_ref, v1_ref, xl, xr, vl, vr
):
    core = lax.axis_index("core")
    near = 2 * CH

    @pl.when(core == 0)
    def _():
        xl[:, :near] = gn_ref[...]
        xl[:, near:] = nb_ref[...]
        xr[:, :near] = sib_ref[...]
        xr[:, near:] = gs_ref[1]

    @pl.when(core == 1)
    def _():
        xl[:, :near] = gs_ref[0]
        xl[:, near:] = sib_ref[...]
        xr[:, :near] = nb_ref[...]
        xr[:, near:] = gn_ref[...]

    for m in range(OWN):
        left, right = conv_pairs(wp_ref[...], [xl[m], xr[m]])
        put_pair(qk_ref, vl.at[pl.ds(0, 2 * CQ)], m, 0, left)
        put_pair(qk_ref, vr.at[pl.ds(ROWS, 2 * CQ)], m, EXT // 2 - 1, right)
        vl[2 * CQ :] = e_ref[m, 0:ROWS]
        vr[0:ROWS] = e_ref[m, ROWS:]
        vr[ROWS + 2 * CQ :] = jnp.zeros((8, LAT), F32)
        for j in range(4):
            put_block(v0_ref, v1_ref, j, m, vl[j * USED : j * USED + ROWS])
            row = (12 + j) * USED - (8 * CQ - ROWS)
            put_block(v0_ref, v1_ref, 12 + j, m, vr[row : row + ROWS])


def gram_kernel(x_ref, g_ref, xs, gs):
    xs[...] = x_ref[...].astype(F32).reshape(TOTAL * CQ, LAT)
    pad = jnp.zeros((LAT - TOTAL, LAT), BF16)
    q, k = [], []
    for r in range(HALF):
        q.append(xs[pl.ds(r, TOTAL, stride=CQ), :].astype(BF16))
        k.append(jnp.concatenate([xs[pl.ds(HALF + r, TOTAL, stride=CQ), :].astype(BF16), pad], axis=0))
    gram = lax.dot_general(
        jnp.concatenate(q, axis=1),
        jnp.concatenate(k, axis=1),
        (((1,), (1,)), ((), ())),
        preferred_element_type=F32,
    )
    lane = lax.broadcasted_iota(jnp.int32, gram.shape, 1)
    gs[0] = gram
    gs[1] = jnp.where(lane < TOTAL, 0.0, pltpu.roll(gram, TOTAL, 1))
    gs[2] = jnp.where(lane < TOTAL, 0.0, pltpu.roll(gram, TOTAL - CUT, 1))
    rest = jnp.zeros((2, LAT), F32)
    for s in range(MEM):
        row = s * OWN
        free = [gs[1 + h, row + 4 : row + 5, :] for h in range(2)]
        g_ref[4 * s : 4 * s + 4] = gs[0, row : row + 4, :] + jnp.concatenate(free + [rest], axis=0)


def header_kernel(g_ref, v0_ref, o_ref, ps):
    whole = g_ref[0] + g_ref[1]
    high = whole.astype(BF16).astype(F32)
    ps[0] = high
    ps[1] = whole - high
    for s in range(MEM):
        parts = [ps[part, 4 * s : 4 * s + 4] for part in range(2)]
        o_ref[s, 0:HEAD] = jnp.concatenate(parts, axis=0).astype(BF16)


def spread_kernel(x_ref, o_ref):
    parts = jnp.sum(x_ref[:, 0:HEAD].astype(F32), axis=0)
    o_ref[...] = jnp.broadcast_to((parts[0:4] + parts[4:8])[None], o_ref.shape)


def softmax_kernel(scale, x_ref, v1_ref, o_ref, gs):
    gs[...] = jnp.zeros(gs.shape, F32)
    gs[0:4] = jnp.sum(x_ref[...], axis=0)
    gram = gs[...]
    head, tail = pltpu.roll(gram, LAT - TOTAL, 1), pltpu.roll(gram, LAT - TOTAL + CUT, 1)
    lane = lax.broadcasted_iota(jnp.int32, gram.shape, 1)
    gs[4:5] = jnp.where(lane[0:1] < CUT, head[0:1], tail[1:2])
    s = jnp.where(lane < TOTAL, gs[...] * scale, -jnp.inf)
    e = jnp.exp(s - jnp.max(s, axis=1, keepdims=True))
    w = e / jnp.sum(e, axis=1, keepdims=True)
    for m in range(OWN):
        o_ref[:, m, USED - 8 : USED - 7, :] = jnp.broadcast_to(
            w[m : m + 1].astype(BF16)[None], (MEM, 1, LAT)
        )


def mix_kernel(v0_ref, v1_ref, o_ref, vs, ms):
    vs[0] = v0_ref[:, HEAD:].astype(F32).reshape(TOTAL * 8, LAT)
    vs[1] = v1_ref[...].astype(F32).reshape(TOTAL * 8, LAT)
    rows = [vs[r // 8, pl.ds(r % 8, TOTAL, stride=8), :].astype(BF16) for r in range(ROWS)]
    w = rows[USED][:, :TOTAL]
    v = jnp.concatenate(rows[:USED], axis=1)
    mixed = jnp.dot(w, v, preferred_element_type=F32)
    for r in range(USED):
        ms[pl.ds(r, TOTAL, stride=ROWS), :] = mixed[:, r * LAT : (r + 1) * LAT]
    o_ref[...] = ms[...].astype(BF16).reshape(o_ref.shape)


def finish_kernel(x_ref, xt_ref, w_ref, o_ref, mc, sh, br, ob, sem):
    copies = [pltpu.make_async_copy(ob.at[m], o_ref.at[m], sem.at[m]) for m in range(OWN)]
    for m in range(OWN):
        for j in range(MEM):
            mc[j * USED : j * USED + ROWS] = x_ref[j, m].astype(F32)
        whole = mc[0 : EXT * CQ]
        before, after = lat_shifts(whole)
        for b, x in enumerate((before, whole, after)):
            sh[b] = x.astype(BF16)
        for i in range(0, COLS, 4):
            patches = []
            for p in (i, i + 2):
                parts = [sh[b, p * CQ : (p + 4) * CQ] for b in range(3)]
                parts.append(xt_ref[m, p * CH : (p + 2) * CH])
                patches.append(jnp.concatenate(parts, axis=0))
            r = jnp.dot(w_ref[...], jnp.concatenate(patches, axis=1), preferred_element_type=F32)
            for n in range(4):
                rows, lanes = (n % 2) * CH, (n // 2) * LAT
                br[pl.ds(i + n, CH, stride=COLS), :] = r[rows : rows + CH, lanes : lanes + LAT]
        ob[m] = br[...].reshape(CH, COLS, LAT).astype(BF16)
        copies[m].start()
    for copy in copies:
        copy.wait()


def shards(fields, w_query, w_key, w_value, w_out):
    edge = jax.ShapeDtypeStruct((OWN, 2 * CH, LAT), BF16)
    plane = pltpu.VMEM((CH * COLS, LAT), F32)
    sib, nb = call(edges_kernel, (edge, edge), [plane], 0, 1_000_000, fields)
    swaps = [(i, (i - 1 if i % 2 == 0 else i + 1) % LON) for i in range(LON)]
    got_nb = lax.ppermute(nb, ("yhi", "x", "core"), swaps)
    got_sib = lax.all_gather(sib, "core", axis=0, tiled=False)
    qk_shape = jax.ShapeDtypeStruct((MEM, OWN, CQ, LAT), BF16)
    v0_shape = jax.ShapeDtypeStruct((MEM, HEAD + OWN * 8, LAT), BF16)
    v1_shape = jax.ShapeDtypeStruct((MEM, OWN, 8, LAT), BF16)
    ends = jax.ShapeDtypeStruct((OWN, 2 * ROWS, LAT), F32)
    pair = jax.ShapeDtypeStruct((18 * CQ, 4 * CH), BF16)
    pair_out = jax.ShapeDtypeStruct((2 * CH, 12 * CQ + 2 * CH), BF16)
    turned = jax.ShapeDtypeStruct((OWN, CH * COLS, LAT), BF16)
    qk, v0, v1, ends, w_pair, w_last, turned = call(
        inner_kernel,
        (qk_shape, v0_shape, v1_shape, ends, pair, pair_out, turned),
        [
            pltpu.VMEM((3 * CQ, 9 * CH), F32),
            plane,
            pltpu.VMEM((OWN, 6 * CQ, LAT), F32),
        ],
        450_000_000,
        2_000_000,
        fields,
        w_query,
        w_key,
        w_value,
        w_out,
    )
    qk, v0, v1 = call(
        outer_kernel,
        (qk_shape, v0_shape, v1_shape),
        [pltpu.VMEM((OWN, 4 * CH, LAT), BF16)] * 2
        + [pltpu.VMEM((2 * CQ + ROWS, LAT), F32), pltpu.VMEM((2 * CQ + ROWS + 8, LAT), F32)],
        300_000_000,
        1_500_000,
        qk,
        v0,
        v1,
        ends,
        w_pair,
        sib,
        nb,
        got_sib,
        got_nb,
        alias={0: 0, 1: 1, 2: 2},
    )
    mem, lon = ("z", "ylo"), ("yhi", "x")
    qk = lax.all_to_all(qk, mem, 0, 0, tiled=True)
    gram = call(
        gram_kernel,
        jax.ShapeDtypeStruct((4 * MEM, LAT), F32),
        [pltpu.VMEM((TOTAL * CQ, LAT), F32), pltpu.VMEM((3, TOTAL, LAT), F32)],
        20_000_000,
        600_000,
        qk,
    )
    gram = lax.all_gather(gram, "core", axis=0, tiled=False)
    v0 = call(
        header_kernel,
        v0_shape,
        [pltpu.VMEM((2, 4 * MEM, LAT), F32)],
        20_000,
        100_000,
        gram,
        v0,
        alias={1: 0},
    )
    v0 = lax.all_to_all(v0, mem, 0, 0, tiled=True)
    copies = jax.ShapeDtypeStruct((LON // 2, 4, LAT), F32)
    gram = call(spread_kernel, copies, [], 40_000, 200_000, v0)
    gram = lax.all_to_all(gram, lon, 0, 0, tiled=True)
    scale = 1.0 / math.sqrt(CQ * LAT * COLS * LON)
    v1 = call(
        functools.partial(softmax_kernel, scale),
        v1_shape,
        [pltpu.VMEM((8, LAT), F32)],
        40_000,
        400_000,
        gram,
        v1,
        alias={1: 0},
    )
    v1 = lax.all_to_all(v1, mem, 0, 0, tiled=True)
    mixed = call(
        mix_kernel,
        jax.ShapeDtypeStruct((MEM, OWN, ROWS, LAT), BF16),
        [pltpu.VMEM((2, TOTAL * 8, LAT), F32), pltpu.VMEM((TOTAL * ROWS, LAT), F32)],
        30_000_000,
        700_000,
        v0,
        v1,
    )
    mixed = lax.all_to_all(mixed, ("z", "ylo"), 0, 0, tiled=True)
    return call(
        finish_kernel,
        jax.ShapeDtypeStruct(fields.shape, BF16),
        [
            pltpu.VMEM((MEM * ROWS, LAT), F32),
            pltpu.VMEM((3, EXT * CQ, LAT), BF16),
            plane,
            pltpu.VMEM(fields.shape, BF16),
            pltpu.SemaphoreType.DMA((OWN,)),
        ],
        150_000_000,
        1_700_000,
        mixed,
        turned,
        w_last,
        far_out=True,
    )


def solution(mesh):
    fine = Mesh(mesh.devices.reshape(MEM // 2, 2, LON // 8, 4, 2), ("z", "ylo", "yhi", "x", "core"))
    spec = P(("z", "ylo"), None, ("yhi", "x", "core"), None)
    return jax.shard_map(
        shards,
        mesh=fine,
        in_specs=(spec, P(), P(), P(), P()),
        out_specs=spec,
        check_vma=False,
    )
```
